32 devices in a mesh: dp: 8 (over y, x, core), mp: 4 (over z).
Axes of the slice: x: 2, y: 2, z: 4, core: 2. Of those that a mesh axis runs over, the one named last changes fastest.
Arguments:
- series: bfloat16 [2, 8192, 96], P(None, ('dp', 'mp')), may hold values from -6 to 6
- targets: float32 [2, 8192, 96], P(None, ('dp', 'mp')), may hold values from -6 to 6
- valid: int32 [2, 8192, 96], P(None, ('dp', 'mp')), may hold values from 0 to 1
- dataset_ids: int32 [2, 8192], P(None, ('dp', 'mp')), may hold values from 0 to 10, as said below
- embed_w: float32 [96, 512], P(None, 'dp'), may hold values from -0.625 to 0.625
- qkv_w: float32 [2, 512, 3, 512], P(None, 'dp', None, 'mp'), may hold values from -0.25 to 0.25
- out_w: float32 [2, 512, 512], P(None, 'dp', 'mp'), may hold values from -1 to 1
- up_w: float32 [2, 512, 2048], P(None, 'dp', 'mp'), may hold values from -0.25 to 0.25
- down_w: float32 [2, 512, 2048], P(None, 'dp', 'mp'), may hold values from -0.125 to 0.125
- head_w: float32 [512, 288], P('dp'), may hold values from -0.25 to 0.25
- norm_params: float32 [5, 2, 512], P(None, None, 'dp'), may hold values from -1 to 3.25
- embed_first: float32 [96, 512], P(None, 'dp'), may hold values from -2.6077032e-08 to 2.6077032e-08
- embed_second: float32 [96, 512], P(None, 'dp'), may hold values from 1.5e-18 to 6.2e-18
- qkv_first: float32 [2, 512, 3, 512], P(None, 'dp', None, 'mp'), may hold values from -2.6077032e-08 to 2.6077032e-08
- qkv_second: float32 [2, 512, 3, 512], P(None, 'dp', None, 'mp'), may hold values from 1.5e-18 to 6.2e-18
- out_first: float32 [2, 512, 512], P(None, 'dp', 'mp'), may hold values from -2.6077032e-08 to 2.6077032e-08
- out_second: float32 [2, 512, 512], P(None, 'dp', 'mp'), may hold values from 1.5e-18 to 6.2e-18
- up_first: float32 [2, 512, 2048], P(None, 'dp', 'mp'), may hold values from -2.6077032e-08 to 2.6077032e-08
- up_second: float32 [2, 512, 2048], P(None, 'dp', 'mp'), may hold values from 1.5e-18 to 6.2e-18
- down_first: float32 [2, 512, 2048], P(None, 'dp', 'mp'), may hold values from -2.6077032e-08 to 2.6077032e-08
- down_second: float32 [2, 512, 2048], P(None, 'dp', 'mp'), may hold values from 1.5e-18 to 6.2e-18
- head_first: float32 [512, 288], P('dp'), may hold values from -2.6077032e-08 to 2.6077032e-08
- head_second: float32 [512, 288], P('dp'), may hold values from 1.5e-18 to 6.2e-18
- norm_first: float32 [5, 2, 512], P(None, None, 'dp'), may hold values from -2.3841858e-07 to 2.3841858e-07
- norm_second: float32 [5, 2, 512], P(None, None, 'dp'), may hold values from 1.5e-16 to 6.2e-16
Outputs:
- loss_sum: float32 [], replicated
- valid_count: float32 [], replicated
- grad_norm: float32 [], replicated
- embed_next: float32 [96, 512], P(None, 'dp')
- embed_first_next: float32 [96, 512], P(None, 'dp')
- embed_second_next: float32 [96, 512], P(None, 'dp')
- qkv_next: float32 [2, 512, 3, 512], P(None, 'dp', None, 'mp')
- qkv_first_next: float32 [2, 512, 3, 512], P(None, 'dp', None, 'mp')
- qkv_second_next: float32 [2, 512, 3, 512], P(None, 'dp', None, 'mp')
- out_next: float32 [2, 512, 512], P(None, 'dp', 'mp')
- out_first_next: float32 [2, 512, 512], P(None, 'dp', 'mp')
- out_second_next: float32 [2, 512, 512], P(None, 'dp', 'mp')
- up_next: float32 [2, 512, 2048], P(None, 'dp', 'mp')
- up_first_next: float32 [2, 512, 2048], P(None, 'dp', 'mp')
- up_second_next: float32 [2, 512, 2048], P(None, 'dp', 'mp')
- down_next: float32 [2, 512, 2048], P(None, 'dp', 'mp')
- down_first_next: float32 [2, 512, 2048], P(None, 'dp', 'mp')
- down_second_next: float32 [2, 512, 2048], P(None, 'dp', 'mp')
- head_next: float32 [512, 288], P('dp')
- head_first_next: float32 [512, 288], P('dp')
- head_second_next: float32 [512, 288], P('dp')
- norm_next: float32 [5, 2, 512], P(None, None, 'dp')
- norm_first_next: float32 [5, 2, 512], P(None, None, 'dp')
- norm_second_next: float32 [5, 2, 512], P(None, None, 'dp')
The draws below stay inside these ranges and needn't reach their ends.
Inputs may be any that keep to these rules, and one draw needn't show every extreme that they name: `dataset_ids`: within each sequence of 1024 tokens the ids never fall, are 0 at its first token and 10 at its last, and one dataset covers a stretch from the sequence's first quarter into its last quarter.
All inputs are finite; a program needn't handle non-finite values.
Results may differ from the reference program's by a relative error of at most 0.02.
Values may be sent and summed in bfloat16 or wider, within the bound.
No kernel may reach another device: no remote copies, remote signals or barrier semaphores. Data moves between devices by JAX's collectives and lax.ppermute only.
A program may use at most 192 MiB of HBM per device.

```python
import math
import jax
import jax.numpy as jnp
from jax import lax

D = 512
HEADS = 8
HEAD_DIM = 64
FF = 2048
LAYERS = 2
LOOK = 96
HOR = 96
QUANT = 3
SEQ = 1024
BLOCK = 512
MICRO = 2
STEP = 10
TOKENS = 8192
NORMS = 5
QH = 288


def draw_valid(key, part):
    key = jax.random.fold_in(key, 11)
    position = jnp.arange(TOKENS, dtype=jnp.int32)
    group_span = max(TOKENS // SEQ - 1, 1)
    group_rank = position // SEQ
    inside = position % SEQ * 1000 // SEQ
    threshold = 100 * (group_span + 2 * group_rank) * (1000 + 2 * inside) // (group_span * 1000)
    rolled = jax.random.randint(key, (MICRO, TOKENS, HOR), 0, 1000)
    return (rolled < threshold[None, :, None]).astype(jnp.int32)


def draw_dataset_ids(key, part):
    key = jax.random.fold_in(key, 23)
    sub_keys = jax.random.split(key, 4)
    seq_count = MICRO * TOKENS // SEQ
    quarter = SEQ // 4
    opening = jax.random.randint(sub_keys[0], (seq_count, 1), 2, quarter)
    closing = jax.random.randint(sub_keys[1], (seq_count, 1), SEQ - quarter, SEQ - 1)
    earlier = jax.random.randint(sub_keys[2], (seq_count, 4), 1, opening)
    later = jax.random.randint(sub_keys[3], (seq_count, 4), closing + 1, SEQ)
    bounds = jnp.concatenate([opening, closing, earlier, later], axis=1)
    position = jnp.arange(SEQ, dtype=jnp.int32)
    dataset_rank = jnp.sum((position[None, :, None] >= bounds[:, None, :]).astype(jnp.int32), axis=-1)
    return dataset_rank.reshape(MICRO, TOKENS).astype(jnp.int32)


def draw_norm_params(key, part):
    key = jax.random.fold_in(key, 37)
    first_key, second_key = jax.random.split(key)
    across = jnp.arange(D, dtype=jnp.float32) / (D - 1)
    rising = 0.6 * jnp.exp(across * math.log(3.0))
    factor = jax.random.uniform(first_key, (NORMS, D), jnp.float32, 0.8, 1.2)
    shift = jnp.clip(0.3 * jax.random.normal(second_key, (NORMS, D), jnp.float32), -1.0, 1.0)
    return jnp.stack([rising[None, :] * factor, shift], axis=1).astype(jnp.float32)


def block_levels(rng, shape, cuts, low, top_value):
    loudness, own = 1.0, jax.random.fold_in(rng, 6)
    for axis_at, blocks in cuts:
        draws = jnp.exp(jax.random.uniform(jax.random.fold_in(own, axis_at), (blocks,), jnp.float32, low / len(cuts), top_value / len(cuts)))
        loudness = loudness * jnp.repeat(draws, shape[axis_at] // blocks).reshape([-1 if axis == axis_at else 1 for axis in range(len(shape))])
    return loudness


def noise(stream_key, shape, spread, bound, shards=(), held_as=jnp.bfloat16):
    level = block_levels(stream_key, shape, shards, -0.22, 0.18) if shards else 1.0
    result = jax.random.normal(stream_key, shape, jnp.float32) * spread * level
    return jnp.minimum(jnp.maximum(result, -bound), bound).astype(held_as)


def setup_inputs(seed: int = 0) -> dict:
    key_of = jax.random.split(jax.random.key(seed), 26)
    series = noise(key_of[0], (MICRO, TOKENS, LOOK), 1.0, 6.0, ((1, 32),))
    targets = noise(key_of[1], (MICRO, TOKENS, HOR), 1.0, 6.0, ((1, 32),), jnp.float32)
    valid = draw_valid(jax.random.fold_in(key_of[25], 71), 0)
    dataset_ids = draw_dataset_ids(jax.random.fold_in(key_of[25], 71), 0)
    embed_w = noise(key_of[4], (LOOK, D), LOOK ** -0.5, 0.625, ((1, 8),), jnp.float32)
    qkv_w = noise(key_of[5], (LAYERS, D, 3, D), D ** -0.5, 0.25, ((1, 8), (3, 4)), jnp.float32)
    out_w = noise(key_of[6], (LAYERS, D, D), (D // 16) ** -0.5, 1.0, ((1, 8), (2, 4)), jnp.float32)
    up_w = noise(key_of[7], (LAYERS, D, FF), D ** -0.5, 0.25, ((1, 8), (2, 4)), jnp.float32)
    down_w = noise(key_of[8], (LAYERS, D, FF), FF ** -0.5, 0.125, ((1, 8), (2, 4)), jnp.float32)
    head_w = noise(key_of[9], (D, QH), D ** -0.5, 0.25, ((0, 8),), jnp.float32)
    norm_params = draw_norm_params(jax.random.fold_in(key_of[25], 71), 0)
    embed_first = noise(key_of[11], (LOOK, D), (4.4e-9), 2.60770320892334e-08, ((1, 8),), jnp.float32)
    embed_second = jnp.clip(jnp.exp(math.log(6.1999999324932105e-18) - 1.4190842 * jax.random.uniform(key_of[12], (LOOK, D), jnp.float32) ** block_levels(key_of[12], (LOOK, D), ((1, 8),), -0.2, 0.2)), 1.5000000170217692e-18, 6.1999999324932105e-18)
    qkv_first = noise(key_of[13], (LAYERS, D, 3, D), (4.4e-9), 2.60770320892334e-08, ((1, 8), (3, 4)), jnp.float32)
    qkv_second = jnp.clip(jnp.exp(math.log(6.1999999324932105e-18) - 1.4190842 * jax.random.uniform(key_of[14], (LAYERS, D, 3, D), jnp.float32) ** block_levels(key_of[14], (LAYERS, D, 3, D), ((1, 8), (3, 4)), -0.2, 0.2)), 1.5000000170217692e-18, 6.1999999324932105e-18)
    out_first = noise(key_of[15], (LAYERS, D, D), (4.4e-9), 2.60770320892334e-08, ((1, 8), (2, 4)), jnp.float32)
    out_second = jnp.clip(jnp.exp(math.log(6.1999999324932105e-18) - 1.4190842 * jax.random.uniform(key_of[16], (LAYERS, D, D), jnp.float32) ** block_levels(key_of[16], (LAYERS, D, D), ((1, 8), (2, 4)), -0.2, 0.2)), 1.5000000170217692e-18, 6.1999999324932105e-18)
    up_first = noise(key_of[17], (LAYERS, D, FF), (4.4e-9), 2.60770320892334e-08, ((1, 8), (2, 4)), jnp.float32)
    up_second = jnp.clip(jnp.exp(math.log(6.1999999324932105e-18) - 1.4190842 * jax.random.uniform(key_of[18], (LAYERS, D, FF), jnp.float32) ** block_levels(key_of[18], (LAYERS, D, FF), ((1, 8), (2, 4)), -0.2, 0.2)), 1.5000000170217692e-18, 6.1999999324932105e-18)
    down_first = noise(key_of[19], (LAYERS, D, FF), (4.4e-9), 2.60770320892334e-08, ((1, 8), (2, 4)), jnp.float32)
    down_second = jnp.clip(jnp.exp(math.log(6.1999999324932105e-18) - 1.4190842 * jax.random.uniform(key_of[20], (LAYERS, D, FF), jnp.float32) ** block_levels(key_of[20], (LAYERS, D, FF), ((1, 8), (2, 4)), -0.2, 0.2)), 1.5000000170217692e-18, 6.1999999324932105e-18)
    head_first = noise(key_of[21], (D, QH), (4.4e-9), 2.60770320892334e-08, ((0, 8),), jnp.float32)
    head_second = jnp.clip(jnp.exp(math.log(6.1999999324932105e-18) - 1.4190842 * jax.random.uniform(key_of[22], (D, QH), jnp.float32) ** block_levels(key_of[22], (D, QH), ((0, 8),), -0.2, 0.2)), 1.5000000170217692e-18, 6.1999999324932105e-18)
    norm_first = noise(key_of[23], (NORMS, 2, D), (4.4e-8), 2.384185791015625e-07, ((2, 8),), jnp.float32)
    norm_second = jnp.clip(jnp.exp(math.log(6.200000064842108e-16) - 1.4190842 * jax.random.uniform(key_of[24], (NORMS, 2, D), jnp.float32) ** block_levels(key_of[24], (NORMS, 2, D), ((2, 8),), -0.2, 0.2)), 1.5000000583807998e-16, 6.200000064842108e-16)
    return {"series": series, "targets": targets, "valid": valid, "dataset_ids": dataset_ids, "embed_w": embed_w, "qkv_w": qkv_w, "out_w": out_w, "up_w": up_w, "down_w": down_w, "head_w": head_w, "norm_params": norm_params, "embed_first": embed_first, "embed_second": embed_second, "qkv_first": qkv_first, "qkv_second": qkv_second, "out_first": out_first, "out_second": out_second, "up_first": up_first, "up_second": up_second, "down_first": down_first, "down_second": down_second, "head_first": head_first, "head_second": head_second, "norm_first": norm_first, "norm_second": norm_second}


PRECISE = lax.Precision.HIGHEST
SMOOTHING = 0.1
LEVELS = (0.1, 0.5, 0.9)
CLIP_NORM = 0.0001
LEARN_RATE = 0.05
NORM_RATE = 0.5
BETA_ONE = 0.9
BETA_TWO = 0.999
EPSILON = 1e-12
WEIGHT_DECAY = 0.1

@jax.custom_vjp
def low(v):
    return lax.optimization_barrier(v.astype(jnp.bfloat16)).astype(jnp.float32)

@jax.custom_vjp
def low_back(v):
    return v

def low_keep(v):
    return (low(v), None)

def low_pass(kept, grad):
    return (grad,)

def back_keep(v):
    return (v, None)

def back_low(kept, grad):
    return (low(grad),)
low.defvjp(low_keep, low_pass)
low_back.defvjp(back_keep, back_low)

def layer_norm(values_in, gain, shift):
    row_mean = lax.optimization_barrier(jnp.mean(values_in, axis=-1, keepdims=True))
    centered = values_in - row_mean
    return centered * lax.rsqrt(lax.optimization_barrier(jnp.mean(centered * centered, axis=-1, keepdims=True)) + 1e-05) * gain + shift

def attend(queries, key_rows, value_rows, seq_ids):

    def one_block(block_args):
        query_part, part_ids = block_args
        scores = low_back(jnp.einsum('qhe,khe->hqk', query_part, key_rows, precision=PRECISE) * 0.125)
        same_set = part_ids[:, None] == seq_ids[None, :]
        probabilities = jax.nn.softmax(jnp.where(same_set[None], scores, -jnp.inf), axis=-1)
        return jnp.einsum('hqk,khe->qhe', low(probabilities), value_rows, precision=PRECISE)
    blocks = lax.map(jax.checkpoint(one_block), (queries.reshape(-1, BLOCK, HEADS, HEAD_DIM), seq_ids.reshape(-1, BLOCK)))
    return blocks.reshape(queries.shape[0], HEADS * HEAD_DIM)

def sequence_loss(params, series, targets, valid, seq_ids, valid_count):
    embed_w, qkv_w, out_w, up_w, down_w, head_w, norm_params = [low(item) for item in params]
    row_count = series.shape[0]
    hidden = low_back(jnp.dot(series, embed_w, precision=PRECISE))
    for layer_index in range(LAYERS):
        qkv = jnp.einsum('nd,dce->nce', low(hidden), qkv_w[layer_index], precision=PRECISE)
        split_heads = low_back(low(qkv)).reshape(row_count, 3, HEADS, HEAD_DIM)
        mixed_out = low_back(low(attend(split_heads[:, 0], split_heads[:, 1], split_heads[:, 2], seq_ids)))
        branch = low_back(jnp.einsum('ni,oi->no', mixed_out, out_w[layer_index], precision=PRECISE))
        first_norm = layer_norm(hidden + branch, norm_params[2 * layer_index, 0], norm_params[2 * layer_index, 1])
        inner_pre = low_back(jnp.einsum('nd,df->nf', low(first_norm), up_w[layer_index], precision=PRECISE))
        activation = low(jax.nn.gelu(inner_pre, approximate=False))
        ffn_out = low_back(jnp.einsum('nf,df->nd', activation, down_w[layer_index], precision=PRECISE))
        hidden = layer_norm(first_norm + ffn_out, norm_params[2 * layer_index + 1, 0], norm_params[2 * layer_index + 1, 1])
    final_norm = layer_norm(hidden, norm_params[NORMS - 1, 0], norm_params[NORMS - 1, 1])
    prediction = low_back(jnp.dot(low(final_norm), head_w, precision=PRECISE)).reshape(row_count, QUANT, HOR)
    gap = targets[:, None, :] - prediction
    levels = jnp.array(LEVELS, jnp.float32)[None, :, None]
    pinball = levels * gap + SMOOTHING * jax.nn.softplus(-gap / SMOOTHING)
    loss_total = jnp.sum(pinball * valid.astype(jnp.float32)[:, None, :])
    return (loss_total / valid_count, loss_total)

def adam_update(weight, gradient, first_moment, second_moment, rate, decay):
    first_moment = BETA_ONE * first_moment + (1 - BETA_ONE) * gradient
    second_moment = BETA_TWO * second_moment + (1 - BETA_TWO) * gradient * gradient
    update = first_moment / (1 - BETA_ONE ** STEP) / (jnp.sqrt(second_moment / (1 - BETA_TWO ** STEP)) + EPSILON)
    return (weight - rate * (update + decay * weight), first_moment, second_moment)

def reference(series, targets, valid, dataset_ids, embed_w, qkv_w, out_w, up_w, down_w, head_w, norm_params, embed_first, embed_second, qkv_first, qkv_second, out_first, out_second, up_first, up_second, down_first, down_second, head_first, head_second, norm_first, norm_second):
    params = (embed_w, qkv_w, out_w, up_w, down_w, head_w, norm_params)
    valid_count = jnp.sum(valid).astype(jnp.float32)
    batches = (series.astype(jnp.float32).reshape(-1, SEQ, LOOK), targets.reshape(-1, SEQ, HOR), valid.reshape(-1, SEQ, HOR), dataset_ids.reshape(-1, SEQ))

    def one_sequence(carry, batch):
        gradients, loss_total = carry

        def loss_of(*weights):
            return sequence_loss(weights, batch[0], batch[1], batch[2], batch[3], valid_count)
        _, pull, part_loss = jax.vjp(loss_of, *params, has_aux=True)
        fresh = pull(jnp.ones((), jnp.float32))
        return ((tuple((old + new for old, new in zip(gradients, fresh))), loss_total + part_loss), None)
    start = (tuple((jnp.zeros_like(item) for item in params)), jnp.zeros((), jnp.float32))
    (gradients, loss_total), _ = lax.scan(one_sequence, start, batches)
    grad_norm = jnp.sqrt(sum((jnp.sum(item * item) for item in gradients)))
    factor = jnp.minimum(1.0, CLIP_NORM / grad_norm)
    g_embed, g_qkv, g_out, g_up, g_down, g_head, g_norm = [item * factor for item in gradients]
    e_new = adam_update(embed_w, g_embed, embed_first, embed_second, LEARN_RATE, WEIGHT_DECAY)
    q_new = adam_update(qkv_w, g_qkv, qkv_first, qkv_second, LEARN_RATE, WEIGHT_DECAY)
    o_new = adam_update(out_w, g_out, out_first, out_second, LEARN_RATE, WEIGHT_DECAY)
    u_new = adam_update(up_w, g_up, up_first, up_second, LEARN_RATE, WEIGHT_DECAY)
    d_new = adam_update(down_w, g_down, down_first, down_second, LEARN_RATE, WEIGHT_DECAY)
    h_new = adam_update(head_w, g_head, head_first, head_second, LEARN_RATE, WEIGHT_DECAY)
    n_new = adam_update(norm_params, g_norm, norm_first, norm_second, NORM_RATE, 0.0)
    return (loss_total, valid_count, grad_norm, e_new[0], e_new[1], e_new[2], q_new[0], q_new[1], q_new[2], o_new[0], o_new[1], o_new[2], u_new[0], u_new[1], u_new[2], d_new[0], d_new[1], d_new[2], h_new[0], h_new[1], h_new[2], n_new[0], n_new[1], n_new[2])
```

```python
import jax
import jax.numpy as jnp
from jax import lax
from jax.sharding import Mesh
from jax.sharding import PartitionSpec as P

HEAD_DIM = 64
LAYERS = 2
HOR = 96
LOOK = 96
QUANT = 3
MICRO = 2
STEP = 10
NORMS = 5
CORES = 2

SMOOTHING = 0.1
LEVELS = (0.1, 0.5, 0.9)
CLIP_NORM = 0.0001
LEARN_RATE = 0.05
NORM_RATE = 0.5
BETA_ONE = 0.9
BETA_TWO = 0.999
EPSILON = 1e-12
WEIGHT_DECAY = 0.1

BF = jnp.bfloat16
F32 = jnp.float32


def swap_core(v):
    return lax.ppermute(v, "core", [(0, 1), (1, 0)])


def swap_hi(v, bit):
    size = lax.axis_size("hi")
    return lax.ppermute(v, "hi", [(i, i ^ (1 << bit)) for i in range(size)])


def turn_mp(v, by):
    size = lax.axis_size("mp")
    return lax.ppermute(v, "mp", [(i, (i + by) % size) for i in range(size)])


def hi_bits():
    return (lax.axis_size("hi") - 1).bit_length()


def bit_order(flip):
    bits = list(range(hi_bits()))
    return bits[::-1] if flip else bits


def gather_width(v, flip):
    bits = hi_bits()
    done = []
    for bit in bit_order(flip):
        axis = sum(1 for other in done if other > bit)
        v = jnp.stack([v, swap_hi(v, bit)], axis=axis)
        done.append(bit)
    v = jnp.stack([v, swap_core(v)], axis=0)
    return v.reshape((-1, v.shape[-1]))


def scatter_width(v, flip):
    bits = hi_bits()
    rows = v.shape[0] // (CORES << bits)
    v = v.reshape((CORES,) + (2,) * bits + (rows, v.shape[-1]))
    v = add_low(v[0], swap_core(v[1]))
    left = list(range(bits))
    for bit in bit_order(flip)[::-1]:
        axis = sum(1 for other in left if other > bit)
        keep = lax.index_in_dim(v, 0, axis, keepdims=False)
        send = lax.index_in_dim(v, 1, axis, keepdims=False)
        v = add_low(keep, swap_hi(send, bit))
        left.remove(bit)
    return v


def add_low(left, right):
    return (left.astype(F32) + right.astype(F32)).astype(left.dtype)


def gather_blocks(v):
    blocks = [v]
    for _ in range(lax.axis_size("mp") - 1):
        blocks.append(turn_mp(blocks[-1], 1))
    half = len(blocks) // 2
    out = []
    for flip in (False, True):
        pair = jnp.concatenate(blocks[flip * half : (flip + 1) * half], axis=1)
        full = gather_width(pair, flip)
        out += jnp.split(full, half, axis=1)
    return out


def scatter_blocks(blocks):
    half = len(blocks) // 2
    parts = []
    for flip in (False, True):
        pair = jnp.concatenate(blocks[flip * half : (flip + 1) * half], axis=1)
        parts += jnp.split(scatter_width(pair, flip), half, axis=1)
    total = parts[1]
    for block in parts[2:]:
        total = add_low(turn_mp(total, 1), block)
    return turn_mp(total, 1).astype(F32) + parts[0].astype(F32)


def mm(a, b):
    return lax.dot_general(a, b, (((1,), (0,)), ((), ())), preferred_element_type=F32)


def mm_nt(a, b):
    return lax.dot_general(a, b, (((1,), (1,)), ((), ())), preferred_element_type=F32)


def mm_tn(a, b):
    return lax.dot_general(a, b, (((0,), (0,)), ((), ())), preferred_element_type=F32)


def norm_forward(values_in, gain, shift):
    row_mean = jnp.mean(values_in, axis=-1, keepdims=True)
    centered = values_in - row_mean
    scaled = lax.rsqrt(jnp.mean(centered * centered, axis=-1, keepdims=True) + 1e-05)
    unit_rows = centered * scaled
    return (unit_rows * gain + shift, (unit_rows, scaled))


def norm_backward(gradient, gain, kept):
    unit_rows, scaled = kept
    d_gain = jnp.sum(gradient * unit_rows, axis=0)
    d_shift = jnp.sum(gradient, axis=0)
    d_unit = gradient * gain
    d_values = scaled * (
        d_unit
        - jnp.mean(d_unit, axis=-1, keepdims=True)
        - unit_rows * jnp.mean(d_unit * unit_rows, axis=-1, keepdims=True)
    )
    return (d_values, jnp.stack([d_gain, d_shift]))


def heads_of(v):
    return v.reshape(v.shape[0], -1, HEAD_DIM)


def attend_forward(q, k, v, ids_here, ids_all):
    scores = jnp.einsum("qhe,khe->hqk", heads_of(q), heads_of(k), preferred_element_type=F32) * 0.125
    scores = jnp.where((ids_here[:, None] == ids_all[None, :])[None], scores, -jnp.inf)
    row_max = jnp.max(scores, axis=-1, keepdims=True)
    log_total = row_max + jnp.log(jnp.sum(jnp.exp(scores - row_max), axis=-1, keepdims=True))
    probs = jnp.exp(scores - log_total).astype(BF)
    mixed = jnp.einsum("hqk,khe->qhe", probs, heads_of(v), preferred_element_type=F32)
    return mixed.reshape(q.shape).astype(BF), log_total


def attend_backward(q, k, v, ids_here, ids_all, log_total, d_mixed):
    scores = jnp.einsum("qhe,khe->hqk", heads_of(q), heads_of(k), preferred_element_type=F32) * 0.125
    scores = jnp.where((ids_here[:, None] == ids_all[None, :])[None], scores, -jnp.inf)
    probs = jnp.exp(scores - log_total)
    d_v = jnp.einsum("hqk,qhe->khe", probs.astype(BF), heads_of(d_mixed), preferred_element_type=F32)
    d_p = jnp.einsum("qhe,khe->hqk", heads_of(d_mixed), heads_of(v), preferred_element_type=F32)
    d_s = (probs * (d_p - jnp.sum(probs * d_p, axis=-1, keepdims=True))).astype(BF)
    d_q = jnp.einsum("hqk,khe->qhe", d_s, heads_of(k), preferred_element_type=F32) * 0.125
    d_k = jnp.einsum("hqk,qhe->khe", d_s, heads_of(q), preferred_element_type=F32) * 0.125
    return d_q.reshape(q.shape), d_k.reshape(k.shape), d_v.reshape(v.shape)


def adam_update(weight, gradient, first_moment, second_moment, rate, decay):
    first_moment = BETA_ONE * first_moment + (1 - BETA_ONE) * gradient
    second_moment = BETA_TWO * second_moment + (1 - BETA_TWO) * gradient * gradient
    update = (
        first_moment
        / (1 - BETA_ONE**STEP)
        / (jnp.sqrt(second_moment / (1 - BETA_TWO**STEP)) + EPSILON)
    )
    return (weight - rate * (update + decay * weight), first_moment, second_moment)


def deal_rows(v):
    rows = v.shape[1] // CORES
    core = lax.axis_index("core")
    v = v.reshape(MICRO, CORES, rows, v.shape[-1])
    keep = lax.dynamic_index_in_dim(v, core, 1, keepdims=False)
    send = lax.dynamic_index_in_dim(v, 1 - core, 1, keepdims=False)
    got = swap_core(send)
    both = jnp.where(core == 0, jnp.concatenate([keep, got]), jnp.concatenate([got, keep]))
    return lax.all_to_all(both, "mp", 0, 0, tiled=True).reshape(-1, v.shape[-1])


def body(
    series,
    targets,
    valid,
    dataset_ids,
    embed_w,
    qkv_w,
    out_w,
    up_w,
    down_w,
    head_w,
    norm_params,
    *moments,
):
    (
        embed_first,
        embed_second,
        qkv_first,
        qkv_second,
        out_first,
        out_second,
        up_first,
        up_second,
        down_first,
        down_second,
        head_first,
        head_second,
        norm_first,
        norm_second,
    ) = moments
    width = embed_w.shape[1]
    part = qkv_w.shape[3]
    wide = up_w.shape[2]
    blocks_n = lax.axis_size("mp")

    rest = gather_width(
        jnp.concatenate(
            [embed_w.T, head_w, norm_params.reshape(-1, width).T], axis=1
        ).astype(BF),
        False,
    )
    embed_t = rest[:, :LOOK]
    head = rest[:, LOOK : LOOK + QUANT * HOR]
    norms = rest[:, LOOK + QUANT * HOR :].T.astype(F32).reshape(NORMS, 2, -1)
    att, ffn = [], []
    for l in range(LAYERS):
        att.append(
            gather_blocks(
                jnp.concatenate([qkv_w[l].reshape(width, -1), out_w[l]], axis=1).astype(BF)
            )
        )
        ffn.append(gather_blocks(jnp.concatenate([up_w[l], down_w[l]], axis=1).astype(BF)))

    low = deal_rows(
        jnp.concatenate(
            [series, valid.astype(BF), dataset_ids[..., None].astype(BF)], axis=-1
        )
    )
    x_in = low[:, :LOOK]
    counted = low[:, LOOK : LOOK + HOR].astype(F32)
    ids_here = low[:, LOOK + HOR]
    ids_all = jnp.concatenate([ids_here, swap_core(ids_here)])
    target = deal_rows(targets)
    rows = x_in.shape[0]

    hidden = mm_nt(x_in, embed_t)
    stored = []
    for l in range(LAYERS):
        h_low = hidden.astype(BF)
        w_qkv = [
            jnp.concatenate([b[:, s * part : (s + 1) * part] for b in att[l]], axis=1)
            for s in range(3)
        ]
        w_out = jnp.concatenate([b[:, 3 * part :] for b in att[l]], axis=1)
        w_up = jnp.concatenate([b[:, :wide] for b in ffn[l]], axis=1)
        w_down = jnp.concatenate([b[:, wide:] for b in ffn[l]], axis=1)
        kv = mm(h_low, jnp.concatenate(w_qkv[1:], axis=1)).astype(BF)
        kv_all = jnp.concatenate([kv, swap_core(kv)])
        q = mm(h_low, w_qkv[0]).astype(BF)
        k, v = jnp.split(kv_all, 2, axis=1)
        mixed, log_total = attend_forward(q, k, v, ids_here, ids_all)
        branch = mm_nt(mixed, w_out)
        first, kept_one = norm_forward(hidden + branch, norms[2 * l, 0], norms[2 * l, 1])
        y_low = first.astype(BF)
        inner = mm(y_low, w_up)
        act = jax.nn.gelu(inner, approximate=False).astype(BF)
        hidden, kept_two = norm_forward(
            first + mm_nt(act, w_down), norms[2 * l + 1, 0], norms[2 * l + 1, 1]
        )
        stored.append(
            (w_qkv, w_out, w_up, w_down, h_low, q, k, v, mixed, log_total, kept_one, y_low, inner, act, kept_two)
        )
    final, kept_last = norm_forward(hidden, norms[NORMS - 1, 0], norms[NORMS - 1, 1])
    final_low = final.astype(BF)
    pred = mm(final_low, head).reshape(rows, QUANT, HOR)
    gap = target[:, None, :] - pred
    levels = jnp.array(LEVELS, F32)[None, :, None]
    mask = counted[:, None, :]
    loss_here = jnp.sum((levels * gap + SMOOTHING * jax.nn.softplus(-gap / SMOOTHING)) * mask)
    d_pred = ((jax.nn.sigmoid(-gap / SMOOTHING) - levels) * mask).reshape(rows, -1).astype(BF)
    g_head = mm_tn(final_low, d_pred)
    d_hidden, gain_last = norm_backward(mm_nt(d_pred, head), norms[NORMS - 1, 0], kept_last)
    gains = [None] * LAYERS
    g_att = [None] * LAYERS
    g_ffn = [None] * LAYERS
    for l in reversed(range(LAYERS)):
        (w_qkv, w_out, w_up, w_down, h_low, q, k, v, mixed, log_total, kept_one, y_low, inner, act, kept_two) = stored[l]
        d_two, gain_two = norm_backward(d_hidden, norms[2 * l + 1, 0], kept_two)
        d_ffn = d_two.astype(BF)
        g_down = mm_tn(d_ffn, act).astype(BF)
        _, pull = jax.vjp(lambda t: jax.nn.gelu(t, approximate=False), inner)
        d_inner = pull(mm(d_ffn, w_down))[0].astype(BF)
        g_up = mm_tn(y_low, d_inner).astype(BF)
        g_ffn[l] = scatter_blocks(
            [
                jnp.concatenate(
                    [g[:, j * wide : (j + 1) * wide] for g in (g_up, g_down)], axis=1
                )
                for j in range(blocks_n)
            ]
        )
        d_one, gain_one = norm_backward(d_two + mm_nt(d_inner, w_up), norms[2 * l, 0], kept_one)
        d_branch = d_one.astype(BF)
        g_out = mm_tn(d_branch, mixed).astype(BF)
        d_mixed = mm(d_branch, w_out).astype(BF)
        d_q, d_k, d_v = attend_backward(q, k, v, ids_here, ids_all, log_total, d_mixed)
        d_kv = jnp.concatenate([d_k, d_v], axis=1)
        d_kv = (d_kv[:rows] + swap_core(d_kv[rows:].astype(BF)).astype(F32)).astype(BF)
        d_q = d_q.astype(BF)
        g_q = mm_tn(h_low, d_q).astype(BF)
        g_kv = mm_tn(h_low, d_kv).astype(BF)
        full = g_q.shape[1]
        g_all = (g_q, g_kv[:, :full], g_kv[:, full:], g_out)
        g_att[l] = scatter_blocks(
            [
                jnp.concatenate([g[:, j * part : (j + 1) * part] for g in g_all], axis=1)
                for j in range(blocks_n)
            ]
        )
        d_hidden = d_one + mm_nt(d_q, w_qkv[0]) + mm_nt(d_kv, jnp.concatenate(w_qkv[1:], axis=1))
        gains[l] = jnp.stack([gain_one, gain_two])
    g_embed = mm_tn(d_hidden.astype(BF), x_in)
    g_norm = jnp.concatenate(gains + [gain_last[None]], axis=0)
    g_rest = jnp.concatenate([g_embed, g_head, g_norm.reshape(-1, g_norm.shape[-1]).T], axis=1)
    g_rest = scatter_width(g_rest.astype(BF), False).astype(F32)
    g_rest = jnp.sum(
        lax.all_to_all(jnp.broadcast_to(g_rest[None], (blocks_n,) + g_rest.shape), "mp", 0, 0, tiled=True),
        axis=0,
    )

    first_rank = (lax.axis_index("mp") == 0).astype(F32)
    squares = first_rank * jnp.sum(g_rest * g_rest)
    for g in g_att + g_ffn:
        squares = squares + jnp.sum(g * g)
    sums = jnp.zeros((1, 128), F32)
    sums = sums.at[0, 0].set(loss_here).at[0, 1].set(jnp.sum(counted)).at[0, 2].set(squares)
    count = lax.axis_size("hi") * CORES * blocks_n
    sums = jnp.sum(
        lax.all_to_all(
            jnp.broadcast_to(sums, (count, 128)), ("hi", "core", "mp"), 0, 0, tiled=True
        ),
        axis=0,
    )
    loss_sum, valid_count = sums[0], sums[1]
    grad_norm = jnp.sqrt(sums[2]) / valid_count
    factor = jnp.minimum(1.0, CLIP_NORM / grad_norm) / valid_count

    ga = jnp.stack(g_att) * factor
    gf = jnp.stack(g_ffn) * factor
    g_rest = g_rest * factor
    e_new = adam_update(embed_w, g_rest[:, :LOOK].T, embed_first, embed_second, LEARN_RATE, WEIGHT_DECAY)
    q_new = adam_update(
        qkv_w, ga[:, :, : 3 * part].reshape(qkv_w.shape), qkv_first, qkv_second, LEARN_RATE, WEIGHT_DECAY
    )
    o_new = adam_update(out_w, ga[:, :, 3 * part :], out_first, out_second, LEARN_RATE, WEIGHT_DECAY)
    u_new = adam_update(up_w, gf[:, :, :wide], up_first, up_second, LEARN_RATE, WEIGHT_DECAY)
    d_new = adam_update(down_w, gf[:, :, wide:], down_first, down_second, LEARN_RATE, WEIGHT_DECAY)
    h_new = adam_update(
        head_w, g_rest[:, LOOK : LOOK + QUANT * HOR], head_first, head_second, LEARN_RATE, WEIGHT_DECAY
    )
    n_new = adam_update(
        norm_params,
        g_rest[:, LOOK + QUANT * HOR :].T.reshape(norm_params.shape),
        norm_first,
        norm_second,
        NORM_RATE,
        0.0,
    )
    return (loss_sum, valid_count, grad_norm, *e_new, *q_new, *o_new, *u_new, *d_new, *h_new, *n_new)


def solution(mesh):
    dp, mp = mesh.devices.shape
    split = Mesh(mesh.devices.reshape(dp // CORES, CORES, mp), ("hi", "core", "mp"))
    wide = ("hi", "core")
    tokens = ("hi", "core", "mp")
    embed = P(None, wide)
    qkv = P(None, wide, None, "mp")
    mat = P(None, wide, "mp")
    head = P(wide, None)
    norm = P(None, None, wide)
    weights = (embed, qkv, mat, mat, mat, head, norm)
    return jax.shard_map(
        body,
        mesh=split,
        in_specs=(P(None, tokens, None),) * 3
        + (P(None, tokens),)
        + weights
        + tuple(spec for spec in weights for _ in range(2)),
        out_specs=(P(),) * 3 + tuple(spec for spec in weights for _ in range(3)),
        check_vma=False,
    )
```

```python
import jax
import jax.numpy as jnp
from jax import lax
from jax.experimental import pallas as pl
from jax.experimental.pallas import tpu as pltpu
import functools
from jax.sharding import Mesh
from jax.sharding import PartitionSpec as P

HEAD_DIM = 64
LAYERS = 2
HOR = 96
LOOK = 96
QUANT = 3
MICRO = 2
STEP = 10
NORMS = 5
CORES = 2
HEAD_PAD = 128

SMOOTHING = 0.1
LEVELS = (0.1, 0.5, 0.9)
CLIP_NORM = 0.0001
LEARN_RATE = 0.05
NORM_RATE = 0.5
BETA_ONE = 0.9
BETA_TWO = 0.999
EPSILON = 1e-12
WEIGHT_DECAY = 0.1

BF = jnp.bfloat16
F32 = jnp.float32


def swap_core(v):
    return lax.ppermute(v, "core", [(0, 1), (1, 0)])


def swap_hi(v, bit):
    size = lax.axis_size("hi")
    return lax.ppermute(v, "hi", [(i, i ^ (1 << bit)) for i in range(size)])


def turn_mp(v, by):
    size = lax.axis_size("mp")
    return lax.ppermute(v, "mp", [(i, (i + by) % size) for i in range(size)])


def hi_bits():
    return (lax.axis_size("hi") - 1).bit_length()


def bit_order(flip):
    bits = list(range(hi_bits()))
    return bits[::-1] if flip else bits


def after(v, *deps):
    return lax.optimization_barrier((v, *deps))[0]


def total_of(terms):
    total = terms[0].astype(F32)
    for term in terms[1:]:
        total = total + term.astype(F32)
    return total


class Gather:
    def __init__(self, v, flip):
        self.v = v
        self.order = bit_order(flip)
        self.done = []

    def hop(self, *deps):
        bit = self.order[len(self.done)]
        axis = sum(1 for other in self.done if other > bit)
        got = swap_hi(after(self.v, *deps) if deps else self.v, bit)
        self.v = jnp.stack([self.v, got], axis=axis)
        self.done.append(bit)
        return got

    def halves(self):
        v = self.v.reshape((-1, self.v.shape[-1]))
        return v, swap_core(v)


class Scatter:
    def __init__(self, own, other, flip):
        self.got = swap_core(other)
        bits = hi_bits()
        rows = own.shape[0] >> bits
        shape = (2,) * bits + (rows, own.shape[-1])
        self.terms = [own.reshape(shape), self.got.reshape(shape)]
        self.order = bit_order(flip)[::-1]
        self.left = list(range(bits))

    def hop(self):
        bit = self.order.pop(0)
        axis = sum(1 for other in self.left if other > bit)
        keep = [lax.index_in_dim(t, 0, axis, keepdims=False) for t in self.terms]
        send = [lax.index_in_dim(t, 1, axis, keepdims=False) for t in self.terms]
        out = total_of(send).astype(BF)
        self.got = swap_hi(out, bit)
        self.terms = keep + [self.got]
        self.left.remove(bit)
        return out


def gather_chunks(chunks):
    size = lax.axis_size("mp")
    half = size // 2
    bits = hi_bits()
    z_done, hop_done = (), [()] * bits
    out = []
    for v in chunks:
        v = after(v, *z_done) if z_done else v
        z_done = tuple(turn_mp(v, by) for by in range(1, size))
        blocks = (v,) + z_done
        pairs = [
            Gather(jnp.concatenate(blocks[flip * half : (flip + 1) * half], axis=1), flip)
            for flip in (False, True)
        ]
        for at in range(bits):
            hop_done[at] = tuple(pair.hop(*hop_done[at]) for pair in pairs)
        out.append(tuple(h for pair in pairs for h in pair.halves()))
    return out


class ScatterChunk:
    def __init__(self, halves):
        self.pairs = [Scatter(halves[0], halves[1], False), Scatter(halves[2], halves[3], True)]
        self.stage = 0

    def got(self):
        return tuple(pair.got for pair in self.pairs)

    def hop(self):
        return tuple(pair.hop() for pair in self.pairs)

    def turn(self):
        size = lax.axis_size("mp")
        half = size // 2
        blocks = []
        for pair in self.pairs:
            cols = pair.terms[0].shape[-1] // half
            for at in range(half):
                blocks.append([t[:, at * cols : (at + 1) * cols] for t in pair.terms])
        sent = [total_of(blocks[by]).astype(BF) for by in range(1, size)]
        self.turned = [turn_mp(v, -by) for by, v in zip(range(1, size), sent)]
        self.own = blocks[0]
        return tuple(sent)

    def step(self):
        if self.stage == hi_bits():
            out = self.turn()
        elif self.stage < hi_bits():
            out = self.hop()
        else:
            out = ()
        self.stage += 1
        return out

    def result(self):
        return total_of(self.own + self.turned)


def mm(a, b):
    return lax.dot_general(a, b, (((1,), (0,)), ((), ())), preferred_element_type=F32)


def mm_nt(a, b):
    return lax.dot_general(a, b, (((1,), (1,)), ((), ())), preferred_element_type=F32)


def mm_tn(a, b):
    return lax.dot_general(a, b, (((0,), (0,)), ((), ())), preferred_element_type=F32)


def unit_of(values):
    mean = jnp.mean(values, axis=-1, keepdims=True)
    centered = values - mean
    scaled = lax.rsqrt(jnp.mean(centered * centered, axis=-1, keepdims=True) + 1e-05)
    return centered * scaled, scaled


def norm_back(gradient, gain, unit, scaled):
    d_gain = jnp.sum(gradient * unit, axis=0, keepdims=True)
    d_shift = jnp.sum(gradient, axis=0, keepdims=True)
    d_unit = gradient * gain
    d_values = scaled * (
        d_unit
        - jnp.mean(d_unit, axis=-1, keepdims=True)
        - unit * jnp.mean(d_unit * unit, axis=-1, keepdims=True)
    )
    return d_values, d_gain, d_shift


def cut(pair, lo, hi):
    return jnp.concatenate([pair[0][:, lo:hi], pair[1][:, lo:hi]], axis=0)


def put(pair, lo, v):
    rows = pair[0].shape[0]
    pair[0][:, lo : lo + v.shape[1]] = v[:rows]
    pair[1][:, lo : lo + v.shape[1]] = v[rows:]


def affine(base, gs, row):
    return base[...] * gs[row : row + 1, :] + gs[row + 1 : row + 2, :]


def qkv_kernel(base, gs, w00, w01, w10, w11, q, kv, *, row, part):
    h = affine(base, gs, row).astype(BF)
    full = q.shape[1]
    for p, w in enumerate(((w00, w01), (w10, w11))):
        count = w[0].shape[1] // (4 * part)
        for jj in range(count):
            j = p * count + jj
            got = mm(h, cut(w, jj * 4 * part, (jj * 4 + 3) * part)).astype(BF)
            q[:, j * part : (j + 1) * part] = got[:, :part]
            kv[:, j * part : (j + 1) * part] = got[:, part : 2 * part]
            kv[:, full + j * part : full + (j + 1) * part] = got[:, 2 * part :]


def fill_bias(bias, id_row, id_col):
    bias[...] = jnp.where(id_col[...] == id_row[...], 0.0, -jnp.inf)


def head_lanes(v, h):
    lane = lax.broadcasted_iota(jnp.int32, v.shape, 1)
    return jnp.where(lane // HEAD_DIM == h, v, jnp.zeros_like(v))


def both_rows(own, other, at, part):
    return jnp.concatenate([own[:, at : at + part], other[:, at : at + part]], axis=0)


def attend_kernel(
    q, kv, kv_other, id_row, id_col, w00, w01, w10, w11, base, gs, mixed, lse, unit, scaled, bias, *, row, part
):
    fill_bias(bias, id_row, id_col)
    full = q.shape[1]
    total = affine(base, gs, row)
    for p, w in enumerate(((w00, w01), (w10, w11))):
        count = w[0].shape[1] // (4 * part)
        for jj in range(count):
            at = (p * count + jj) * part
            q_part = q[:, at : at + part] * 0.125
            k_part = both_rows(kv, kv_other, at, part)
            v_flip = both_rows(kv, kv_other, full + at, part).T
            outs = []
            for h in range(part // HEAD_DIM):
                s = mm_nt(k_part, head_lanes(q_part, h)) + bias[...]
                top = jnp.max(s, axis=0, keepdims=True)
                e = jnp.exp(s - top)
                sums = jnp.sum(e, axis=0, keepdims=True)
                o = mm(v_flip[h * HEAD_DIM : (h + 1) * HEAD_DIM], e.astype(BF))
                outs.append(o * (1.0 / sums))
                head = at // HEAD_DIM + h
                lse[head : head + 1, :] = top + jnp.log(sums)
            mixed_part = jnp.concatenate(outs, axis=0).T.astype(BF)
            mixed[:, at : at + part] = mixed_part
            total = total + mm_nt(mixed_part, cut(w, (jj * 4 + 3) * part, (jj * 4 + 4) * part))
    unit[...], scaled[...] = unit_of(total)


def erf(x):
    x = jnp.clip(x, -3.832506856900711, 3.832506856900711)
    x2 = x * x
    top = 0.00022905065861350646
    for c in (0.0034082910107109506, 0.050955695062380861, 0.18520832239976145, 1.128379143519084):
        top = top * x2 + c
    low = -1.1791602954361697e-7
    for c in (
        0.000023547966471313185,
        0.0010179625278914885,
        0.014070470171167667,
        0.11098505178285362,
        0.49746925110067538,
        1.0,
    ):
        low = low * x2 + c
    return x * top / low


def feed_kernel(unit_in, gs, w00, w01, w10, w11, act, slope, unit, scaled, *, row, wide):
    first = affine(unit_in, gs, row)
    y = first.astype(BF)
    total = first
    for p, w in enumerate(((w00, w01), (w10, w11))):
        count = w[0].shape[1] // (2 * wide)
        for jj in range(count):
            at = (p * count + jj) * wide
            lo = jj * 2 * wide
            inner = mm(y, cut(w, lo, lo + wide))
            cdf = 0.5 + 0.5 * erf(inner * 0.7071067811865476)
            bell = jnp.exp(-0.5 * inner * inner) * 0.3989422804014327
            act_part = (inner * cdf).astype(BF)
            act[:, at : at + wide] = act_part
            slope[:, at : at + wide] = (cdf + inner * bell).astype(BF)
            total = total + mm_nt(act_part, cut(w, lo + wide, lo + 2 * wide))
    unit[...], scaled[...] = unit_of(total)


def head_kernel(unit_in, gs, rest0, rest1, target, counted, loss, g_head0, g_head1, d_hidden, d_norm, *, row, last):
    unit, scaled = unit_of(affine(unit_in, gs, row))
    gain = gs[last : last + 1, :]
    final = (unit * gain + gs[last + 1 : last + 2, :]).astype(BF)
    size = rest0.shape[1] // (QUANT + 1)
    head = cut((rest0, rest1), size, rest0.shape[1])
    pred = mm(final, head)
    total = jnp.zeros((1, size), F32)
    grads = []
    for t, level in enumerate(LEVELS):
        gap = target[...] - pred[:, t * size : (t + 1) * size]
        x = gap * (-1.0 / SMOOTHING)
        e = jnp.exp(-jnp.abs(x))
        soft = jnp.maximum(x, 0.0) + jnp.log(1.0 + e)
        sig = jnp.where(x >= 0, 1.0, e) / (1.0 + e)
        total = total + jnp.sum((level * gap + SMOOTHING * soft) * counted[...], axis=0, keepdims=True)
        grads.append(((sig - level) * counted[...]).astype(BF))
    loss[...] = total
    d_pred = jnp.concatenate(grads, axis=1)
    put((g_head0, g_head1), 0, mm(final.T, d_pred).astype(BF))
    d_hidden[...], d_gain, d_shift = norm_back(mm_nt(d_pred, head), gain, unit, scaled)
    d_norm[...] = jnp.concatenate([d_gain, d_shift], axis=0)


def feed_back_kernel(
    grad, unit_two, scaled_two, unit_one, scaled_one, gs, act, slope, w00, w01, w10, w11,
    g00, g01, g10, g11, d_one, d_norm, *, row, wide,
):
    d_two, gain_two, shift_two = norm_back(
        grad[...], gs[row + 2 : row + 3, :], unit_two[...], scaled_two[...]
    )
    d_ffn = d_two.astype(BF)
    d_flip = d_ffn.T
    y_flip = affine(unit_one, gs, row).astype(BF).T
    total = d_two
    for p, (w, g) in enumerate((((w00, w01), (g00, g01)), ((w10, w11), (g10, g11)))):
        count = w[0].shape[1] // (2 * wide)
        for jj in range(count):
            at = (p * count + jj) * wide
            lo = jj * 2 * wide
            put(g, lo + wide, mm(d_flip, act[:, at : at + wide]).astype(BF))
            d_act = mm(d_ffn, cut(w, lo + wide, lo + 2 * wide))
            d_inner = (d_act * slope[:, at : at + wide].astype(F32)).astype(BF)
            put(g, lo, mm(y_flip, d_inner).astype(BF))
            total = total + mm_nt(d_inner, cut(w, lo, lo + wide))
    d_one[...], gain_one, shift_one = norm_back(
        total, gs[row : row + 1, :], unit_one[...], scaled_one[...]
    )
    d_norm[...] = jnp.concatenate([gain_one, shift_one, gain_two, shift_two], axis=0)


def attend_back_kernel(
    d_one, q, kv, kv_other, id_row, id_col, lse, mixed, w00, w01, w10, w11,
    g_out, d_q, d_kv, d_kv_other, bias, *, part,
):
    fill_bias(bias, id_row, id_col)
    full = q.shape[1]
    rows = q.shape[0]
    d_branch = d_one[...].astype(BF)
    g_out[...] = mm(d_branch.T, mixed[...]).astype(BF)
    for p, w in enumerate(((w00, w01), (w10, w11))):
        count = w[0].shape[1] // (4 * part)
        for jj in range(count):
            at = (p * count + jj) * part
            d_mixed = mm(d_branch, cut(w, (jj * 4 + 3) * part, (jj * 4 + 4) * part)).astype(BF)
            q_part = q[:, at : at + part] * 0.125
            k_part = both_rows(kv, kv_other, at, part)
            v_part = both_rows(kv, kv_other, full + at, part)
            k_flip = k_part.T
            pair = (d_mixed.astype(F32) * mixed[:, at : at + part].astype(F32)).T
            d_k = d_v = None
            d_q_flip = []
            for h in range(part // HEAD_DIM):
                head = at // HEAD_DIM + h
                q_head = head_lanes(q_part, h)
                d_head = head_lanes(d_mixed, h)
                probs = jnp.exp(mm_nt(k_part, q_head) + bias[...] - lse[head : head + 1, :])
                dots = jnp.sum(pair[h * HEAD_DIM : (h + 1) * HEAD_DIM], axis=0, keepdims=True)
                d_s = (probs * (mm_nt(v_part, d_head) - dots)).astype(BF)
                more_v = mm(probs.astype(BF), d_head)
                more_k = mm(d_s, q_head)
                d_v = more_v if d_v is None else d_v + more_v
                d_k = more_k if d_k is None else d_k + more_k
                d_q_flip.append(mm(k_flip[h * HEAD_DIM : (h + 1) * HEAD_DIM], d_s))
            d_q[:, at : at + part] = (jnp.concatenate(d_q_flip, axis=0) * 0.125).T.astype(BF)
            d_kv[:, at : at + part] = d_k[:rows]
            d_kv_other[:, at : at + part] = d_k[rows:].astype(BF)
            d_kv[:, full + at : full + at + part] = d_v[:rows]
            d_kv_other[:, full + at : full + at + part] = d_v[rows:].astype(BF)


def qkv_back_kernel(d_one, base, gs, d_q, d_kv, got, g_out, w00, w01, w10, w11, g00, g01, g10, g11, d_hidden, *, row, part):
    full = d_q.shape[1]
    h_flip = affine(base, gs, row).astype(BF).T
    total = d_one[...]
    for p, (w, g) in enumerate((((w00, w01), (g00, g01)), ((w10, w11), (g10, g11)))):
        count = w[0].shape[1] // (4 * part)
        for jj in range(count):
            at = (p * count + jj) * part
            lo = jj * 4 * part
            d_all = [d_q[:, at : at + part]]
            for base_at in (at, full + at):
                d_all.append(
                    (
                        d_kv[:, base_at : base_at + part]
                        + got[:, base_at : base_at + part].astype(F32)
                    ).astype(BF)
                )
            d_all = jnp.concatenate(d_all, axis=1)
            put(g, lo, mm(h_flip, d_all).astype(BF))
            put(g, lo + 3 * part, g_out[:, at : at + part])
            total = total + mm_nt(d_all, cut(w, lo, lo + 3 * part))
    d_hidden[...] = total


def kernel_call(kernel, outs, *args, scratch=(), us=1.0, **static):
    moved = sum(a.size * a.dtype.itemsize for a in args)
    moved += sum(o.size * jnp.dtype(o.dtype).itemsize for o in outs)
    whole = pl.BlockSpec(memory_space=pltpu.VMEM)
    return pl.pallas_call(
        functools.partial(kernel, **static),
        out_shape=tuple(outs),
        in_specs=[whole] * len(args),
        out_specs=tuple(whole for _ in outs),
        scratch_shapes=scratch,
        compiler_params=pltpu.CompilerParams(vmem_limit_bytes=48 * 1024 * 1024),
        cost_estimate=pl.CostEstimate(flops=int(us * 1.15e9), bytes_accessed=moved, transcendentals=0),
    )(*args)


def like(shape, dtype):
    return jax.ShapeDtypeStruct(shape, dtype)


def adam_update(weight, gradient, first_moment, second_moment, rate, decay):
    first_moment = BETA_ONE * first_moment + (1 - BETA_ONE) * gradient
    second_moment = BETA_TWO * second_moment + (1 - BETA_TWO) * gradient * gradient
    update = (
        first_moment
        / (1 - BETA_ONE**STEP)
        / (jnp.sqrt(second_moment / (1 - BETA_TWO**STEP)) + EPSILON)
    )
    return (weight - rate * (update + decay * weight), first_moment, second_moment)


def deal_rows(v):
    rows = v.shape[1] // CORES
    core = lax.axis_index("core")
    v = v.reshape(MICRO, CORES, rows, v.shape[-1])
    keep = lax.dynamic_index_in_dim(v, core, 1, keepdims=False)
    send = lax.dynamic_index_in_dim(v, 1 - core, 1, keepdims=False)
    got = swap_core(send)
    both = jnp.where(core == 0, jnp.concatenate([keep, got]), jnp.concatenate([got, keep]))
    return lax.all_to_all(both, "mp", 0, 0, tiled=True).reshape(-1, v.shape[-1])


def body(
    series,
    targets,
    valid,
    dataset_ids,
    embed_w,
    qkv_w,
    out_w,
    up_w,
    down_w,
    head_w,
    norm_params,
    *moments,
):
    (
        embed_first,
        embed_second,
        qkv_first,
        qkv_second,
        out_first,
        out_second,
        up_first,
        up_second,
        down_first,
        down_second,
        head_first,
        head_second,
        norm_first,
        norm_second,
    ) = moments
    width = embed_w.shape[1]
    part = qkv_w.shape[3]
    wide = up_w.shape[2]
    blocks_n = lax.axis_size("mp")

    low_pad = HEAD_PAD - LOOK - 2 * NORMS
    embed_cols = jnp.concatenate([embed_w.T, norm_params.reshape(-1, width).T], axis=1)
    head_cols = jnp.pad(head_w.reshape(width, QUANT, HOR), ((0, 0), (0, 0), (0, HEAD_PAD - HOR)))
    rest = Gather(
        jnp.concatenate(
            [jnp.pad(embed_cols, ((0, 0), (0, low_pad))), head_cols.reshape(width, -1)], axis=1
        ).astype(BF),
        False,
    )
    chunks = []
    for l in range(LAYERS):
        chunks.append(jnp.concatenate([qkv_w[l].reshape(width, -1), out_w[l]], axis=1).astype(BF))
        chunks.append(jnp.concatenate([up_w[l], down_w[l]], axis=1).astype(BF))
    chunks = gather_chunks(chunks)
    att, ffn = chunks[::2], chunks[1::2]
    for _ in range(hi_bits()):
        rest.hop()
    rest = rest.halves()
    embed_t = jnp.concatenate([r[:, :HEAD_PAD] for r in rest])
    model = embed_t.shape[0]
    ident = 2 * NORMS
    gs = jnp.concatenate(
        [
            embed_t[:, LOOK : LOOK + 2 * NORMS].T.astype(F32),
            jnp.ones((1, model), F32),
            jnp.zeros((5, model), F32),
        ],
        axis=0,
    )

    low = deal_rows(
        jnp.concatenate(
            [series, valid.astype(BF), dataset_ids[..., None].astype(BF)], axis=-1
        )
    )
    x_in = jnp.pad(low[:, :LOOK], ((0, 0), (0, HEAD_PAD - LOOK)))
    counted = jnp.pad(low[:, LOOK : LOOK + HOR].astype(F32), ((0, 0), (0, HEAD_PAD - HOR)))
    ids_here = low[:, LOOK + HOR :]
    ids_col = jnp.concatenate([ids_here, swap_core(ids_here)]).astype(F32)
    ids_row = ids_here.astype(F32).reshape(1, -1)
    target = jnp.pad(deal_rows(targets), ((0, 0), (0, HEAD_PAD - HOR)))
    rows = x_in.shape[0]
    heads = model // HEAD_DIM
    hidden_n = wide * blocks_n

    base, row = after(mm_nt(x_in, embed_t), target), ident
    stored = []
    for l in range(LAYERS):
        q, kv = kernel_call(
            qkv_kernel,
            (like((rows, model), BF), like((rows, 2 * model), BF)),
            base, gs, *att[l],
            us=1.3, row=row, part=part,
        )
        kv_other = swap_core(kv)
        mixed, lse, unit_one, scaled_one = kernel_call(
            attend_kernel,
            (like((rows, model), BF), like((heads, rows), F32), like((rows, model), F32), like((rows, 1), F32)),
            q, kv, kv_other, ids_row, ids_col, *att[l], base, gs,
            scratch=(pltpu.VMEM((2 * rows, rows), F32),),
            us=11, row=row, part=part,
        )
        act, slope, unit_two, scaled_two = kernel_call(
            feed_kernel,
            (like((rows, hidden_n), BF), like((rows, hidden_n), BF), like((rows, model), F32), like((rows, 1), F32)),
            unit_one, gs, *ffn[l],
            us=10, row=4 * l, wide=wide,
        )
        stored.append((base, row, q, kv, kv_other, mixed, lse, unit_one, scaled_one, act, slope, unit_two, scaled_two))
        base, row = unit_two, 4 * l + 2
    loss_row, *g_head, grad, d_norm_last = kernel_call(
        head_kernel,
        (like((1, HEAD_PAD), F32),)
        + (like((model // CORES, QUANT * HEAD_PAD), BF),) * CORES
        + (like((rows, model), F32), like((2, model), F32)),
        base, gs, *rest, target, counted,
        us=2, row=row, last=2 * NORMS - 2,
    )
    loss_here = jnp.sum(loss_row)
    norm_grads = [None] * LAYERS
    sums = []

    def steps():
        return [v for s in sums for v in s.step()]

    for l in reversed(range(LAYERS)):
        (base, row, q, kv, kv_other, mixed, lse, unit_one, scaled_one, act, slope, unit_two, scaled_two) = stored[l]
        *halves, d_one, norm_grads[l] = kernel_call(
            feed_back_kernel,
            tuple(like(w.shape, BF) for w in ffn[l]) + (like((rows, model), F32), like((4, model), F32)),
            grad, unit_two, scaled_two, unit_one, scaled_one, gs, act, slope, *ffn[l],
            us=10.5, row=4 * l, wide=wide,
        )
        d_one = after(d_one, *steps())
        sums.append(ScatterChunk(halves))
        g_out, d_q, d_kv, d_kv_other = kernel_call(
            attend_back_kernel,
            (like((model, model), BF), like((rows, model), BF), like((rows, 2 * model), F32), like((rows, 2 * model), BF)),
            d_one, q, kv, kv_other, ids_row, ids_col, lse, mixed, *att[l],
            scratch=(pltpu.VMEM((2 * rows, rows), F32),),
            us=15.5, part=part,
        )
        got = swap_core(d_kv_other)
        d_q = after(d_q, *steps())
        *halves, grad = kernel_call(
            qkv_back_kernel,
            tuple(like(w.shape, BF) for w in att[l]) + (like((rows, model), F32),),
            d_one, base, gs, d_q, d_kv, got, g_out, *att[l],
            us=5.5, row=row, part=part,
        )
        grad = after(grad, *steps())
        sums.append(ScatterChunk(halves))
    g_embed = mm_tn(grad.astype(BF), x_in)
    g_norm = jnp.concatenate(norm_grads + [d_norm_last], axis=0)
    g_low = jnp.concatenate(
        [g_embed[:, :LOOK], g_norm.T, g_embed[:, LOOK + 2 * NORMS :]], axis=1
    ).astype(BF)
    half = model // CORES
    g_rest = Scatter(
        jnp.concatenate([g_low[:half], g_head[0]], axis=1),
        jnp.concatenate([g_low[half:], g_head[1]], axis=1),
        False,
    )
    for _ in range(hi_bits()):
        g_rest.hop()
        steps()
    while steps():
        pass
    (g_ffn1, g_att1, g_ffn0, g_att0) = [s.result() for s in sums]
    g_att, g_ffn = (g_att0, g_att1), (g_ffn0, g_ffn1)
    mine = total_of(g_rest.terms).astype(BF)
    held = jnp.stack([mine] + [turn_mp(mine, by) for by in range(1, blocks_n)])
    rank = lax.axis_index("mp")
    g_rest = total_of(
        [
            lax.dynamic_index_in_dim(held, (rank - at) % blocks_n, 0, keepdims=False)
            for at in range(blocks_n)
        ]
    )
    head_part = g_rest[:, HEAD_PAD:].reshape(width, QUANT, HEAD_PAD)[:, :, :HOR].reshape(width, -1)
    g_rest = jnp.concatenate([g_rest[:, :LOOK], head_part, g_rest[:, LOOK : LOOK + 2 * NORMS]], axis=1)

    first_rank = (lax.axis_index("mp") == 0).astype(F32)
    squares = first_rank * jnp.sum(g_rest * g_rest)
    for g in g_att + g_ffn:
        squares = squares + jnp.sum(g * g)
    sums = jnp.zeros((1, 128), F32)
    sums = sums.at[0, 0].set(loss_here).at[0, 1].set(jnp.sum(counted)).at[0, 2].set(squares)
    count = lax.axis_size("hi") * CORES * blocks_n
    sums = jnp.sum(
        lax.all_to_all(
            jnp.broadcast_to(sums, (count, 128)), ("hi", "core", "mp"), 0, 0, tiled=True
        ),
        axis=0,
    )
    loss_sum, valid_count = sums[0], sums[1]
    grad_norm = jnp.sqrt(sums[2]) / valid_count
    factor = jnp.minimum(1.0, CLIP_NORM / grad_norm) / valid_count

    ga = jnp.stack(g_att) * factor
    gf = jnp.stack(g_ffn) * factor
    g_rest = g_rest * factor
    e_new = adam_update(embed_w, g_rest[:, :LOOK].T, embed_first, embed_second, LEARN_RATE, WEIGHT_DECAY)
    q_new = adam_update(
        qkv_w, ga[:, :, : 3 * part].reshape(qkv_w.shape), qkv_first, qkv_second, LEARN_RATE, WEIGHT_DECAY
    )
    o_new = adam_update(out_w, ga[:, :, 3 * part :], out_first, out_second, LEARN_RATE, WEIGHT_DECAY)
    u_new = adam_update(up_w, gf[:, :, :wide], up_first, up_second, LEARN_RATE, WEIGHT_DECAY)
    d_new = adam_update(down_w, gf[:, :, wide:], down_first, down_second, LEARN_RATE, WEIGHT_DECAY)
    h_new = adam_update(
        head_w, g_rest[:, LOOK : LOOK + QUANT * HOR], head_first, head_second, LEARN_RATE, WEIGHT_DECAY
    )
    n_new = adam_update(
        norm_params,
        g_rest[:, LOOK + QUANT * HOR :].T.reshape(norm_params.shape),
        norm_first,
        norm_second,
        NORM_RATE,
        0.0,
    )
    return (loss_sum, valid_count, grad_norm, *e_new, *q_new, *o_new, *u_new, *d_new, *h_new, *n_new)


def solution(mesh):
    dp, mp = mesh.devices.shape
    split = Mesh(mesh.devices.reshape(dp // CORES, CORES, mp), ("hi", "core", "mp"))
    wide = ("hi", "core")
    tokens = ("hi", "core", "mp")
    embed = P(None, wide)
    qkv = P(None, wide, None, "mp")
    mat = P(None, wide, "mp")
    head = P(wide, None)
    norm = P(None, None, wide)
    weights = (embed, qkv, mat, mat, mat, head, norm)
    return jax.shard_map(
        body,
        mesh=split,
        in_specs=(P(None, tokens, None),) * 3
        + (P(None, tokens),)
        + weights
        + tuple(spec for spec in weights for _ in range(2)),
        out_specs=(P(),) * 3 + tuple(spec for spec in weights for _ in range(3)),
        check_vma=False,
    )
```

```python
import functools

import jax
import jax.numpy as jnp
from jax import lax
from jax.experimental import pallas as pl
from jax.experimental.pallas import tpu as pltpu
from jax.sharding import Mesh
from jax.sharding import PartitionSpec as P

HEAD_DIM = 64
LAYERS = 2
HOR = 96
LOOK = 96
QUANT = 3
MICRO = 2
STEP = 10
NORMS = 5
CORES = 2
HEAD_PAD = 128

SMOOTHING = 0.1
LEVELS = (0.1, 0.5, 0.9)
CLIP_NORM = 0.0001
LEARN_RATE = 0.05
NORM_RATE = 0.5
BETA_ONE = 0.9
BETA_TWO = 0.999
EPSILON = 1e-12
WEIGHT_DECAY = 0.1

BF = jnp.bfloat16
F32 = jnp.float32


def swap_core(v):
    return lax.ppermute(v, "core", [(0, 1), (1, 0)])


def swap_hi(v, bit):
    size = lax.axis_size("hi")
    return lax.ppermute(v, "hi", [(i, i ^ (1 << bit)) for i in range(size)])


def turn_mp(v, by):
    size = lax.axis_size("mp")
    return lax.ppermute(v, "mp", [(i, (i + by) % size) for i in range(size)])


def hi_bits():
    return (lax.axis_size("hi") - 1).bit_length()


def bit_order(flip):
    bits = list(range(hi_bits()))
    return bits[::-1] if flip else bits


def after(v, *deps):
    return lax.optimization_barrier((v, *deps))[0] if deps else v


def total_of(terms):
    total = terms[0].astype(F32)
    for term in terms[1:]:
        total = total + term.astype(F32)
    return total


class Gather:
    def __init__(self, v, flip):
        self.v = v
        self.order = bit_order(flip)
        self.done = []

    def hop(self, before=(), beside=()):
        bit = self.order[len(self.done)]
        axis = sum(1 for other in self.done if other > bit)
        got = swap_hi(after(self.v, *before), bit)
        self.v = jnp.stack([self.v, after(got, *beside)], axis=axis)
        self.done.append(bit)
        return got

    def halves(self):
        v = self.v.reshape((-1, self.v.shape[-1]))
        return v, swap_core(v)


class Scatter:
    def __init__(self, own, other, cols):
        self.own, self.cols = own, cols
        self.got = swap_core(other)
        self.stages = [self.spread, self.turn]

    def step(self, *deps):
        return self.stages.pop(0)(*deps) if self.stages else []

    def spread(self, *deps):
        size = lax.axis_size("hi")
        rows = self.own.shape[0] // size
        got = after(self.got, *deps)
        parts = [[v[r * rows : (r + 1) * rows] for v in (self.own, got)] for r in range(size)]
        sent = [total_of(part).astype(BF) for part in parts[1:]]
        self.terms = parts[0]
        self.got = [
            lax.ppermute(v, "hi", [(i, i ^ r) for i in range(size)]) for r, v in zip(range(1, size), sent)
        ]
        return sent

    def turn(self, *deps):
        self.terms = self.terms + [after(v, *deps) for v in self.got]
        return self.send()

    def send(self):
        size = lax.axis_size("mp")
        cols = self.cols

        def block(j):
            return total_of([v[:, j * cols : (j + 1) * cols] for v in self.terms])

        shared = total_of([v[:, size * cols :] for v in self.terms]).astype(BF)
        sent = [jnp.concatenate([block(j).astype(BF), shared], axis=1) for j in range(1, size)]
        self.parts = [block(0), shared] + [turn_mp(v, -j) for j, v in zip(range(1, size), sent)]
        return sent


class Halving:
    def __init__(self, halves, cols):
        self.cols = cols
        self.got = [swap_core(halves[1]), swap_core(halves[3])]
        self.stages = [self.halve] * hi_bits() + [self.turn]
        self.shape = (2,) * hi_bits() + (halves[0].shape[0] >> hi_bits(), halves[0].shape[1])
        self.pairs = [[halves[0].reshape(self.shape)], [halves[2].reshape(self.shape)]]
        self.orders = [bit_order(flip)[::-1] for flip in (False, True)]
        self.left = [list(range(hi_bits())) for _ in range(2)]

    def step(self, *deps):
        return self.stages.pop(0)(*deps) if self.stages else []

    def land(self, *deps):
        for p in range(2):
            self.pairs[p].append(after(self.got[p], *deps).reshape(self.pairs[p][0].shape))

    def halve(self, *deps):
        self.land(*deps)
        sent = []
        for p in range(2):
            bit = self.orders[p].pop(0)
            axis = sum(1 for other in self.left[p] if other > bit)
            send = total_of([lax.index_in_dim(t, 1, axis, keepdims=False) for t in self.pairs[p]]).astype(BF)
            self.pairs[p] = [lax.index_in_dim(t, 0, axis, keepdims=False) for t in self.pairs[p]]
            self.left[p].remove(bit)
            self.got[p] = swap_hi(send, bit)
            sent.append(send)
        return sent

    def turn(self, *deps):
        self.land(*deps)
        size = lax.axis_size("mp") // 2
        cols = self.cols

        def block(j):
            p, at = j // size, j % size * cols
            return total_of([v[:, at : at + cols] for v in self.pairs[p]])

        sent = [block(j).astype(BF) for j in range(1, 2 * size)]
        self.parts = [block(0), sent[0][:0]] + [turn_mp(v, -j) for j, v in enumerate(sent, 1)]
        return sent

    def landed(self):
        return [] if self.stages else self.parts[2:]


def turns(v):
    return tuple(turn_mp(v, by) for by in range(1, lax.axis_size("mp")))


def pairs_of(v, turned):
    half = lax.axis_size("mp") // 2
    blocks = (v,) + turned
    return [
        Gather(jnp.concatenate(blocks[flip * half : (flip + 1) * half], axis=1), flip)
        for flip in (False, True)
    ]


def halves_of(pairs):
    return tuple(h for pair in pairs for h in pair.halves())


class Halves:
    def __init__(self, arrays):
        self.arrays = arrays
        self.blocks = lax.axis_size("mp")

    def specs(self):
        return [pl.BlockSpec(memory_space=pltpu.VMEM)] * len(self.arrays)

    def reader(self, refs):
        half = self.blocks // 2

        def read(j, lo, hi):
            own, other = refs[2 * (j // half)], refs[2 * (j // half) + 1]
            at = j % half * (own.shape[1] // half)
            return cut((own, other), at + lo, at + hi)

        return read


class Shards:
    def __init__(self, own, at, other, size):
        self.own, self.at, self.other, self.size = own, at, other, size
        self.blocks = lax.axis_size("mp")
        self.hi = lax.axis_size("hi")
        self.arrays = ((own,) * self.hi + (other,) * self.hi) * self.blocks

    def specs(self):
        width, blocks, size = self.own.shape[1], self.blocks, self.size
        return [
            pl.BlockSpec(
                (1, width, size),
                lambda i, pos, r=r, j=j, at=at: (
                    (pos[2] ^ r) * blocks + (pos[1] + blocks - j) % blocks, 0, at,
                ),
            )
            for j in range(blocks)
            for at in (self.at, 0)
            for r in range(self.hi)
        ]

    def reader(self, refs):
        def read(j, lo, hi):
            count = CORES * self.hi
            return jnp.concatenate([ref[0, :, lo:hi] for ref in refs[j * count : (j + 1) * count]], axis=0)

        return read


class GradOut:
    def __init__(self, width, cols, more=0, pairs=True):
        self.cols = cols
        self.count = lax.axis_size("mp") // 2 if pairs else lax.axis_size("mp") + 1
        size = self.count * cols if pairs else (self.count - 1) * cols + more
        self.shapes = (like((width // CORES, size), BF),) * (4 if pairs else 2)

    def writer(self, refs, pos):
        def write(j, lo, v):
            p = j // self.count
            put(refs[2 * p : 2 * p + 2], j % self.count * self.cols + lo, v)

        return write


def mm(a, b):
    return lax.dot_general(a, b, (((1,), (0,)), ((), ())), preferred_element_type=F32)


def mm_nt(a, b):
    return lax.dot_general(a, b, (((1,), (1,)), ((), ())), preferred_element_type=F32)


def mm_tn(a, b):
    return lax.dot_general(a, b, (((0,), (0,)), ((), ())), preferred_element_type=F32)


def unit_of(values):
    mean = jnp.mean(values, axis=-1, keepdims=True)
    centered = values - mean
    scaled = lax.rsqrt(jnp.mean(centered * centered, axis=-1, keepdims=True) + 1e-05)
    return centered * scaled, scaled


def norm_back(gradient, gain, unit, scaled):
    d_gain = jnp.sum(gradient * unit, axis=0, keepdims=True)
    d_shift = jnp.sum(gradient, axis=0, keepdims=True)
    d_unit = gradient * gain
    d_values = scaled * (
        d_unit
        - jnp.mean(d_unit, axis=-1, keepdims=True)
        - unit * jnp.mean(d_unit * unit, axis=-1, keepdims=True)
    )
    return d_values, d_gain, d_shift


def cut(pair, lo, hi):
    return jnp.concatenate([pair[0][:, lo:hi], pair[1][:, lo:hi]], axis=0)


def put(pair, lo, v):
    rows = pair[0].shape[0]
    pair[0][:, lo : lo + v.shape[1]] = v[:rows]
    pair[1][:, lo : lo + v.shape[1]] = v[rows:]


def affine(base, gs, row):
    return base[...] * gs[row : row + 1, :] + gs[row + 1 : row + 2, :]


def pack_kernel(qkv, out, up, down, *outs):
    part, wide = out.shape[2], up.shape[2]
    outs = list(outs)
    places = [(0, outs[0], 0), (1, outs[-1], outs[-1].shape[1] - 4 * part)]
    for l, ref, at in places:
        for c in range(3):
            ref[:, at + c * part : at + (c + 1) * part] = qkv[l, :, c, :].astype(BF)
        ref[:, at + 3 * part : at + 4 * part] = out[l].astype(BF)
    for l in range(LAYERS):
        outs[1 + l][:, :wide] = up[l].astype(BF)
        outs[1 + l][:, wide : 2 * wide] = down[l].astype(BF)


def qkv_kernel(ins, w, outs, *, row, part):
    base, gs = ins
    q, kv = outs
    h = affine(base, gs, row).astype(BF)
    full = q.shape[1]
    for j in range(full // part):
        got = mm(h, w(j, 0, 3 * part)).astype(BF)
        q[:, j * part : (j + 1) * part] = got[:, :part]
        kv[:, j * part : (j + 1) * part] = got[:, part : 2 * part]
        kv[:, full + j * part : full + (j + 1) * part] = got[:, 2 * part :]


def fill_bias(bias, id_row, id_col):
    bias[...] = jnp.where(id_col[...] == id_row[...], 0.0, -jnp.inf)


def head_lanes(v, h):
    lane = lax.broadcasted_iota(jnp.int32, v.shape, 1)
    return jnp.where(lane // HEAD_DIM == h, v, jnp.zeros_like(v))


def both_rows(own, other, at, part):
    return jnp.concatenate([own[:, at : at + part], other[:, at : at + part]], axis=0)


def attend_kernel(ins, w, outs, bias, *, row, part):
    q, kv, kv_other, id_row, id_col, base, gs = ins
    mixed, lse, unit, scaled = outs
    fill_bias(bias, id_row, id_col)
    full = q.shape[1]
    total = affine(base, gs, row)
    for j in range(full // part):
        at = j * part
        q_part = q[:, at : at + part] * 0.125
        k_part = both_rows(kv, kv_other, at, part)
        v_flip = both_rows(kv, kv_other, full + at, part).T
        flat = []
        for h in range(part // HEAD_DIM):
            s = mm_nt(k_part, head_lanes(q_part, h)) + bias[...]
            top = jnp.max(s, axis=0, keepdims=True)
            e = jnp.exp(s - top)
            sums = jnp.sum(e, axis=0, keepdims=True)
            o = mm(v_flip[h * HEAD_DIM : (h + 1) * HEAD_DIM], e.astype(BF))
            flat.append(o * (1.0 / sums))
            head = at // HEAD_DIM + h
            lse[head : head + 1, :] = top + jnp.log(sums)
        mixed_part = jnp.concatenate(flat, axis=0).T.astype(BF)
        mixed[:, at : at + part] = mixed_part
        total = total + mm_nt(mixed_part, w(j, 3 * part, 4 * part))
    unit[...], scaled[...] = unit_of(total)


def erf(x):
    x = jnp.clip(x, -3.832506856900711, 3.832506856900711)
    x2 = x * x
    top = 0.00022905065861350646
    for c in (0.0034082910107109506, 0.050955695062380861, 0.18520832239976145, 1.128379143519084):
        top = top * x2 + c
    low = -1.1791602954361697e-7
    for c in (
        0.000023547966471313185,
        0.0010179625278914885,
        0.014070470171167667,
        0.11098505178285362,
        0.49746925110067538,
        1.0,
    ):
        low = low * x2 + c
    return x * top / low


def feed_kernel(ins, w, outs, *, row, wide):
    unit_in, gs = ins
    act, slope, unit, scaled = outs
    first = affine(unit_in, gs, row)
    y = first.astype(BF)
    total = first
    for j in range(act.shape[1] // wide):
        at = j * wide
        inner = mm(y, w(j, 0, wide))
        cdf = 0.5 + 0.5 * erf(inner * 0.7071067811865476)
        bell = jnp.exp(-0.5 * inner * inner) * 0.3989422804014327
        act_part = (inner * cdf).astype(BF)
        act[:, at : at + wide] = act_part
        slope[:, at : at + wide] = (cdf + inner * bell).astype(BF)
        total = total + mm_nt(act_part, w(j, wide, 2 * wide))
    unit[...], scaled[...] = unit_of(total)


def head_kernel(ins, w, outs, *, row, last):
    unit_in, gs, rest0, rest1, target, counted = ins
    loss, g_head0, g_head1, d_hidden, d_norm = outs
    unit, scaled = unit_of(affine(unit_in, gs, row))
    gain = gs[last : last + 1, :]
    final = (unit * gain + gs[last + 1 : last + 2, :]).astype(BF)
    size = rest0.shape[1] // (QUANT + 1)
    head = cut((rest0, rest1), size, rest0.shape[1])
    pred = mm(final, head)
    total = jnp.zeros((1, size), F32)
    grads = []
    for t, level in enumerate(LEVELS):
        gap = target[...] - pred[:, t * size : (t + 1) * size]
        x = gap * (-1.0 / SMOOTHING)
        e = jnp.exp(-jnp.abs(x))
        soft = jnp.maximum(x, 0.0) + jnp.log(1.0 + e)
        sig = jnp.where(x >= 0, 1.0, e) / (1.0 + e)
        total = total + jnp.sum((level * gap + SMOOTHING * soft) * counted[...], axis=0, keepdims=True)
        grads.append(((sig - level) * counted[...]).astype(BF))
    loss[...] = jnp.concatenate([total, jnp.sum(counted[...], axis=0, keepdims=True)], axis=0)
    d_pred = jnp.concatenate(grads, axis=1)
    put((g_head0, g_head1), 0, mm(final.T, d_pred).astype(BF))
    d_hidden[...], d_gain, d_shift = norm_back(mm_nt(d_pred, head), gain, unit, scaled)
    d_norm[...] = jnp.concatenate([d_gain, d_shift], axis=0)


def feed_back_kernel(ins, w, outs, g, *, row, wide):
    grad, unit_two, scaled_two, unit_one, scaled_one, gs, act, slope = ins
    d_one, d_norm = outs
    d_two, gain_two, shift_two = norm_back(
        grad[...], gs[row + 2 : row + 3, :], unit_two[...], scaled_two[...]
    )
    d_ffn = d_two.astype(BF)
    d_flip = d_ffn.T
    y_flip = affine(unit_one, gs, row).astype(BF).T
    total = d_two
    for j in range(act.shape[1] // wide):
        at = j * wide
        g(j, wide, mm(d_flip, act[:, at : at + wide]).astype(BF))
        d_act = mm(d_ffn, w(j, wide, 2 * wide))
        d_inner = (d_act * slope[:, at : at + wide].astype(F32)).astype(BF)
        g(j, 0, mm(y_flip, d_inner).astype(BF))
        total = total + mm_nt(d_inner, w(j, 0, wide))
    d_one[...], gain_one, shift_one = norm_back(
        total, gs[row : row + 1, :], unit_one[...], scaled_one[...]
    )
    d_norm[...] = jnp.concatenate([gain_one, shift_one, gain_two, shift_two], axis=0)


def attend_back_kernel(ins, w, outs, bias, *, part, first):
    d_one, q, kv, kv_other, id_row, id_col, lse, mixed = ins
    g_out, d_q, d_kv, d_kv_other = outs
    fill_bias(bias, id_row, id_col)
    full = q.shape[1]
    rows, here = d_q.shape
    d_branch = d_one[...].astype(BF)
    g_out[...] = mm(d_branch.T, mixed[:, first * part : first * part + here]).astype(BF)
    for j in range(first, first + here // part):
        at, to = j * part, (j - first) * part
        d_mixed = mm(d_branch, w(j, 3 * part, 4 * part)).astype(BF)
        q_part = q[:, at : at + part] * 0.125
        k_part = both_rows(kv, kv_other, at, part)
        v_part = both_rows(kv, kv_other, full + at, part)
        k_flip = k_part.T
        pair = (d_mixed.astype(F32) * mixed[:, at : at + part].astype(F32)).T
        d_k = d_v = None
        d_q_flip = []
        for h in range(part // HEAD_DIM):
            head = at // HEAD_DIM + h
            q_head = head_lanes(q_part, h)
            d_head = head_lanes(d_mixed, h)
            probs = jnp.exp(mm_nt(k_part, q_head) + bias[...] - lse[head : head + 1, :])
            dots = jnp.sum(pair[h * HEAD_DIM : (h + 1) * HEAD_DIM], axis=0, keepdims=True)
            d_s = (probs * (mm_nt(v_part, d_head) - dots)).astype(BF)
            more_v = mm(probs.astype(BF), d_head)
            more_k = mm(d_s, q_head)
            d_v = more_v if d_v is None else d_v + more_v
            d_k = more_k if d_k is None else d_k + more_k
            d_q_flip.append(mm(k_flip[h * HEAD_DIM : (h + 1) * HEAD_DIM], d_s))
        d_q[:, to : to + part] = (jnp.concatenate(d_q_flip, axis=0) * 0.125).T.astype(BF)
        d_kv[:, to : to + part] = d_k[:rows]
        d_kv_other[:, to : to + part] = d_k[rows:].astype(BF)
        d_kv[:, here + to : here + to + part] = d_v[:rows]
        d_kv_other[:, here + to : here + to + part] = d_v[rows:].astype(BF)


def qkv_back_kernel(ins, w, outs, g, *, row, part):
    d_one, base, gs, *rest = ins
    halves, rest = (rest[:4], rest[4:8]), rest[8:]
    (d_hidden,) = outs
    full = d_one.shape[1]
    h_flip = affine(base, gs, row).astype(BF).T
    total = d_one[...]
    for j in range(full // part):
        here = halves[0][0].shape[1]
        d_q, d_kv, got, g_out = halves[j * part // here]
        at = j * part % here
        d_all = [d_q[:, at : at + part]]
        for base_at in (at, here + at):
            d_all.append(
                (
                    d_kv[:, base_at : base_at + part] + got[:, base_at : base_at + part].astype(F32)
                ).astype(BF)
            )
        d_all = jnp.concatenate(d_all, axis=1)
        g(j, 0, mm(h_flip, d_all).astype(BF))
        g(j, 3 * part, g_out[:, at : at + part])
        total = total + mm_nt(d_all, w(j, 0, 3 * part))
    d_hidden[...] = total
    if rest:
        x_in, head0, head1, *norms = rest
        rows = [jnp.zeros((LOOK, total.shape[1]), F32)] + [n[...] for n in norms]
        rows.append(jnp.zeros((HEAD_PAD - LOOK - 2 * NORMS, total.shape[1]), F32))
        g_low = mm(total.astype(BF).T, x_in[...]) + jnp.concatenate(rows, axis=0).T
        g(full // part, 0, g_low.astype(BF))
        g(full // part, HEAD_PAD, jnp.concatenate([head0[...], head1[...]], axis=0))


def finish_kernel(at, *refs, blocks, shared):
    count = len(shared)
    ins, outs = refs[: 1 + count * (blocks + 1)], refs[1 + count * (blocks + 1) :]
    z = at[1]
    squares = jnp.zeros((), F32)
    for c in range(count):
        own, common, *turned = ins[1 + c * (blocks + 1) : 1 + (c + 1) * (blocks + 1)]
        cols = own.shape[1]
        total = own[...]
        for t in turned:
            total = total + t[:, :cols].astype(F32)
        outs[c][...] = total
        squares = squares + jnp.sum(total * total)
        if shared[c]:
            held = [common[...].astype(F32)] + [t[:, cols:].astype(F32) for t in turned]
            total = jnp.zeros_like(held[0])
            for owner in range(blocks):
                by = (z + blocks - owner) % blocks
                term = held[0]
                for j in range(1, blocks):
                    term = jnp.where(by == j, held[j], term)
                total = total + term
            outs[count][...] = total
            squares = squares + jnp.where(z == 0, jnp.sum(total * total), 0.0)
    loss = ins[0]
    place = lax.broadcasted_iota(jnp.int32, outs[-1].shape, 1)
    outs[-1][...] = jnp.where(
        place == 0,
        jnp.sum(loss[0:1, :]),
        jnp.where(place == 1, jnp.sum(loss[1:2, :]), jnp.where(place == 2, squares, 0.0)),
    )


def kernel_call(kernel, pos, ins, weights, outs, grads=None, scratch=(), us=1.0, **static):
    whole = pl.BlockSpec(memory_space=pltpu.VMEM)
    w_arrays = weights.arrays if weights else ()
    g_shapes = grads.shapes if grads else ()

    def run(at, *refs):
        refs = list(refs)

        def take(count):
            got = refs[:count]
            del refs[:count]
            return got

        in_refs = take(len(ins))
        w_refs = take(len(w_arrays))
        out_refs = take(len(outs))
        g_refs = take(len(g_shapes))
        more = [grads.writer(g_refs, at)] if grads else []
        kernel(in_refs, weights.reader(w_refs) if weights else None, out_refs, *more, *refs, **static)

    return pl.pallas_call(
        run,
        out_shape=tuple(outs) + tuple(g_shapes),
        grid_spec=pltpu.PrefetchScalarGridSpec(
            num_scalar_prefetch=1,
            grid=(1,),
            in_specs=[whole] * len(ins) + (weights.specs() if weights else []),
            out_specs=tuple(whole for _ in range(len(outs) + len(g_shapes))),
            scratch_shapes=scratch,
        ),
        compiler_params=pltpu.CompilerParams(vmem_limit_bytes=20 * 1024 * 1024),
        cost_estimate=pl.CostEstimate(flops=int(us * 1.15e9), bytes_accessed=0, transcendentals=0),
    )(pos, *ins, *w_arrays)


def kernel_call_plain(kernel, outs, *args, pos=None):
    whole = pl.BlockSpec(memory_space=pltpu.VMEM)
    first = [] if pos is None else [pl.BlockSpec(memory_space=pltpu.SMEM)]
    return pl.pallas_call(
        kernel,
        out_shape=outs,
        in_specs=first + [whole] * len(args),
        out_specs=tuple(whole for _ in outs),
        compiler_params=pltpu.CompilerParams(vmem_limit_bytes=20 * 1024 * 1024),
    )(*(() if pos is None else (pos,)), *args)


def like(shape, dtype):
    return jax.ShapeDtypeStruct(shape, dtype)


def adam_update(weight, gradient, first_moment, second_moment, rate, decay):
    first_moment = BETA_ONE * first_moment + (1 - BETA_ONE) * gradient
    second_moment = BETA_TWO * second_moment + (1 - BETA_TWO) * gradient * gradient
    update = (
        first_moment
        / (1 - BETA_ONE**STEP)
        / (jnp.sqrt(second_moment / (1 - BETA_TWO**STEP)) + EPSILON)
    )
    return (weight - rate * (update + decay * weight), first_moment, second_moment)


def deal_swap(v):
    rows = v.shape[1] // CORES
    core = lax.axis_index("core")
    v = v.reshape(MICRO, CORES, rows, v.shape[-1])
    keep = lax.dynamic_index_in_dim(v, core, 1, keepdims=False)
    send = lax.dynamic_index_in_dim(v, 1 - core, 1, keepdims=False)
    got = swap_core(send)
    return jnp.where(core == 0, jnp.concatenate([keep, got]), jnp.concatenate([got, keep]))


def deal_rows(v):
    size = lax.axis_size("mp")
    z = lax.axis_index("mp")
    parts = [lax.dynamic_index_in_dim(v, (z + by) % size, 0, keepdims=False) for by in range(size)]
    return jnp.concatenate(parts[:1] + [turn_mp(parts[by], by) for by in range(1, size)])


def body(
    series,
    targets,
    valid,
    dataset_ids,
    embed_w,
    qkv_w,
    out_w,
    up_w,
    down_w,
    head_w,
    norm_params,
    *moments,
):
    (
        embed_first,
        embed_second,
        qkv_first,
        qkv_second,
        out_first,
        out_second,
        up_first,
        up_second,
        down_first,
        down_second,
        head_first,
        head_second,
        norm_first,
        norm_second,
    ) = moments
    width = embed_w.shape[1]
    part = qkv_w.shape[3]
    wide = up_w.shape[2]
    blocks_n = lax.axis_size("mp")

    bits = hi_bits()
    hi_at, core_at, z_at = lax.axis_index("hi"), lax.axis_index("core"), lax.axis_index("mp")
    pos = jnp.stack([hi_at * CORES + core_at, z_at, hi_at]).astype(jnp.int32)
    att_w, ffn_w, late = {}, {}, None
    placed = width % 16 == 0
    packed = kernel_call_plain(
        pack_kernel,
        tuple(like((width, cols), BF) for cols in (4 * part, 2 * wide, 2 * wide, 4 * part))
        if not placed
        else (like((width, 4 * part), BF), like((width, 2 * wide), BF), like((width, 2 * wide + 4 * part), BF)),
        qkv_w, out_w, up_w, down_w,
    )
    att_w[0], ffn_w[0], ffn_w[1], att_w[1] = (*packed, None) if placed else packed
    if placed:
        late = lax.all_gather(ffn_w[1], ("hi", "mp"), axis=0, tiled=False)
        late = late.reshape((-1,) + late.shape[-2:])

    low_pad = HEAD_PAD - LOOK - 2 * NORMS
    embed_cols = jnp.concatenate([embed_w.T, norm_params.reshape(-1, width).T], axis=1)
    head_cols = jnp.pad(head_w.reshape(width, QUANT, HOR), ((0, 0), (0, 0), (0, HEAD_PAD - HOR)))
    rest = Gather(
        jnp.concatenate(
            [jnp.pad(embed_cols, ((0, 0), (0, low_pad))), head_cols.reshape(width, -1)], axis=1
        ).astype(BF),
        False,
    )
    low = deal_swap(
        jnp.concatenate([series, valid.astype(BF), dataset_ids[..., None].astype(BF)], axis=-1)
    )
    z_att = turns(att_w[0])
    rest.hop()
    att_pairs = pairs_of(att_w[0], z_att)
    hop_att = [pair.hop() for pair in att_pairs]
    low = deal_rows(after(low, *hop_att))
    for _ in range(1, bits):
        rest.hop(before=hop_att)
    rest = rest.halves()
    ffn_first = after(ffn_w[0], *hop_att)
    z_ffn = turns(ffn_first)
    for _ in range(1, bits):
        hop_att = [pair.hop() for pair in att_pairs]
    att = [Halves(halves_of(att_pairs))]
    ffn_pairs = pairs_of(ffn_first, z_ffn)
    for _ in range(bits - 1):
        for pair in ffn_pairs:
            pair.hop()

    embed_t = jnp.concatenate([r[:, :HEAD_PAD] for r in rest])
    model = embed_t.shape[0]
    ident = 2 * NORMS
    gs = jnp.concatenate(
        [
            embed_t[:, LOOK : LOOK + 2 * NORMS].T.astype(F32),
            jnp.ones((1, model), F32),
            jnp.zeros((5, model), F32),
        ],
        axis=0,
    )
    x_in = jnp.pad(low[:, :LOOK], ((0, 0), (0, HEAD_PAD - LOOK)))
    counted = jnp.pad(low[:, LOOK : LOOK + HOR].astype(F32), ((0, 0), (0, HEAD_PAD - HOR)))
    ids_here = low[:, LOOK + HOR :]
    ids_col = jnp.concatenate([ids_here, swap_core(ids_here)]).astype(F32)
    ids_row = ids_here.astype(F32).reshape(1, -1)
    rows = x_in.shape[0]
    heads = model // HEAD_DIM
    hidden_n = wide * blocks_n

    base, row = mm_nt(x_in, embed_t), ident
    stored = []
    ffn = []
    for l in range(LAYERS):
        q, kv = kernel_call(
            qkv_kernel, pos, (base, gs), att[l],
            (like((rows, model), BF), like((rows, 2 * model), BF)),
            us=1.3, row=row, part=part,
        )
        kv_other = swap_core(kv)
        if l == 0:
            q = after(q, *(pair.v for pair in ffn_pairs))
        mixed, lse, unit_one, scaled_one = kernel_call(
            attend_kernel, pos, (q, kv, kv_other, ids_row, ids_col, base, gs), att[l],
            (like((rows, model), BF), like((heads, rows), F32), like((rows, model), F32), like((rows, 1), F32)),
            scratch=(pltpu.VMEM((2 * rows, rows), F32),),
            us=11, row=row, part=part,
        )
        if l == 0:
            for pair in ffn_pairs:
                pair.hop(before=(kv,), beside=(mixed,))
            ffn.append(Halves(halves_of(ffn_pairs)))
            if not placed:
                for kept, v in ((att, att_w[1]), (ffn, ffn_w[1])):
                    pairs = pairs_of(v, turns(v))
                    for _ in range(bits):
                        for pair in pairs:
                            pair.hop()
                    kept.append(Halves(halves_of(pairs)))
        act, slope, unit_two, scaled_two = kernel_call(
            feed_kernel, pos, (unit_one, gs), ffn[l],
            (like((rows, hidden_n), BF), like((rows, hidden_n), BF), like((rows, model), F32), like((rows, 1), F32)),
            us=10, row=4 * l, wide=wide,
        )
        stored.append((base, row, q, kv, kv_other, mixed, lse, unit_one, scaled_one, act, slope, unit_two, scaled_two))
        base, row = unit_two, 4 * l + 2
        if l == 0 and placed:
            late = after(late, unit_two)
            first, second = late[:, :, 2 * wide :], late[:, :, : 2 * wide]
            other = swap_core(first)
            att.append(Shards(late, 2 * wide // (4 * part), other, 4 * part))
            ffn.append(Shards(late, 0, swap_core(after(second, other)), 2 * wide))
        if l == 0:
            target = deal_rows(deal_swap(after(targets, unit_two)))
            target = jnp.pad(target, ((0, 0), (0, HEAD_PAD - HOR)))
            base = after(base, target)
    loss_row, *g_head, grad, d_norm_last = kernel_call(
        head_kernel, pos, (base, gs, *rest, target, counted), None,
        (like((2, HEAD_PAD), F32),)
        + (like((model // CORES, QUANT * HEAD_PAD), BF),) * CORES
        + (like((rows, model), F32), like((2, model), F32)),
        us=2, row=row, last=2 * NORMS - 2,
    )
    norm_grads = [None] * LAYERS
    sums = []

    def feed_back(l, grad):
        unit_one, scaled_one, act, slope, unit_two, scaled_two = stored[l][7:]
        return kernel_call(
            feed_back_kernel, pos,
            (grad, unit_two, scaled_two, unit_one, scaled_one, gs, act, slope), ffn[l],
            (like((rows, model), F32), like((4, model), F32)),
            grads=GradOut(model, 2 * wide),
            us=10.5, row=4 * l, wide=wide,
        )

    def attend_back(l, d_one, half):
        q, kv, kv_other, mixed, lse = stored[l][2:7]
        here = model // 2
        g_out, d_q, d_kv, d_kv_other = kernel_call(
            attend_back_kernel, pos,
            (d_one, q, kv, kv_other, ids_row, ids_col, lse, mixed), att[l],
            (like((model, here), BF), like((rows, here), BF), like((rows, 2 * here), F32), like((rows, 2 * here), BF)),
            scratch=(pltpu.VMEM((2 * rows, rows), F32),),
            us=8, part=part, first=half * here // part,
        )
        return d_q, d_kv, swap_core(d_kv_other), g_out

    def qkv_back(l, d_one, *args):
        base, row = stored[l][:2]
        more = (x_in, *g_head, *norm_grads, d_norm_last) if l == 0 else ()
        return kernel_call(
            qkv_back_kernel, pos, (d_one, base, gs, *args, *more), att[l],
            (like((rows, model), F32),),
            grads=GradOut(model, 4 * part, more=(1 + QUANT) * HEAD_PAD, pairs=l > 0),
            us=5.5, row=row, part=part,
        )

    d_one, norm_grads[1], *halves = feed_back(1, grad)
    ffn_sum = Halving(halves, 2 * wide)
    first = attend_back(1, d_one, 0)
    sent = ffn_sum.step(first[0])
    second = attend_back(1, after(d_one, first[0], *sent), 1)
    sent = ffn_sum.step(second[0])
    grad, *halves = qkv_back(1, after(d_one, *sent), *first, *second)
    att_sum = Halving(halves, 4 * part)
    sent = ffn_sum.step(grad)

    d_one, norm_grads[0], *halves = feed_back(0, after(grad, *sent))
    ffn_low = Halving(halves, 2 * wide)
    sent = att_sum.step(d_one) + ffn_sum.step(d_one)
    d_one = after(d_one, *sent, *ffn_sum.landed())
    first = attend_back(0, d_one, 0)
    sent = att_sum.step(first[0]) + ffn_low.step(first[0])
    second = attend_back(0, after(d_one, first[0], *sent), 1)
    sent = att_sum.step(second[0]) + ffn_low.step(second[0])
    _, own, other = qkv_back(0, after(d_one, *sent), *first, *second)
    att_low = Scatter(own, after(other, *att_sum.landed()), 4 * part)
    for chunk in (ffn_sum, att_sum, ffn_low):
        while chunk.stages:
            chunk.step(own)
    att_low.step()
    att_low.step(*ffn_low.landed())
    sums = [ffn_sum, att_sum, ffn_low, att_low]

    count = lax.axis_size("hi") * CORES * blocks_n
    *grads, g_rest, scalars = kernel_call_plain(
        functools.partial(finish_kernel, blocks=blocks_n, shared=(False, False, False, True)),
        tuple(like((width, s.cols), F32) for s in sums)
        + (like((width, (1 + QUANT) * HEAD_PAD), F32), like((count, 128), F32)),
        loss_row,
        *(v for s in sums for v in (s.parts if s.parts[1].size else [s.parts[0], s.parts[0]] + s.parts[2:])),
        pos=pos,
    )
    g_ffn1, g_att1, g_ffn0, g_att0 = grads
    scalars = lax.all_to_all(
        scalars.reshape(count, 1, 128), ("hi", "core", "mp"), 0, 0, tiled=True
    ).reshape(count, 128)
    g_qkv = jnp.stack([g[:, : 3 * part].reshape(qkv_w.shape[1:]) for g in (g_att0, g_att1)])
    g_out = jnp.stack([g[:, 3 * part :] for g in (g_att0, g_att1)])
    g_up = jnp.stack([g[:, :wide] for g in (g_ffn0, g_ffn1)])
    g_down = jnp.stack([g[:, wide:] for g in (g_ffn0, g_ffn1)])
    g_embed = g_rest[:, :LOOK].T
    g_norm = g_rest[:, LOOK : LOOK + 2 * NORMS].T.reshape(norm_params.shape)
    g_head = g_rest[:, HEAD_PAD:].reshape(width, QUANT, HEAD_PAD)[:, :, :HOR].reshape(width, -1)
    loss_sum, valid_count, squares = jnp.sum(scalars, axis=0)[:3]
    grad_norm = jnp.sqrt(squares) / valid_count
    factor = jnp.minimum(1.0, CLIP_NORM / grad_norm) / valid_count
    news = []
    for w, first, second, g in (
        (embed_w, embed_first, embed_second, g_embed),
        (qkv_w, qkv_first, qkv_second, g_qkv),
        (out_w, out_first, out_second, g_out),
        (up_w, up_first, up_second, g_up),
        (down_w, down_first, down_second, g_down),
        (head_w, head_first, head_second, g_head),
    ):
        news += adam_update(w, g * factor, first, second, LEARN_RATE, WEIGHT_DECAY)
    news += adam_update(norm_params, g_norm * factor, norm_first, norm_second, NORM_RATE, 0.0)
    return (loss_sum, valid_count, grad_norm, *news)


def solution(mesh):
    dp, mp = mesh.devices.shape
    split = Mesh(mesh.devices.reshape(dp // CORES, CORES, mp), ("hi", "core", "mp"))
    wide = ("hi", "core")
    tokens = ("hi", "core", "mp")
    embed = P(None, wide)
    qkv = P(None, wide, None, "mp")
    mat = P(None, wide, "mp")
    head = P(wide, None)
    norm = P(None, None, wide)
    weights = (embed, qkv, mat, mat, mat, head, norm)
    return jax.shard_map(
        body,
        mesh=split,
        in_specs=(P(None, tokens, None),) * 3
        + (P(None, tokens),)
        + weights
        + tuple(spec for spec in weights for _ in range(2)),
        out_specs=(P(),) * 3 + tuple(spec for spec in weights for _ in range(3)),
        check_vma=False,
    )
```

```python
import functools

import jax
import jax.numpy as jnp
from jax import lax
from jax.experimental import pallas as pl
from jax.experimental.pallas import tpu as pltpu
from jax.sharding import Mesh
from jax.sharding import PartitionSpec as P

HEAD_DIM = 64
LAYERS = 2
HOR = 96
LOOK = 96
QUANT = 3
MICRO = 2
STEP = 10
NORMS = 5
CORES = 2
HEAD_PAD = 128
SETS = 16
FAR = -1e30

SMOOTHING = 0.1
LEVELS = (0.1, 0.5, 0.9)
CLIP_NORM = 0.0001
LEARN_RATE = 0.05
NORM_RATE = 0.5
BETA_ONE = 0.9
BETA_TWO = 0.999
EPSILON = 1e-12
WEIGHT_DECAY = 0.1

BF = jnp.bfloat16
F32 = jnp.float32


def swap_core(v):
    return lax.ppermute(v, "core", [(0, 1), (1, 0)])


def swap_hi(v, bit):
    size = lax.axis_size("hi")
    return lax.ppermute(v, "hi", [(i, i ^ (1 << bit)) for i in range(size)])


def swap_mp(v, by):
    size = lax.axis_size("mp")
    return lax.ppermute(v, "mp", [(i, i ^ by) for i in range(size)])


def hi_bits():
    return (lax.axis_size("hi") - 1).bit_length()


def bit_order(flip):
    bits = list(range(hi_bits()))
    return bits[::-1] if flip else bits


def after(v, *deps):
    return lax.optimization_barrier((v, *deps))[0] if deps else v


def together(vs, *deps):
    return list(lax.optimization_barrier((*vs, *deps)))[: len(vs)]


def total_of(terms):
    total = terms[0].astype(F32)
    for term in terms[1:]:
        total = total + term.astype(F32)
    return total


class Gather:
    def __init__(self, v, flip):
        self.v = v
        self.order = bit_order(flip)
        self.done = []

    def hop(self, before=(), beside=()):
        bit = self.order[len(self.done)]
        axis = sum(1 for other in self.done if other > bit)
        got = swap_hi(after(self.v, *before), bit)
        self.v = jnp.stack([self.v, after(got, *beside)], axis=axis)
        self.done.append(bit)
        return got

    def halves(self):
        v = self.v.reshape((-1, self.v.shape[-1]))
        return v, swap_core(v)


class Scatter:
    def __init__(self, own, other, cols):
        self.own, self.cols = own, cols
        self.got = swap_core(other)
        self.stages = [self.spread, self.turn]

    def step(self, *deps):
        return self.stages.pop(0)(*deps) if self.stages else []

    def spread(self, *deps):
        size = lax.axis_size("hi")
        rows = self.own.shape[0] // size
        got = after(self.got, *deps)
        parts = [[v[r * rows : (r + 1) * rows] for v in (self.own, got)] for r in range(size)]
        sent = [total_of(part).astype(BF) for part in parts[1:]]
        self.terms = parts[0]
        self.got = [
            lax.ppermute(v, "hi", [(i, i ^ r) for i in range(size)]) for r, v in zip(range(1, size), sent)
        ]
        return sent

    def turn(self, *deps):
        self.terms = self.terms + [after(v, *deps) for v in self.got]
        return self.send()

    def landed(self):
        return [] if self.stages else self.parts[2:]

    def send(self):
        size = lax.axis_size("mp")
        cols = self.cols

        def block(j):
            return total_of([v[:, j * cols : (j + 1) * cols] for v in self.terms])

        shared = total_of([v[:, size * cols :] for v in self.terms]).astype(BF)
        sent = [jnp.concatenate([block(j).astype(BF), shared], axis=1) for j in range(1, size)]
        self.parts = [block(0), shared] + [swap_mp(v, j) for j, v in zip(range(1, size), sent)]
        return sent


class Halving:
    def __init__(self, halves, cols):
        self.cols = cols
        self.got = [swap_core(halves[1]), swap_core(halves[3])]
        self.stages = [self.halve] * hi_bits() + [self.turn]
        self.shape = (2,) * hi_bits() + (halves[0].shape[0] >> hi_bits(), halves[0].shape[1])
        self.pairs = [[halves[0].reshape(self.shape)], [halves[2].reshape(self.shape)]]
        self.orders = [bit_order(flip)[::-1] for flip in (False, True)]
        self.left = [list(range(hi_bits())) for _ in range(2)]

    def step(self, *deps):
        return self.stages.pop(0)(*deps) if self.stages else []

    def land(self, *deps):
        for p in range(2):
            self.pairs[p].append(after(self.got[p], *deps).reshape(self.pairs[p][0].shape))

    def halve(self, *deps):
        self.land(*deps)
        sent = []
        for p in range(2):
            bit = self.orders[p].pop(0)
            axis = sum(1 for other in self.left[p] if other > bit)
            send = total_of([lax.index_in_dim(t, 1, axis, keepdims=False) for t in self.pairs[p]]).astype(BF)
            self.pairs[p] = [lax.index_in_dim(t, 0, axis, keepdims=False) for t in self.pairs[p]]
            self.left[p].remove(bit)
            self.got[p] = swap_hi(send, bit)
            sent.append(send)
        return sent

    def turn(self, *deps):
        self.land(*deps)
        size = lax.axis_size("mp") // 2
        cols = self.cols

        def block(j):
            p, at = j // size, j % size * cols
            return total_of([v[:, at : at + cols] for v in self.pairs[p]])

        sent = [block(j).astype(BF) for j in range(1, 2 * size)]
        self.parts = [block(0), sent[0][:0]] + [swap_mp(v, j) for j, v in enumerate(sent, 1)]
        return sent

    def landed(self):
        return [] if self.stages else self.parts[2:]


def turns(v):
    return tuple(swap_mp(v, by) for by in range(1, lax.axis_size("mp")))


def pairs_of(v, turned):
    half = lax.axis_size("mp") // 2
    blocks = (v,) + turned
    return [
        Gather(jnp.concatenate(blocks[flip * half : (flip + 1) * half], axis=1), flip)
        for flip in (False, True)
    ]


def halves_of(pairs):
    return tuple(h for pair in pairs for h in pair.halves())


class Halves:
    def __init__(self, arrays):
        self.arrays = arrays
        self.blocks = lax.axis_size("mp")

    def specs(self):
        return [pl.BlockSpec(memory_space=pltpu.VMEM)] * len(self.arrays)

    def reader(self, refs):
        half = self.blocks // 2

        def read(j, lo, hi):
            own, other = refs[2 * (j // half)], refs[2 * (j // half) + 1]
            at = j % half * (own.shape[1] // half)
            return cut((own, other), at + lo, at + hi)

        return read


class Shards:
    def __init__(self, own, other, at, size):
        self.own, self.at, self.size = own, at, size
        self.blocks = lax.axis_size("mp")
        self.hi = lax.axis_size("hi")
        self.arrays = ((own,) * self.hi + (other,) * self.hi) * self.blocks

    def specs(self):
        width, blocks, at, size = self.own.shape[1], self.blocks, self.at, self.size
        return [
            pl.BlockSpec(
                (1, width, size),
                lambda i, pos, r=r, j=j: (
                    (pos[2] ^ r) * blocks + (pos[1] ^ j), 0, at,
                ),
            )
            for j in range(blocks)
            for _ in range(CORES)
            for r in range(self.hi)
        ]

    def reader(self, refs):
        def read(j, lo, hi):
            count = CORES * self.hi
            return jnp.concatenate([ref[0, :, lo:hi] for ref in refs[j * count : (j + 1) * count]], axis=0)

        return read


class GradOut:
    def __init__(self, width, cols, more=0, pairs=True):
        self.cols = cols
        self.count = lax.axis_size("mp") // 2 if pairs else lax.axis_size("mp") + 1
        size = self.count * cols if pairs else (self.count - 1) * cols + more
        self.shapes = (like((width // CORES, size), BF),) * (4 if pairs else 2)

    def writer(self, refs, pos):
        def write(j, lo, v):
            p = j // self.count
            put(refs[2 * p : 2 * p + 2], j % self.count * self.cols + lo, v)

        return write


def mm(a, b):
    return lax.dot_general(a, b, (((1,), (0,)), ((), ())), preferred_element_type=F32)


def mm_nt(a, b):
    return lax.dot_general(a, b, (((1,), (1,)), ((), ())), preferred_element_type=F32)


def mm_tn(a, b):
    return lax.dot_general(a, b, (((0,), (0,)), ((), ())), preferred_element_type=F32)


def unit_of(values):
    mean = jnp.mean(values, axis=-1, keepdims=True)
    centered = values - mean
    scaled = lax.rsqrt(jnp.mean(centered * centered, axis=-1, keepdims=True) + 1e-05)
    return centered * scaled, scaled


def norm_back(gradient, gain, unit, scaled):
    d_gain = jnp.sum(gradient * unit, axis=0, keepdims=True)
    d_shift = jnp.sum(gradient, axis=0, keepdims=True)
    d_unit = gradient * gain
    d_values = scaled * (
        d_unit
        - jnp.mean(d_unit, axis=-1, keepdims=True)
        - unit * jnp.mean(d_unit * unit, axis=-1, keepdims=True)
    )
    return d_values, d_gain, d_shift


def cut(pair, lo, hi):
    return jnp.concatenate([pair[0][:, lo:hi], pair[1][:, lo:hi]], axis=0)


def put(pair, lo, v):
    rows = pair[0].shape[0]
    pair[0][:, lo : lo + v.shape[1]] = v[:rows]
    pair[1][:, lo : lo + v.shape[1]] = v[rows:]


def affine(base, gs, row):
    return base[...] * gs[row : row + 1, :] + gs[row + 1 : row + 2, :]


def pack_kernel(qkv, out, up, down, *outs):
    part, wide = out.shape[2], up.shape[2]
    outs = list(outs)
    places = [(0, outs[0], 0), (1, outs[-1], outs[-1].shape[1] - 4 * part)]
    for l, ref, at in places:
        for c in range(3):
            ref[:, at + c * part : at + (c + 1) * part] = qkv[l, :, c, :].astype(BF)
        ref[:, at + 3 * part : at + 4 * part] = out[l].astype(BF)
    for l in range(LAYERS):
        outs[1 + l][:, :wide] = up[l].astype(BF)
        outs[1 + l][:, wide : 2 * wide] = down[l].astype(BF)


def qkv_kernel(ins, w, outs, *, row, part):
    if len(ins) == 2:
        h = affine(*ins, row).astype(BF)
    else:
        x_in, *rest = ins
        base, gs, head = outs[2:]
        embed = cut(rest, 0, HEAD_PAD)
        base[...] = mm_nt(x_in[...], embed)
        h = base[...].astype(BF)
        gs[...] = jnp.zeros_like(gs)
        gs[: 2 * NORMS, :] = embed.astype(F32).T[LOOK : LOOK + 2 * NORMS]
        gs[row : row + 1, :] = jnp.ones((1, gs.shape[1]), F32)
        head[...] = cut(rest, HEAD_PAD, rest[0].shape[1])
    q, kv = outs[:2]
    full = q.shape[1]
    for j in range(full // part):
        got = mm(h, w(j, 0, 3 * part)).astype(BF)
        q[:, j * part : (j + 1) * part] = got[:, :part]
        kv[:, j * part : (j + 1) * part] = got[:, part : 2 * part]
        kv[:, full + j * part : full + (j + 1) * part] = got[:, 2 * part :]


def lane_of(v):
    return lax.broadcasted_iota(jnp.int32, v.shape, 1)


def head_with(v, h, more):
    return jnp.where(lane_of(v) // HEAD_DIM == h, v, more)


def set_tags(id_row, width):
    id_col = jnp.broadcast_to(id_row[...], (8, id_row.shape[1])).T[:, :1]
    rows = id_col.shape[0]
    lane = (lax.broadcasted_iota(jnp.int32, (rows, width), 1) % HEAD_DIM).astype(F32)
    same = lane == id_col
    keys = jnp.where(same, 1.0, 0.0)
    queries = jnp.where(same[: rows // CORES], 0.0, FAR)
    return keys, queries


def three_parts(v):
    first = v.astype(BF).astype(F32)
    second = (v - first).astype(BF).astype(F32)
    return first, second, v - first - second


def with_lanes(tags, first, values):
    lane = lane_of(tags) % HEAD_DIM
    for k, value in enumerate(values):
        tags = jnp.where(lane == first + k, value, tags)
    return tags


def both_rows(own, other, at, part):
    return jnp.concatenate([own[:, at : at + part], other[:, at : at + part]], axis=0)


def attend_kernel(ins, w, outs, *, row, part):
    q, kv, kv_other, id_col, base, gs = ins
    mixed, lse, unit, scaled = outs
    key_tags, query_tags = (t.astype(BF) for t in set_tags(id_col, part))
    full = q.shape[1]
    total = affine(base, gs, row)
    for j in range(full // part):
        at = j * part
        q_part = q[:, at : at + part] * 0.125
        k_part = both_rows(kv, kv_other, at, part)
        v_flip = both_rows(kv, kv_other, full + at, part).T
        flat = []
        for h in range(part // HEAD_DIM):
            s = mm_nt(head_with(k_part, h, key_tags), head_with(q_part, h, query_tags))
            top = jnp.max(s, axis=0, keepdims=True)
            e = jnp.exp(s - top)
            sums = jnp.sum(e, axis=0, keepdims=True)
            o = mm(v_flip[h * HEAD_DIM : (h + 1) * HEAD_DIM], e.astype(BF))
            flat.append(o * (1.0 / sums))
            head = at // HEAD_DIM + h
            lse[head : head + 1, :] = top + jnp.log(sums)
        mixed_part = jnp.concatenate(flat, axis=0).T.astype(BF)
        mixed[:, at : at + part] = mixed_part
        total = total + mm_nt(mixed_part, w(j, 3 * part, 4 * part))
    unit[...], scaled[...] = unit_of(total)


def normal_cdf(x):
    bell = jnp.exp(-0.5 * x * x)
    t = 1.0 / (1.0 + 0.2316418876 * jnp.abs(x))
    tail = 0.5307027145
    for c in (-0.7265760135, 0.7107068705, -0.142248368, 0.127414796):
        tail = tail * t + c
    tail = tail * t * bell
    return jnp.where(x < 0, tail, 1.0 - tail), bell


def feed_kernel(ins, w, outs, *, row, wide):
    unit_in, gs = ins
    act, slope, unit, scaled = outs
    first = affine(unit_in, gs, row)
    y = first.astype(BF)
    total = first
    for j in range(act.shape[1] // wide):
        at = j * wide
        inner = mm(y, w(j, 0, wide))
        cdf, bell = normal_cdf(inner)
        act_part = (inner * cdf).astype(BF)
        act[:, at : at + wide] = act_part
        slope[:, at : at + wide] = (cdf + inner * bell * 0.3989422804014327).astype(BF)
        total = total + mm_nt(act_part, w(j, wide, 2 * wide))
    unit[...], scaled[...] = unit_of(total)


def head_kernel(ins, w, outs, *, row, last):
    unit_in, gs, head_w, counted, *targets = ins
    target = jnp.concatenate([t[...] for t in targets], axis=0)
    counted = counted[...].astype(F32)
    counted = jnp.where(lane_of(counted) < HOR, counted, 0.0)
    loss, g_head0, g_head1, d_hidden, d_norm = outs
    unit, scaled = unit_of(affine(unit_in, gs, row))
    gain = gs[last : last + 1, :]
    final = (unit * gain + gs[last + 1 : last + 2, :]).astype(BF)
    size = head_w.shape[1] // QUANT
    head = head_w[...]
    pred = mm(final, head)
    total = jnp.zeros((1, size), F32)
    grads = []
    for t, level in enumerate(LEVELS):
        gap = target - pred[:, t * size : (t + 1) * size]
        x = gap * (-1.0 / SMOOTHING)
        e = jnp.exp(-jnp.abs(x))
        soft = jnp.maximum(x, 0.0) + jnp.log(1.0 + e)
        sig = jnp.where(x >= 0, 1.0, e) / (1.0 + e)
        total = total + jnp.sum((level * gap + SMOOTHING * soft) * counted, axis=0, keepdims=True)
        grads.append(((sig - level) * counted).astype(BF))
    loss[...] = jnp.concatenate([total, jnp.sum(counted, axis=0, keepdims=True)], axis=0)
    d_pred = jnp.concatenate(grads, axis=1)
    put((g_head0, g_head1), 0, mm(final.T, d_pred).astype(BF))
    d_hidden[...], d_gain, d_shift = norm_back(mm_nt(d_pred, head), gain, unit, scaled)
    d_norm[...] = jnp.concatenate([d_gain, d_shift], axis=0)


def feed_back_kernel(ins, w, outs, g, *, row, wide):
    grad, unit_two, scaled_two, unit_one, scaled_one, gs, act, slope = ins
    d_one, d_norm = outs
    d_two, gain_two, shift_two = norm_back(
        grad[...], gs[row + 2 : row + 3, :], unit_two[...], scaled_two[...]
    )
    d_ffn = d_two.astype(BF)
    d_flip = d_ffn.T
    y_flip = affine(unit_one, gs, row).astype(BF).T
    total = d_two
    for j in range(act.shape[1] // wide):
        at = j * wide
        g(j, wide, mm(d_flip, act[:, at : at + wide]).astype(BF))
        d_act = mm(d_ffn, w(j, wide, 2 * wide))
        d_inner = (d_act * slope[:, at : at + wide].astype(F32)).astype(BF)
        g(j, 0, mm(y_flip, d_inner).astype(BF))
        total = total + mm_nt(d_inner, w(j, 0, wide))
    d_one[...], gain_one, shift_one = norm_back(
        total, gs[row : row + 1, :], unit_one[...], scaled_one[...]
    )
    d_norm[...] = jnp.concatenate([gain_one, shift_one, gain_two, shift_two], axis=0)


def attend_back_kernel(ins, w, outs, *, part, first):
    d_one, q, kv, kv_other, id_col, lse, mixed = ins
    g_out, d_q, d_kv, d_kv_other = outs
    key_tags, query_tags = set_tags(id_col, part)
    key_tags = with_lanes(key_tags, SETS, (1.0, 1.0, 1.0)).astype(BF)
    value_tags = with_lanes(jnp.zeros(key_tags.shape, F32), 0, (1.0, 1.0, 1.0)).astype(BF)
    log_sums = lse[...].T
    full = q.shape[1]
    rows, here = d_q.shape
    d_branch = d_one[...].astype(BF)
    g_out[...] = mm(d_branch.T, mixed[:, first * part : first * part + here]).astype(BF)
    for j in range(first, first + here // part):
        at, to = j * part, (j - first) * part
        d_mixed_wide = mm(d_branch, w(j, 3 * part, 4 * part))
        d_mixed = d_mixed_wide.astype(BF)
        q_part = q[:, at : at + part] * 0.125
        k_part = both_rows(kv, kv_other, at, part)
        v_part = both_rows(kv, kv_other, full + at, part)
        k_flip = k_part.T
        product = d_mixed.astype(F32) * mixed[:, at : at + part].astype(F32)
        d_k = d_v = None
        d_q_flip = []
        for h in range(part // HEAD_DIM):
            head = at // HEAD_DIM + h
            log_sum = log_sums[:, head : head + 1]
            dots = jnp.sum(head_with(product, h, 0.0), axis=1, keepdims=True)
            q_tags = with_lanes(query_tags, SETS, three_parts(-log_sum)).astype(BF)
            d_tags = with_lanes(jnp.zeros_like(product), 0, three_parts(-dots)).astype(BF)
            probs = jnp.exp(mm_nt(head_with(k_part, h, key_tags), head_with(q_part, h, q_tags)))
            shifted = mm_nt(head_with(v_part, h, value_tags), head_with(d_mixed, h, d_tags))
            d_s = (probs * shifted).astype(BF)
            more_v = mm(probs.astype(BF), d_mixed)
            more_k = mm(d_s, q_part)
            d_v = more_v if d_v is None else head_with(more_v, h, d_v)
            d_k = more_k if d_k is None else head_with(more_k, h, d_k)
            d_q_flip.append(mm(k_flip[h * HEAD_DIM : (h + 1) * HEAD_DIM], d_s))
        d_q[:, to : to + part] = (jnp.concatenate(d_q_flip, axis=0) * 0.125).T.astype(BF)
        d_kv[:, to : to + part] = d_k[:rows]
        d_kv_other[:, to : to + part] = d_k[rows:].astype(BF)
        d_kv[:, here + to : here + to + part] = d_v[:rows]
        d_kv_other[:, here + to : here + to + part] = d_v[rows:].astype(BF)


def qkv_back_kernel(ins, w, outs, g, *, row, part):
    d_one, base, gs, *rest = ins
    halves, rest = (rest[:4], rest[4:8]), rest[8:]
    (d_hidden,) = outs
    full = d_one.shape[1]
    h_flip = affine(base, gs, row).astype(BF).T
    total = d_one[...]
    for j in range(full // part):
        here = halves[0][0].shape[1]
        d_q, d_kv, got, g_out = halves[j * part // here]
        at = j * part % here
        d_all = [d_q[:, at : at + part]]
        for base_at in (at, here + at):
            d_all.append(
                (
                    d_kv[:, base_at : base_at + part] + got[:, base_at : base_at + part].astype(F32)
                ).astype(BF)
            )
        d_all = jnp.concatenate(d_all, axis=1)
        g(j, 0, mm(h_flip, d_all).astype(BF))
        g(j, 3 * part, g_out[:, at : at + part])
        total = total + mm_nt(d_all, w(j, 0, 3 * part))
    d_hidden[...] = total
    if len(rest) == CORES:
        g(full // part, 0, jnp.concatenate([r[...] for r in rest], axis=0))
    else:
        x_in, *norms = rest
        rows = [jnp.zeros((LOOK, total.shape[1]), F32)] + [n[...] for n in norms]
        rows.append(jnp.zeros((HEAD_PAD - LOOK - 2 * NORMS, total.shape[1]), F32))
        g(full // part, 0, (mm(total.astype(BF).T, x_in[...]) + jnp.concatenate(rows, axis=0).T).astype(BF))


def finish_kernel(at, *refs, blocks, shared):
    count = len(shared)
    ins, outs = refs[: 1 + count * (blocks + 1)], refs[1 + count * (blocks + 1) :]
    z = at[1]
    squares = jnp.zeros((), F32)
    for c in range(count):
        own, common, *turned = ins[1 + c * (blocks + 1) : 1 + (c + 1) * (blocks + 1)]
        cols = own.shape[1]
        total = own[...]
        for t in turned:
            total = total + t[:, :cols].astype(F32)
        outs[c][...] = total
        squares = squares + jnp.sum(total * total)
        if shared[c]:
            held = [common[...].astype(F32)] + [t[:, cols:].astype(F32) for t in turned]
            total = jnp.zeros_like(held[0])
            for owner in range(blocks):
                by = z ^ owner
                term = held[0]
                for j in range(1, blocks):
                    term = jnp.where(by == j, held[j], term)
                total = total + term
            outs[count + sum(shared[:c])][...] = total
            squares = squares + jnp.where(z == 0, jnp.sum(total * total), 0.0)
    loss = ins[0]
    place = lax.broadcasted_iota(jnp.int32, outs[-1].shape, 1)
    outs[-1][...] = jnp.where(
        place == 0,
        jnp.sum(loss[0:1, :]),
        jnp.where(place == 1, jnp.sum(loss[1:2, :]), jnp.where(place == 2, squares, 0.0)),
    )


def kernel_call(kernel, pos, ins, weights, outs, grads=None, scratch=(), us=1.0, **static):
    whole = pl.BlockSpec(memory_space=pltpu.VMEM)
    w_arrays = weights.arrays if weights else ()
    g_shapes = grads.shapes if grads else ()

    def run(at, *refs):
        refs = list(refs)

        def take(count):
            got = refs[:count]
            del refs[:count]
            return got

        in_refs = take(len(ins))
        w_refs = take(len(w_arrays))
        out_refs = take(len(outs))
        g_refs = take(len(g_shapes))
        more = [grads.writer(g_refs, at)] if grads else []
        kernel(in_refs, weights.reader(w_refs) if weights else None, out_refs, *more, *refs, **static)

    return pl.pallas_call(
        run,
        out_shape=tuple(outs) + tuple(g_shapes),
        grid_spec=pltpu.PrefetchScalarGridSpec(
            num_scalar_prefetch=1,
            grid=(1,),
            in_specs=[whole] * len(ins) + (weights.specs() if weights else []),
            out_specs=tuple(whole for _ in range(len(outs) + len(g_shapes))),
            scratch_shapes=scratch,
        ),
        compiler_params=pltpu.CompilerParams(vmem_limit_bytes=20 * 1024 * 1024),
        cost_estimate=pl.CostEstimate(flops=int(us * 1.15e9), bytes_accessed=0, transcendentals=0),
    )(pos, *ins, *w_arrays)


def kernel_call_plain(kernel, outs, *args, pos=None, limit=20):
    whole = pl.BlockSpec(memory_space=pltpu.VMEM)
    first = [] if pos is None else [pl.BlockSpec(memory_space=pltpu.SMEM)]
    return pl.pallas_call(
        kernel,
        out_shape=outs,
        in_specs=first + [whole] * len(args),
        out_specs=tuple(whole for _ in outs),
        compiler_params=pltpu.CompilerParams(vmem_limit_bytes=limit * 1024 * 1024),
    )(*(() if pos is None else (pos,)), *args)


def like(shape, dtype):
    return jax.ShapeDtypeStruct(shape, dtype)


def adam_update(weight, gradient, first_moment, second_moment, rate, decay):
    first_moment = BETA_ONE * first_moment + (1 - BETA_ONE) * gradient
    second_moment = BETA_TWO * second_moment + (1 - BETA_TWO) * gradient * gradient
    update = (
        first_moment
        / (1 - BETA_ONE**STEP)
        / (jnp.sqrt(second_moment / (1 - BETA_TWO**STEP)) + EPSILON)
    )
    return (weight - rate * (update + decay * weight), first_moment, second_moment)


def deal_swap(v):
    rows = v.shape[1] // CORES
    core = lax.axis_index("core")
    v = v.reshape(MICRO, CORES, rows, v.shape[-1])
    keep = lax.dynamic_index_in_dim(v, core, 1, keepdims=False)
    send = lax.dynamic_index_in_dim(v, 1 - core, 1, keepdims=False)
    got = swap_core(send)
    return jnp.where(core == 0, jnp.concatenate([keep, got]), jnp.concatenate([got, keep]))


def deal_halves_kernel(at, whole, keep, send):
    rows = keep.shape[1]
    for m in range(MICRO):
        keep[m] = whole[m, pl.ds(pl.multiple_of(at[3] * rows, rows), rows), :]
        send[m] = whole[m, pl.ds(pl.multiple_of((1 - at[3]) * rows, rows), rows), :]


def deal_parts_kernel(at, keep, got, *parts):
    for by, part in enumerate(parts):
        owner = at[1] ^ by
        part[...] = jnp.zeros_like(part)
        part[:, : keep.shape[2]] = jnp.where(
            owner // MICRO == at[3], keep[owner % MICRO], got[owner % MICRO]
        )


def deal_rows(v):
    size = lax.axis_size("mp")
    z = lax.axis_index("mp")
    parts = [lax.dynamic_index_in_dim(v, z ^ by, 0, keepdims=False) for by in range(size)]
    return jnp.concatenate(parts[:1] + [swap_mp(parts[by], by) for by in range(1, size)])


def body(
    series,
    targets,
    valid,
    dataset_ids,
    embed_w,
    qkv_w,
    out_w,
    up_w,
    down_w,
    head_w,
    norm_params,
    *moments,
):
    (
        embed_first,
        embed_second,
        qkv_first,
        qkv_second,
        out_first,
        out_second,
        up_first,
        up_second,
        down_first,
        down_second,
        head_first,
        head_second,
        norm_first,
        norm_second,
    ) = moments
    width = embed_w.shape[1]
    part = qkv_w.shape[3]
    wide = up_w.shape[2]
    blocks_n = lax.axis_size("mp")

    bits = hi_bits()
    hi_at, core_at, z_at = lax.axis_index("hi"), lax.axis_index("core"), lax.axis_index("mp")
    pos = jnp.stack([hi_at * CORES + core_at, z_at, hi_at, core_at]).astype(jnp.int32)
    att_w, ffn_w, late = {}, {}, None
    placed = width % 16 == 0
    packed = kernel_call_plain(
        pack_kernel,
        tuple(like((width, cols), BF) for cols in (4 * part, 2 * wide, 2 * wide, 4 * part))
        if not placed
        else (like((width, 4 * part), BF), like((width, 2 * wide), BF), like((width, 2 * wide + 4 * part), BF)),
        qkv_w, out_w, up_w, down_w,
        limit=56,
    )
    att_w[0], ffn_w[0], ffn_w[1], att_w[1] = (*packed, None) if placed else packed
    if placed:
        late = lax.all_gather(ffn_w[1], ("hi", "mp"), axis=0, tiled=False)
        late = late.reshape((-1,) + late.shape[-2:])

    low_pad = HEAD_PAD - LOOK - 2 * NORMS
    embed_cols = jnp.concatenate([embed_w.T, norm_params.reshape(-1, width).T], axis=1)
    head_cols = jnp.pad(head_w.reshape(width, QUANT, HOR), ((0, 0), (0, 0), (0, HEAD_PAD - HOR)))
    rest = Gather(
        jnp.concatenate(
            [jnp.pad(embed_cols, ((0, 0), (0, low_pad))), head_cols.reshape(width, -1)], axis=1
        ).astype(BF),
        False,
    )
    low = deal_swap(
        jnp.pad(
            jnp.concatenate(
                [
                    jnp.pad(series, ((0, 0), (0, 0), (0, HEAD_PAD - LOOK))),
                    valid.astype(BF),
                    dataset_ids[..., None].astype(BF),
                ],
                axis=-1,
            ),
            ((0, 0), (0, 0), (0, HEAD_PAD - HOR - 1)),
        )
    )
    z_att = turns(att_w[0])
    rest.hop()
    att_pairs = pairs_of(att_w[0], z_att)
    hop_att = [pair.hop() for pair in att_pairs]
    low = deal_rows(after(low, *z_att))
    for _ in range(1, bits):
        rest.hop(before=hop_att)
    rest = rest.halves()
    ffn_first = after(ffn_w[0], *hop_att)
    z_ffn = turns(ffn_first)
    for _ in range(1, bits):
        hop_att = [pair.hop() for pair in att_pairs]
    att = [Halves(halves_of(att_pairs))]
    ffn_pairs = pairs_of(ffn_first, z_ffn)
    for _ in range(bits - 1):
        for pair in ffn_pairs:
            pair.hop()

    model = CORES * rest[0].shape[0]
    ident = 2 * NORMS
    x_in = low[:, :HEAD_PAD]
    counted = low[:, HEAD_PAD : 2 * HEAD_PAD]
    ids_here = low[:, HEAD_PAD + HOR].reshape(1, -1)
    ids = jnp.concatenate([ids_here, swap_core(ids_here)], axis=1).astype(F32)
    rows = x_in.shape[0]
    heads = model // HEAD_DIM
    hidden_n = wide * blocks_n

    base, row = None, ident
    stored = []
    ffn = []
    for l in range(LAYERS):
        q, kv, *more = kernel_call(
            qkv_kernel, pos, (base, gs) if l else (x_in, *rest), att[l],
            (like((rows, model), BF), like((rows, 2 * model), BF))
            + (() if l else (like((rows, model), F32), like((16, model), F32), like((model, QUANT * HEAD_PAD), BF))),
            us=1.3, row=row, part=part,
        )
        if l == 0:
            base, gs, head_w_all = more
        kv_other = swap_core(kv)
        if l == 0:
            q = after(q, *(pair.v for pair in ffn_pairs))
        mixed, lse, unit_one, scaled_one = kernel_call(
            attend_kernel, pos, (q, kv, kv_other, ids, base, gs), att[l],
            (like((rows, model), BF), like((heads, rows), F32), like((rows, model), F32), like((rows, 1), F32)),
            us=11, row=row, part=part,
        )
        if l == 1:
            target = [parts[0]] + [swap_mp(parts[by], by) for by in range(1, blocks_n)]
            unit_one = after(unit_one, *together(target, mixed))
        if l == 0:
            for pair in ffn_pairs:
                pair.hop(before=(kv,), beside=(mixed,))
            ffn.append(Halves(halves_of(ffn_pairs)))
            if not placed:
                for kept, v in ((att, att_w[1]), (ffn, ffn_w[1])):
                    pairs = pairs_of(v, turns(v))
                    for _ in range(bits):
                        for pair in pairs:
                            pair.hop()
                    kept.append(Halves(halves_of(pairs)))
        act, slope, unit_two, scaled_two = kernel_call(
            feed_kernel, pos, (unit_one, gs), ffn[l],
            (like((rows, hidden_n), BF), like((rows, hidden_n), BF), like((rows, model), F32), like((rows, 1), F32)),
            us=10, row=4 * l, wide=wide,
        )
        stored.append((base, row, q, kv, kv_other, mixed, lse, unit_one, scaled_one, act, slope, unit_two, scaled_two))
        base, row = unit_two, 4 * l + 2
        if l == 0:
            half = (MICRO, targets.shape[1] // CORES, HOR)
            keep, send = kernel_call_plain(
                deal_halves_kernel, (like(half, F32), like(half, F32)), after(targets, unit_two), pos=pos
            )
            parts = kernel_call_plain(
                deal_parts_kernel,
                (like((half[1], HEAD_PAD), F32),) * blocks_n,
                keep, swap_core(send),
                pos=pos,
            )
            base = after(base, *parts)
        if l == 0 and placed:
            late = after(late, unit_two)
            other = swap_core(late)
            att.append(Shards(late, other, 2 * wide // (4 * part), 4 * part))
            ffn.append(Shards(late, other, 0, 2 * wide))
    loss_row, *g_head, grad, d_norm_last = kernel_call(
        head_kernel, pos, (base, gs, head_w_all, counted, *target), None,
        (like((2, HEAD_PAD), F32),)
        + (like((model // CORES, QUANT * HEAD_PAD), BF),) * CORES
        + (like((rows, model), F32), like((2, model), F32)),
        us=2, row=row, last=2 * NORMS - 2,
    )
    norm_grads = [None] * LAYERS
    sums = []

    def feed_back(l, grad):
        unit_one, scaled_one, act, slope, unit_two, scaled_two = stored[l][7:]
        return kernel_call(
            feed_back_kernel, pos,
            (grad, unit_two, scaled_two, unit_one, scaled_one, gs, act, slope), ffn[l],
            (like((rows, model), F32), like((4, model), F32)),
            grads=GradOut(model, 2 * wide),
            us=10.5, row=4 * l, wide=wide,
        )

    def attend_back(l, d_one, half):
        q, kv, kv_other, mixed, lse = stored[l][2:7]
        here = model // 2
        g_out, d_q, d_kv, d_kv_other = kernel_call(
            attend_back_kernel, pos,
            (d_one, q, kv, kv_other, ids, lse, mixed), att[l],
            (like((model, here), BF), like((rows, here), BF), like((rows, 2 * here), F32), like((rows, 2 * here), BF)),
            us=8, part=part, first=half * here // part,
        )
        return d_q, d_kv, swap_core(d_kv_other), g_out

    def qkv_back(l, d_one, *args):
        base, row = stored[l][:2]
        more = (x_in, *norm_grads, d_norm_last) if l == 0 else tuple(g_head)
        return kernel_call(
            qkv_back_kernel, pos, (d_one, base, gs, *args, *more), att[l],
            (like((rows, model), F32),),
            grads=GradOut(model, 4 * part, more=HEAD_PAD if l == 0 else QUANT * HEAD_PAD, pairs=False),
            us=5.5, row=row, part=part,
        )

    d_one, norm_grads[1], *halves = feed_back(1, grad)
    ffn_sum = Halving(halves, 2 * wide)
    first = attend_back(1, d_one, 0)
    sent = ffn_sum.step(first[0])
    second = attend_back(1, after(d_one, first[0], *sent), 1)
    sent = ffn_sum.step(second[0])
    grad, *halves = qkv_back(1, after(d_one, *sent), *first, *second)
    att_sum = Scatter(*halves, 4 * part)
    sent = ffn_sum.step(grad)

    d_one, norm_grads[0], *halves = feed_back(0, after(grad, *sent))
    ffn_low = Halving(halves, 2 * wide)
    sent = att_sum.step(d_one) + ffn_sum.step(d_one)
    d_one = after(d_one, *sent, *ffn_sum.landed())
    first = attend_back(0, d_one, 0)
    sent = ffn_low.step(first[0])
    second = attend_back(0, after(d_one, first[0], *sent), 1)
    sent = att_sum.step(second[0]) + ffn_low.step(second[0])
    _, own, other = qkv_back(0, after(d_one, *sent), *first, *second)
    att_low = Scatter(own, after(other, *att_sum.landed()), 4 * part)
    for chunk in (ffn_sum, att_sum, ffn_low):
        while chunk.stages:
            chunk.step(own)
    att_low.step()
    att_low.step(*ffn_low.landed())
    sums = [ffn_sum, att_sum, ffn_low, att_low]

    count = lax.axis_size("hi") * CORES * blocks_n
    *grads, g_head, g_low, scalars = kernel_call_plain(
        functools.partial(finish_kernel, blocks=blocks_n, shared=(False, True, False, True)),
        tuple(like((width, s.cols), F32) for s in sums)
        + (like((width, QUANT * HEAD_PAD), F32), like((width, HEAD_PAD), F32), like((count, 128), F32)),
        loss_row,
        *(v for s in sums for v in (s.parts if s.parts[1].size else [s.parts[0], s.parts[0]] + s.parts[2:])),
        pos=pos,
    )
    g_ffn1, g_att1, g_ffn0, g_att0 = grads
    scalars = lax.all_to_all(
        scalars.reshape(count, 1, 128), ("hi", "core", "mp"), 0, 0, tiled=True
    ).reshape(count, 128)
    g_qkv = jnp.stack([g[:, : 3 * part].reshape(qkv_w.shape[1:]) for g in (g_att0, g_att1)])
    g_out = jnp.stack([g[:, 3 * part :] for g in (g_att0, g_att1)])
    g_up = jnp.stack([g[:, :wide] for g in (g_ffn0, g_ffn1)])
    g_down = jnp.stack([g[:, wide:] for g in (g_ffn0, g_ffn1)])
    g_embed = g_low[:, :LOOK].T
    g_norm = g_low[:, LOOK : LOOK + 2 * NORMS].T.reshape(norm_params.shape)
    g_head = g_head.reshape(width, QUANT, HEAD_PAD)[:, :, :HOR].reshape(width, -1)
    loss_sum, valid_count, squares = jnp.sum(scalars, axis=0)[:3]
    grad_norm = jnp.sqrt(squares) / valid_count
    factor = jnp.minimum(1.0, CLIP_NORM / grad_norm) / valid_count
    news = []
    for w, first, second, g in (
        (embed_w, embed_first, embed_second, g_embed),
        (qkv_w, qkv_first, qkv_second, g_qkv),
        (out_w, out_first, out_second, g_out),
        (up_w, up_first, up_second, g_up),
        (down_w, down_first, down_second, g_down),
        (head_w, head_first, head_second, g_head),
    ):
        news += adam_update(w, g * factor, first, second, LEARN_RATE, WEIGHT_DECAY)
    news += adam_update(norm_params, g_norm * factor, norm_first, norm_second, NORM_RATE, 0.0)
    return (loss_sum, valid_count, grad_norm, *news)


def solution(mesh):
    dp, mp = mesh.devices.shape
    split = Mesh(mesh.devices.reshape(dp // CORES, CORES, mp), ("hi", "core", "mp"))
    wide = ("hi", "core")
    tokens = ("hi", "core", "mp")
    embed = P(None, wide)
    qkv = P(None, wide, None, "mp")
    mat = P(None, wide, "mp")
    head = P(wide, None)
    norm = P(None, None, wide)
    weights = (embed, qkv, mat, mat, mat, head, norm)
    return jax.shard_map(
        body,
        mesh=split,
        in_specs=(P(None, tokens, None),) * 3
        + (P(None, tokens),)
        + weights
        + tuple(spec for spec in weights for _ in range(2)),
        out_specs=(P(),) * 3 + tuple(spec for spec in weights for _ in range(3)),
        check_vma=False,
    )
```

```python
import functools

import jax
import jax.numpy as jnp
from jax import lax
from jax.experimental import pallas as pl
from jax.experimental.pallas import tpu as pltpu
from jax.sharding import Mesh
from jax.sharding import PartitionSpec as P

HEAD_DIM = 64
LAYERS = 2
HOR = 96
LOOK = 96
QUANT = 3
MICRO = 2
STEP = 10
NORMS = 5
CORES = 2
HEAD_PAD = 128
SETS = 16
FAR = -1e30

SMOOTHING = 0.1
LEVELS = (0.1, 0.5, 0.9)
CLIP_NORM = 0.0001
LEARN_RATE = 0.05
NORM_RATE = 0.5
BETA_ONE = 0.9
BETA_TWO = 0.999
EPSILON = 1e-12
WEIGHT_DECAY = 0.1

BF = jnp.bfloat16
F32 = jnp.float32


def swap_core(v):
    return lax.ppermute(v, "core", [(0, 1), (1, 0)])


def swap_hi(v, bit):
    size = lax.axis_size("hi")
    return lax.ppermute(v, "hi", [(i, i ^ (1 << bit)) for i in range(size)])


def swap_mp(v, by):
    size = lax.axis_size("mp")
    return lax.ppermute(v, "mp", [(i, i ^ by) for i in range(size)])


def hi_bits():
    return (lax.axis_size("hi") - 1).bit_length()


def bit_order(flip):
    bits = list(range(hi_bits()))
    return bits[::-1] if flip else bits


def after(v, *deps):
    return lax.optimization_barrier((v, *deps))[0] if deps else v


def together(vs, *deps):
    return list(lax.optimization_barrier((*vs, *deps)))[: len(vs)]


def total_of(terms):
    total = terms[0].astype(F32)
    for term in terms[1:]:
        total = total + term.astype(F32)
    return total


class Gather:
    def __init__(self, v, flip):
        self.v = v
        self.order = bit_order(flip)
        self.done = []

    def hop(self, before=(), beside=()):
        bit = self.order[len(self.done)]
        axis = sum(1 for other in self.done if other > bit)
        got = swap_hi(after(self.v, *before), bit)
        self.v = jnp.stack([self.v, after(got, *beside)], axis=axis)
        self.done.append(bit)
        return got

    def halves(self):
        v = self.v.reshape((-1, self.v.shape[-1]))
        return v, swap_core(v)


class Scatter:
    def __init__(self, own, other, cols):
        self.own, self.cols = own, cols
        self.got = swap_core(other)
        self.stages = [self.spread, self.turn]

    def step(self, *deps):
        return self.stages.pop(0)(*deps) if self.stages else []

    def spread(self, *deps):
        size = lax.axis_size("hi")
        rows = self.own.shape[0] // size
        got = after(self.got, *deps)
        parts = [[v[r * rows : (r + 1) * rows] for v in (self.own, got)] for r in range(size)]
        sent = [total_of(part).astype(BF) for part in parts[1:]]
        self.terms = parts[0]
        self.got = [
            lax.ppermute(v, "hi", [(i, i ^ r) for i in range(size)]) for r, v in zip(range(1, size), sent)
        ]
        return sent

    def turn(self, *deps):
        self.terms = self.terms + [after(v, *deps) for v in self.got]
        return self.send()

    def landed(self):
        return [] if self.stages else self.parts[2:]

    def send(self):
        size = lax.axis_size("mp")
        cols = self.cols

        def block(j):
            return total_of([v[:, j * cols : (j + 1) * cols] for v in self.terms])

        shared = total_of([v[:, size * cols :] for v in self.terms]).astype(BF)
        sent = [jnp.concatenate([block(j).astype(BF), shared], axis=1) for j in range(1, size)]
        self.parts = [block(0), shared] + [swap_mp(v, j) for j, v in zip(range(1, size), sent)]
        return sent


class Halving:
    def __init__(self, halves, cols):
        self.cols = cols
        self.got = [swap_core(halves[1]), swap_core(halves[3])]
        self.stages = [self.halve] * hi_bits() + [self.turn]
        self.shape = (2,) * hi_bits() + (halves[0].shape[0] >> hi_bits(), halves[0].shape[1])
        self.pairs = [[halves[0].reshape(self.shape)], [halves[2].reshape(self.shape)]]
        self.orders = [bit_order(flip)[::-1] for flip in (False, True)]
        self.left = [list(range(hi_bits())) for _ in range(2)]

    def step(self, *deps):
        return self.stages.pop(0)(*deps) if self.stages else []

    def land(self, *deps):
        for p in range(2):
            self.pairs[p].append(after(self.got[p], *deps).reshape(self.pairs[p][0].shape))

    def halve(self, *deps):
        self.land(*deps)
        sent = []
        for p in range(2):
            bit = self.orders[p].pop(0)
            axis = sum(1 for other in self.left[p] if other > bit)
            send = total_of([lax.index_in_dim(t, 1, axis, keepdims=False) for t in self.pairs[p]]).astype(BF)
            self.pairs[p] = [lax.index_in_dim(t, 0, axis, keepdims=False) for t in self.pairs[p]]
            self.left[p].remove(bit)
            self.got[p] = swap_hi(send, bit)
            sent.append(send)
        return sent

    def turn(self, *deps):
        self.land(*deps)
        size = lax.axis_size("mp") // 2
        cols = self.cols

        def block(j):
            p, at = j // size, j % size * cols
            return total_of([v[:, at : at + cols] for v in self.pairs[p]])

        sent = [block(j).astype(BF) for j in range(1, 2 * size)]
        self.parts = [block(0), sent[0][:0]] + [swap_mp(v, j) for j, v in enumerate(sent, 1)]
        return sent

    def landed(self):
        return [] if self.stages else self.parts[2:]


def turns(v):
    return tuple(swap_mp(v, by) for by in range(1, lax.axis_size("mp")))


def pairs_of(v, turned):
    half = lax.axis_size("mp") // 2
    blocks = (v,) + turned
    return [
        Gather(jnp.concatenate(blocks[flip * half : (flip + 1) * half], axis=1), flip)
        for flip in (False, True)
    ]


def halves_of(pairs):
    return tuple(h for pair in pairs for h in pair.halves())


class Halves:
    def __init__(self, arrays):
        self.arrays = arrays
        self.blocks = lax.axis_size("mp")

    def specs(self):
        return [pl.BlockSpec(memory_space=pltpu.VMEM)] * len(self.arrays)

    def reader(self, refs):
        half = self.blocks // 2

        def read(j, lo, hi):
            own, other = refs[2 * (j // half)], refs[2 * (j // half) + 1]
            at = j % half * (own.shape[1] // half)
            return cut((own, other), at + lo, at + hi)

        return read


class Shards:
    def __init__(self, own, other, at, size):
        self.own, self.at, self.size = own, at, size
        self.blocks = lax.axis_size("mp")
        self.hi = lax.axis_size("hi")
        self.arrays = ((own,) * self.hi + (other,) * self.hi) * self.blocks

    def specs(self):
        width, blocks, at, size = self.own.shape[1], self.blocks, self.at, self.size
        return [
            pl.BlockSpec(
                (1, width, size),
                lambda i, pos, r=r, j=j: (
                    (pos[2] ^ r) * blocks + (pos[1] ^ j), 0, at,
                ),
            )
            for j in range(blocks)
            for _ in range(CORES)
            for r in range(self.hi)
        ]

    def reader(self, refs):
        def read(j, lo, hi):
            count = CORES * self.hi
            return jnp.concatenate([ref[0, :, lo:hi] for ref in refs[j * count : (j + 1) * count]], axis=0)

        return read


class GradOut:
    def __init__(self, width, cols, more=0, pairs=True):
        self.cols = cols
        self.count = lax.axis_size("mp") // 2 if pairs else lax.axis_size("mp") + 1
        size = self.count * cols if pairs else (self.count - 1) * cols + more
        self.shapes = (like((width // CORES, size), BF),) * (4 if pairs else 2)

    def writer(self, refs, pos):
        def write(j, lo, v):
            p = j // self.count
            put(refs[2 * p : 2 * p + 2], j % self.count * self.cols + lo, v)

        return write


def mm(a, b):
    return lax.dot_general(a, b, (((1,), (0,)), ((), ())), preferred_element_type=F32)


def mm_nt(a, b):
    return lax.dot_general(a, b, (((1,), (1,)), ((), ())), preferred_element_type=F32)


def mm_tn(a, b):
    return lax.dot_general(a, b, (((0,), (0,)), ((), ())), preferred_element_type=F32)


def unit_of(values):
    mean = jnp.mean(values, axis=-1, keepdims=True)
    centered = values - mean
    scaled = lax.rsqrt(jnp.mean(centered * centered, axis=-1, keepdims=True) + 1e-05)
    return centered * scaled, scaled


def norm_back(gradient, gain, unit, scaled):
    d_gain = jnp.sum(gradient * unit, axis=0, keepdims=True)
    d_shift = jnp.sum(gradient, axis=0, keepdims=True)
    d_unit = gradient * gain
    d_values = scaled * (
        d_unit
        - jnp.mean(d_unit, axis=-1, keepdims=True)
        - unit * jnp.mean(d_unit * unit, axis=-1, keepdims=True)
    )
    return d_values, d_gain, d_shift


def cut(pair, lo, hi):
    return jnp.concatenate([pair[0][:, lo:hi], pair[1][:, lo:hi]], axis=0)


def put(pair, lo, v):
    rows = pair[0].shape[0]
    pair[0][:, lo : lo + v.shape[1]] = v[:rows]
    pair[1][:, lo : lo + v.shape[1]] = v[rows:]


def affine(base, gs, row):
    return base[...] * gs[row : row + 1, :] + gs[row + 1 : row + 2, :]


def pack_kernel(qkv, out, up, down, *outs):
    part, wide = out.shape[2], up.shape[2]
    outs = list(outs)
    places = [(0, outs[0], 0), (1, outs[-1], outs[-1].shape[1] - 4 * part)]
    for l, ref, at in places:
        for c in range(3):
            ref[:, at + c * part : at + (c + 1) * part] = qkv[l, c].astype(BF)
        ref[:, at + 3 * part : at + 4 * part] = out[l].astype(BF)
    for l in range(LAYERS):
        outs[1 + l][:, :wide] = up[l].astype(BF)
        outs[1 + l][:, wide : 2 * wide] = down[l].astype(BF)


def qkv_kernel(ins, w, outs, *, row, part):
    if len(ins) == 2:
        h = affine(*ins, row).astype(BF)
    else:
        x_in, *rest = ins
        base, gs, head = outs[2:]
        embed = cut(rest, 0, HEAD_PAD)
        base[...] = mm_nt(x_in[...], embed)
        h = base[...].astype(BF)
        gs[...] = jnp.zeros_like(gs)
        gs[: 2 * NORMS, :] = embed.astype(F32).T[LOOK : LOOK + 2 * NORMS]
        gs[row : row + 1, :] = jnp.ones((1, gs.shape[1]), F32)
        head[...] = cut(rest, HEAD_PAD, rest[0].shape[1])
    q, kv = outs[:2]
    full = q.shape[1]
    for j in range(full // part):
        got = mm(h, w(j, 0, 3 * part)).astype(BF)
        q[:, j * part : (j + 1) * part] = got[:, :part]
        kv[:, j * part : (j + 1) * part] = got[:, part : 2 * part]
        kv[:, full + j * part : full + (j + 1) * part] = got[:, 2 * part :]


def lane_of(v):
    return lax.broadcasted_iota(jnp.int32, v.shape, 1)


def head_with(v, h, more):
    return jnp.where(lane_of(v) // HEAD_DIM == h, v, more)


def set_tags(id_row, width):
    id_col = jnp.broadcast_to(id_row[...], (8, id_row.shape[1])).T[:, :1]
    rows = id_col.shape[0]
    lane = (lax.broadcasted_iota(jnp.int32, (rows, width), 1) % HEAD_DIM).astype(F32)
    same = lane == id_col
    keys = jnp.where(same, 1.0, 0.0)
    queries = jnp.where(same[: rows // CORES], 0.0, FAR)
    return keys, queries


def three_parts(v):
    first = v.astype(BF).astype(F32)
    second = (v - first).astype(BF).astype(F32)
    return first, second, v - first - second


def with_lanes(tags, first, values):
    lane = lane_of(tags) % HEAD_DIM
    for k, value in enumerate(values):
        tags = jnp.where(lane == first + k, value, tags)
    return tags


def both_rows(own, other, at, part):
    return jnp.concatenate([own[:, at : at + part], other[:, at : at + part]], axis=0)


def attend_kernel(ins, w, outs, *, row, part):
    q, kv, kv_other, id_col, base, gs = ins
    mixed, lse, unit, scaled = outs
    key_tags, query_tags = (t.astype(BF) for t in set_tags(id_col, part))
    full = q.shape[1]
    total = affine(base, gs, row)
    for j in range(full // part):
        at = j * part
        q_part = q[:, at : at + part] * 0.125
        k_part = both_rows(kv, kv_other, at, part)
        v_flip = both_rows(kv, kv_other, full + at, part).T
        flat = []
        for h in range(part // HEAD_DIM):
            s = mm_nt(head_with(k_part, h, key_tags), head_with(q_part, h, query_tags))
            top = jnp.max(s, axis=0, keepdims=True)
            e = jnp.exp(s - top)
            sums = jnp.sum(e, axis=0, keepdims=True)
            o = mm(v_flip[h * HEAD_DIM : (h + 1) * HEAD_DIM], e.astype(BF))
            flat.append(o * (1.0 / sums))
            head = at // HEAD_DIM + h
            lse[head : head + 1, :] = top + jnp.log(sums)
        mixed_part = jnp.concatenate(flat, axis=0).T.astype(BF)
        mixed[:, at : at + part] = mixed_part
        total = total + mm_nt(mixed_part, w(j, 3 * part, 4 * part))
    unit[...], scaled[...] = unit_of(total)


def normal_cdf(x):
    bell = jnp.exp(-0.5 * x * x)
    t = 1.0 / (1.0 + 0.2316418876 * jnp.abs(x))
    tail = 0.5307027145
    for c in (-0.7265760135, 0.7107068705, -0.142248368, 0.127414796):
        tail = tail * t + c
    tail = tail * t * bell
    return jnp.where(x < 0, tail, 1.0 - tail), bell


def feed_kernel(ins, w, outs, *, row, wide):
    unit_in, gs = ins
    act, slope, unit, scaled = outs
    first = affine(unit_in, gs, row)
    y = first.astype(BF)
    total = first
    for j in range(act.shape[1] // wide):
        at = j * wide
        inner = mm(y, w(j, 0, wide))
        cdf, bell = normal_cdf(inner)
        act_part = (inner * cdf).astype(BF)
        act[:, at : at + wide] = act_part
        slope[:, at : at + wide] = (cdf + inner * bell * 0.3989422804014327).astype(BF)
        total = total + mm_nt(act_part, w(j, wide, 2 * wide))
    unit[...], scaled[...] = unit_of(total)


def head_kernel(ins, w, outs, *, row, last):
    unit_in, gs, head_w, counted, *targets = ins
    target = jnp.concatenate([t[...] for t in targets], axis=0)
    counted = counted[...].astype(F32)
    counted = jnp.where(lane_of(counted) < HOR, counted, 0.0)
    loss, g_head0, g_head1, d_hidden, d_norm = outs
    unit, scaled = unit_of(affine(unit_in, gs, row))
    gain = gs[last : last + 1, :]
    final = (unit * gain + gs[last + 1 : last + 2, :]).astype(BF)
    size = head_w.shape[1] // QUANT
    head = head_w[...]
    pred = mm(final, head)
    total = jnp.zeros((1, size), F32)
    grads = []
    for t, level in enumerate(LEVELS):
        gap = target - pred[:, t * size : (t + 1) * size]
        x = gap * (-1.0 / SMOOTHING)
        e = jnp.exp(-jnp.abs(x))
        soft = jnp.maximum(x, 0.0) + jnp.log(1.0 + e)
        sig = jnp.where(x >= 0, 1.0, e) / (1.0 + e)
        total = total + jnp.sum((level * gap + SMOOTHING * soft) * counted, axis=0, keepdims=True)
        grads.append(((sig - level) * counted).astype(BF))
    loss[...] = jnp.concatenate([total, jnp.sum(counted, axis=0, keepdims=True)], axis=0)
    d_pred = jnp.concatenate(grads, axis=1)
    put((g_head0, g_head1), 0, mm(final.T, d_pred).astype(BF))
    d_hidden[...], d_gain, d_shift = norm_back(mm_nt(d_pred, head), gain, unit, scaled)
    d_norm[...] = jnp.concatenate([d_gain, d_shift], axis=0)


def feed_back_kernel(ins, w, outs, g, *, row, wide):
    grad, unit_two, scaled_two, unit_one, scaled_one, gs, act, slope = ins
    d_one, d_norm = outs
    d_two, gain_two, shift_two = norm_back(
        grad[...], gs[row + 2 : row + 3, :], unit_two[...], scaled_two[...]
    )
    d_ffn = d_two.astype(BF)
    d_flip = d_ffn.T
    y_flip = affine(unit_one, gs, row).astype(BF).T
    total = d_two
    for j in range(act.shape[1] // wide):
        at = j * wide
        g(j, wide, mm(d_flip, act[:, at : at + wide]).astype(BF))
        d_act = mm(d_ffn, w(j, wide, 2 * wide))
        d_inner = (d_act * slope[:, at : at + wide].astype(F32)).astype(BF)
        g(j, 0, mm(y_flip, d_inner).astype(BF))
        total = total + mm_nt(d_inner, w(j, 0, wide))
    d_one[...], gain_one, shift_one = norm_back(
        total, gs[row : row + 1, :], unit_one[...], scaled_one[...]
    )
    d_norm[...] = jnp.concatenate([gain_one, shift_one, gain_two, shift_two], axis=0)


def attend_back_kernel(ins, w, outs, *, part, first):
    d_one, q, kv, kv_other, id_col, lse, mixed = ins
    g_out, d_q, d_kv, d_kv_other = outs
    key_tags, query_tags = set_tags(id_col, part)
    key_tags = with_lanes(key_tags, SETS, (1.0, 1.0, 1.0)).astype(BF)
    value_tags = with_lanes(jnp.zeros(key_tags.shape, F32), 0, (1.0, 1.0, 1.0)).astype(BF)
    log_sums = lse[...].T
    full = q.shape[1]
    rows, here = d_q.shape
    d_branch = d_one[...].astype(BF)
    g_out[...] = mm(d_branch.T, mixed[:, first * part : first * part + here]).astype(BF)
    for j in range(first, first + here // part):
        at, to = j * part, (j - first) * part
        d_mixed_wide = mm(d_branch, w(j, 3 * part, 4 * part))
        d_mixed = d_mixed_wide.astype(BF)
        q_part = q[:, at : at + part] * 0.125
        k_part = both_rows(kv, kv_other, at, part)
        v_part = both_rows(kv, kv_other, full + at, part)
        k_flip = k_part.T
        product = d_mixed.astype(F32) * mixed[:, at : at + part].astype(F32)
        d_k = d_v = None
        d_q_flip = []
        for h in range(part // HEAD_DIM):
            head = at // HEAD_DIM + h
            log_sum = log_sums[:, head : head + 1]
            dots = jnp.sum(head_with(product, h, 0.0), axis=1, keepdims=True)
            q_tags = with_lanes(query_tags, SETS, three_parts(-log_sum)).astype(BF)
            d_tags = with_lanes(jnp.zeros_like(product), 0, three_parts(-dots)).astype(BF)
            probs = jnp.exp(mm_nt(head_with(k_part, h, key_tags), head_with(q_part, h, q_tags)))
            shifted = mm_nt(head_with(v_part, h, value_tags), head_with(d_mixed, h, d_tags))
            d_s = (probs * shifted).astype(BF)
            more_v = mm(probs.astype(BF), d_mixed)
            more_k = mm(d_s, q_part)
            d_v = more_v if d_v is None else head_with(more_v, h, d_v)
            d_k = more_k if d_k is None else head_with(more_k, h, d_k)
            d_q_flip.append(mm(k_flip[h * HEAD_DIM : (h + 1) * HEAD_DIM], d_s))
        d_q[:, to : to + part] = (jnp.concatenate(d_q_flip, axis=0) * 0.125).T.astype(BF)
        d_kv[:, to : to + part] = d_k[:rows]
        d_kv_other[:, to : to + part] = d_k[rows:].astype(BF)
        d_kv[:, here + to : here + to + part] = d_v[:rows]
        d_kv_other[:, here + to : here + to + part] = d_v[rows:].astype(BF)


def qkv_back_kernel(ins, w, outs, g, *, row, part):
    d_one, base, gs, *rest = ins
    halves, rest = (rest[:4], rest[4:8]), rest[8:]
    (d_hidden,) = outs
    full = d_one.shape[1]
    h_flip = affine(base, gs, row).astype(BF).T
    total = d_one[...]
    for j in range(full // part):
        here = halves[0][0].shape[1]
        d_q, d_kv, got, g_out = halves[j * part // here]
        at = j * part % here
        d_all = [d_q[:, at : at + part]]
        for base_at in (at, here + at):
            d_all.append(
                (
                    d_kv[:, base_at : base_at + part] + got[:, base_at : base_at + part].astype(F32)
                ).astype(BF)
            )
        d_all = jnp.concatenate(d_all, axis=1)
        g(j, 0, mm(h_flip, d_all).astype(BF))
        g(j, 3 * part, g_out[:, at : at + part])
        total = total + mm_nt(d_all, w(j, 0, 3 * part))
    d_hidden[...] = total
    if len(rest) == CORES:
        g(full // part, 0, jnp.concatenate([r[...] for r in rest], axis=0))
    else:
        x_in, *norms = rest
        rows = [jnp.zeros((LOOK, total.shape[1]), F32)] + [n[...] for n in norms]
        rows.append(jnp.zeros((HEAD_PAD - LOOK - 2 * NORMS, total.shape[1]), F32))
        g(full // part, 0, (mm(total.astype(BF).T, x_in[...]) + jnp.concatenate(rows, axis=0).T).astype(BF))


def finish_kernel(at, *refs, blocks, shared):
    count = len(shared)
    ins, outs = refs[: 1 + count * (blocks + 1)], refs[1 + count * (blocks + 1) :]
    z = at[1]
    squares = jnp.zeros((), F32)
    for c in range(count):
        own, common, *turned = ins[1 + c * (blocks + 1) : 1 + (c + 1) * (blocks + 1)]
        cols = own.shape[1]
        total = own[...]
        for t in turned:
            total = total + t[:, :cols].astype(F32)
        outs[c][...] = total
        squares = squares + jnp.sum(total * total)
        if shared[c]:
            held = [common[...].astype(F32)] + [t[:, cols:].astype(F32) for t in turned]
            total = jnp.zeros_like(held[0])
            for owner in range(blocks):
                by = z ^ owner
                term = held[0]
                for j in range(1, blocks):
                    term = jnp.where(by == j, held[j], term)
                total = total + term
            outs[count + sum(shared[:c])][...] = total
            squares = squares + jnp.where(z == 0, jnp.sum(total * total), 0.0)
    loss = ins[0]
    place = lax.broadcasted_iota(jnp.int32, outs[-1].shape, 1)
    outs[-1][...] = jnp.where(
        place == 0,
        jnp.sum(loss[0:1, :]),
        jnp.where(place == 1, jnp.sum(loss[1:2, :]), jnp.where(place == 2, squares, 0.0)),
    )


def scalars_of(sums):
    total = jnp.sum(sums, axis=0, keepdims=True)

    def lane(k):
        return jnp.sum(jnp.where(lane_of(total) == k, total, 0.0), axis=1, keepdims=True)

    valid_count = lane(1)
    grad_norm = jnp.sqrt(lane(2)) / valid_count
    factor = jnp.minimum(1.0, CLIP_NORM / grad_norm) / valid_count
    place = lane_of(total)
    return jnp.where(place == 2, grad_norm, jnp.where(place == 3, factor, total)), factor


def scalars_kernel(sums, out):
    out[...], _ = scalars_of(sums[...])


def update_kernel(sums, *refs, count):
    grads, held, refs = refs[:count], refs[count : 4 * count], refs[4 * count :]
    scalars, outs, refs = refs[0], refs[1 : 1 + 3 * count], refs[1 + 3 * count :]
    old, new, (arrived, left) = refs[: 3 * count], refs[3 * count : 6 * count], refs[6 * count :]
    into = [pltpu.make_async_copy(a, b, arrived.at[k]) for k, (a, b) in enumerate(zip(held, old))]
    back = [pltpu.make_async_copy(a, b, left.at[k]) for k, (a, b) in enumerate(zip(new, outs))]
    for copy in into:
        copy.start()
    scalars[...], factor = scalars_of(sums[...])
    for n in range(count):
        for k in range(3 * n, 3 * n + 3):
            into[k].wait()
        w, m, v = (ref[...] for ref in old[3 * n : 3 * n + 3])
        g = grads[n][...] * factor.reshape((1,) * len(w.shape))
        done = adam_update(w, g, m, v, LEARN_RATE, WEIGHT_DECAY)
        for k, value in enumerate(done, 3 * n):
            new[k][...] = value
            back[k].start()
    for copy in back:
        copy.wait()


def kernel_call(kernel, pos, ins, weights, outs, grads=None, scratch=(), us=1.0, **static):
    whole = pl.BlockSpec(memory_space=pltpu.VMEM)
    w_arrays = weights.arrays if weights else ()
    g_shapes = grads.shapes if grads else ()

    def run(at, *refs):
        refs = list(refs)

        def take(count):
            got = refs[:count]
            del refs[:count]
            return got

        in_refs = take(len(ins))
        w_refs = take(len(w_arrays))
        out_refs = take(len(outs))
        g_refs = take(len(g_shapes))
        more = [grads.writer(g_refs, at)] if grads else []
        kernel(in_refs, weights.reader(w_refs) if weights else None, out_refs, *more, *refs, **static)

    return pl.pallas_call(
        run,
        out_shape=tuple(outs) + tuple(g_shapes),
        grid_spec=pltpu.PrefetchScalarGridSpec(
            num_scalar_prefetch=1,
            grid=(1,),
            in_specs=[whole] * len(ins) + (weights.specs() if weights else []),
            out_specs=tuple(whole for _ in range(len(outs) + len(g_shapes))),
            scratch_shapes=scratch,
        ),
        compiler_params=pltpu.CompilerParams(vmem_limit_bytes=20 * 1024 * 1024),
        cost_estimate=pl.CostEstimate(flops=int(us * 1.15e9), bytes_accessed=0, transcendentals=0),
    )(pos, *ins, *w_arrays)


def kernel_call_plain(kernel, outs, *args, pos=None, limit=20):
    whole = pl.BlockSpec(memory_space=pltpu.VMEM)
    first = [] if pos is None else [pl.BlockSpec(memory_space=pltpu.SMEM)]
    return pl.pallas_call(
        kernel,
        out_shape=outs,
        in_specs=first + [whole] * len(args),
        out_specs=tuple(whole for _ in outs),
        compiler_params=pltpu.CompilerParams(vmem_limit_bytes=limit * 1024 * 1024),
    )(*(() if pos is None else (pos,)), *args)


def like(shape, dtype):
    return jax.ShapeDtypeStruct(shape, dtype)


def adam_update(weight, gradient, first_moment, second_moment, rate, decay):
    first_moment = BETA_ONE * first_moment + (1 - BETA_ONE) * gradient
    second_moment = BETA_TWO * second_moment + (1 - BETA_TWO) * gradient * gradient
    update = (
        first_moment
        / (1 - BETA_ONE**STEP)
        / (jnp.sqrt(second_moment / (1 - BETA_TWO**STEP)) + EPSILON)
    )
    return (weight - rate * (update + decay * weight), first_moment, second_moment)


def deal_swap(v):
    rows = v.shape[1] // CORES
    core = lax.axis_index("core")
    v = v.reshape(MICRO, CORES, rows, v.shape[-1])
    keep = lax.dynamic_index_in_dim(v, core, 1, keepdims=False)
    send = lax.dynamic_index_in_dim(v, 1 - core, 1, keepdims=False)
    got = swap_core(send)
    return jnp.where(core == 0, jnp.concatenate([keep, got]), jnp.concatenate([got, keep]))


def deal_halves_kernel(at, whole, keep, send):
    rows = keep.shape[1]
    for m in range(MICRO):
        keep[m] = whole[m, pl.ds(pl.multiple_of(at[3] * rows, rows), rows), :]
        send[m] = whole[m, pl.ds(pl.multiple_of((1 - at[3]) * rows, rows), rows), :]


def deal_parts_kernel(at, keep, got, *parts):
    for by, part in enumerate(parts):
        owner = at[1] ^ by
        part[...] = jnp.zeros_like(part)
        part[:, : keep.shape[2]] = jnp.where(
            owner // MICRO == at[3], keep[owner % MICRO], got[owner % MICRO]
        )


def deal_rows(v):
    size = lax.axis_size("mp")
    z = lax.axis_index("mp")
    parts = [lax.dynamic_index_in_dim(v, z ^ by, 0, keepdims=False) for by in range(size)]
    return jnp.concatenate(parts[:1] + [swap_mp(parts[by], by) for by in range(1, size)])


def body(
    series,
    targets,
    valid,
    dataset_ids,
    embed_w,
    qkv_w,
    out_w,
    up_w,
    down_w,
    head_w,
    norm_params,
    *moments,
):
    (
        embed_first,
        embed_second,
        qkv_first,
        qkv_second,
        out_first,
        out_second,
        up_first,
        up_second,
        down_first,
        down_second,
        head_first,
        head_second,
        norm_first,
        norm_second,
    ) = moments
    width = embed_w.shape[1]
    part = qkv_w.shape[3]
    wide = up_w.shape[2]
    blocks_n = lax.axis_size("mp")

    bits = hi_bits()
    hi_at, core_at, z_at = lax.axis_index("hi"), lax.axis_index("core"), lax.axis_index("mp")
    pos = jnp.stack([hi_at * CORES + core_at, z_at, hi_at, core_at]).astype(jnp.int32)
    att_w, ffn_w, late = {}, {}, None
    placed = width % 16 == 0
    packed = kernel_call_plain(
        pack_kernel,
        tuple(like((width, cols), BF) for cols in (4 * part, 2 * wide, 2 * wide, 4 * part))
        if not placed
        else (like((width, 4 * part), BF), like((width, 2 * wide), BF), like((width, 2 * wide + 4 * part), BF)),
        qkv_w.transpose(0, 2, 1, 3), out_w, up_w, down_w,
        limit=56,
    )
    att_w[0], ffn_w[0], ffn_w[1], att_w[1] = (*packed, None) if placed else packed
    if placed:
        late = lax.all_gather(ffn_w[1], ("hi", "mp"), axis=0, tiled=False)
        late = late.reshape((-1,) + late.shape[-2:])

    low_pad = HEAD_PAD - LOOK - 2 * NORMS
    embed_cols = jnp.concatenate([embed_w.T, norm_params.reshape(-1, width).T], axis=1)
    head_cols = jnp.pad(head_w.reshape(width, QUANT, HOR), ((0, 0), (0, 0), (0, HEAD_PAD - HOR)))
    rest = Gather(
        jnp.concatenate(
            [jnp.pad(embed_cols, ((0, 0), (0, low_pad))), head_cols.reshape(width, -1)], axis=1
        ).astype(BF),
        False,
    )
    low = deal_swap(
        jnp.pad(
            jnp.concatenate(
                [
                    jnp.pad(series, ((0, 0), (0, 0), (0, HEAD_PAD - LOOK))),
                    valid.astype(BF),
                    dataset_ids[..., None].astype(BF),
                ],
                axis=-1,
            ),
            ((0, 0), (0, 0), (0, HEAD_PAD - HOR - 1)),
        )
    )
    z_att = turns(att_w[0])
    rest.hop()
    att_pairs = pairs_of(att_w[0], z_att)
    hop_att = [pair.hop() for pair in att_pairs]
    low = deal_rows(after(low, *z_att))
    for _ in range(1, bits):
        rest.hop(before=hop_att)
    rest = rest.halves()
    ffn_first = after(ffn_w[0], *hop_att)
    z_ffn = turns(ffn_first)
    for _ in range(1, bits):
        hop_att = [pair.hop() for pair in att_pairs]
    att = [Halves(halves_of(att_pairs))]
    ffn_pairs = pairs_of(ffn_first, z_ffn)
    for _ in range(bits - 1):
        for pair in ffn_pairs:
            pair.hop()

    model = CORES * rest[0].shape[0]
    ident = 2 * NORMS
    x_in = low[:, :HEAD_PAD]
    counted = low[:, HEAD_PAD : 2 * HEAD_PAD]
    ids_here = low[:, HEAD_PAD + HOR].reshape(1, -1)
    ids = jnp.concatenate([ids_here, swap_core(ids_here)], axis=1).astype(F32)
    rows = x_in.shape[0]
    heads = model // HEAD_DIM
    hidden_n = wide * blocks_n

    base, row = None, ident
    stored = []
    ffn = []
    for l in range(LAYERS):
        q, kv, *more = kernel_call(
            qkv_kernel, pos, (base, gs) if l else (x_in, *rest), att[l],
            (like((rows, model), BF), like((rows, 2 * model), BF))
            + (() if l else (like((rows, model), F32), like((16, model), F32), like((model, QUANT * HEAD_PAD), BF))),
            us=1.3, row=row, part=part,
        )
        if l == 0:
            base, gs, head_w_all = more
        kv_other = swap_core(kv)
        if l == 0:
            q = after(q, *(pair.v for pair in ffn_pairs))
        mixed, lse, unit_one, scaled_one = kernel_call(
            attend_kernel, pos, (q, kv, kv_other, ids, base, gs), att[l],
            (like((rows, model), BF), like((heads, rows), F32), like((rows, model), F32), like((rows, 1), F32)),
            us=11, row=row, part=part,
        )
        if l == 1:
            target = [parts[0]] + [swap_mp(parts[by], by) for by in range(1, blocks_n)]
            unit_one = after(unit_one, *together(target, mixed))
        if l == 0:
            for pair in ffn_pairs:
                pair.hop(before=(kv,), beside=(mixed,))
            ffn.append(Halves(halves_of(ffn_pairs)))
            if not placed:
                for kept, v in ((att, att_w[1]), (ffn, ffn_w[1])):
                    pairs = pairs_of(v, turns(v))
                    for _ in range(bits):
                        for pair in pairs:
                            pair.hop()
                    kept.append(Halves(halves_of(pairs)))
        act, slope, unit_two, scaled_two = kernel_call(
            feed_kernel, pos, (unit_one, gs), ffn[l],
            (like((rows, hidden_n), BF), like((rows, hidden_n), BF), like((rows, model), F32), like((rows, 1), F32)),
            us=10, row=4 * l, wide=wide,
        )
        stored.append((base, row, q, kv, kv_other, mixed, lse, unit_one, scaled_one, act, slope, unit_two, scaled_two))
        base, row = unit_two, 4 * l + 2
        if l == 0:
            half = (MICRO, targets.shape[1] // CORES, HOR)
            keep, send = kernel_call_plain(
                deal_halves_kernel, (like(half, F32), like(half, F32)), after(targets, unit_two), pos=pos
            )
            parts = kernel_call_plain(
                deal_parts_kernel,
                (like((half[1], HEAD_PAD), F32),) * blocks_n,
                keep, swap_core(send),
                pos=pos,
            )
            base = after(base, *parts)
        if l == 0 and placed:
            late = after(late, unit_two)
            other = swap_core(late)
            att.append(Shards(late, other, 2 * wide // (4 * part), 4 * part))
            ffn.append(Shards(late, other, 0, 2 * wide))
    loss_row, *g_head, grad, d_norm_last = kernel_call(
        head_kernel, pos, (base, gs, head_w_all, counted, *target), None,
        (like((2, HEAD_PAD), F32),)
        + (like((model // CORES, QUANT * HEAD_PAD), BF),) * CORES
        + (like((rows, model), F32), like((2, model), F32)),
        us=2, row=row, last=2 * NORMS - 2,
    )
    norm_grads = [None] * LAYERS
    sums = []

    def feed_back(l, grad):
        unit_one, scaled_one, act, slope, unit_two, scaled_two = stored[l][7:]
        return kernel_call(
            feed_back_kernel, pos,
            (grad, unit_two, scaled_two, unit_one, scaled_one, gs, act, slope), ffn[l],
            (like((rows, model), F32), like((4, model), F32)),
            grads=GradOut(model, 2 * wide),
            us=10.5, row=4 * l, wide=wide,
        )

    def attend_back(l, d_one, half):
        q, kv, kv_other, mixed, lse = stored[l][2:7]
        here = model // 2
        g_out, d_q, d_kv, d_kv_other = kernel_call(
            attend_back_kernel, pos,
            (d_one, q, kv, kv_other, ids, lse, mixed), att[l],
            (like((model, here), BF), like((rows, here), BF), like((rows, 2 * here), F32), like((rows, 2 * here), BF)),
            us=8, part=part, first=half * here // part,
        )
        return d_q, d_kv, swap_core(d_kv_other), g_out

    def qkv_back(l, d_one, *args):
        base, row = stored[l][:2]
        more = (x_in, *norm_grads, d_norm_last) if l == 0 else tuple(g_head)
        return kernel_call(
            qkv_back_kernel, pos, (d_one, base, gs, *args, *more), att[l],
            (like((rows, model), F32),),
            grads=GradOut(model, 4 * part, more=HEAD_PAD if l == 0 else QUANT * HEAD_PAD, pairs=False),
            us=5.5, row=row, part=part,
        )

    d_one, norm_grads[1], *halves = feed_back(1, grad)
    ffn_sum = Halving(halves, 2 * wide)
    first = attend_back(1, d_one, 0)
    sent = ffn_sum.step(first[0])
    second = attend_back(1, after(d_one, first[0], *sent), 1)
    sent = ffn_sum.step(second[0])
    grad, *halves = qkv_back(1, after(d_one, *sent), *first, *second)
    att_sum = Scatter(*halves, 4 * part)
    sent = ffn_sum.step(grad)

    d_one, norm_grads[0], *halves = feed_back(0, after(grad, *sent))
    ffn_low = Halving(halves, 2 * wide)
    sent = att_sum.step(d_one) + ffn_sum.step(d_one)
    d_one = after(d_one, *sent, *ffn_sum.landed())
    first = attend_back(0, d_one, 0)
    sent = ffn_low.step(first[0])
    second = attend_back(0, after(d_one, first[0], *sent), 1)
    sent = att_sum.step(second[0]) + ffn_low.step(second[0])
    _, own, other = qkv_back(0, after(d_one, *sent), *first, *second)
    att_low = Scatter(own, after(other, *att_sum.landed()), 4 * part)
    for chunk in (ffn_sum, att_sum, ffn_low):
        while chunk.stages:
            chunk.step(own)
    att_low.step()
    att_low.step(*ffn_low.landed())
    sums = [ffn_sum, att_sum, ffn_low, att_low]

    count = lax.axis_size("hi") * CORES * blocks_n
    *grads, g_head, g_low, scalars = kernel_call_plain(
        functools.partial(finish_kernel, blocks=blocks_n, shared=(False, True, False, True)),
        tuple(like((width, s.cols), F32) for s in sums)
        + (like((width, QUANT * HEAD_PAD), F32), like((width, HEAD_PAD), F32), like((count, 128), F32)),
        loss_row,
        *(v for s in sums for v in (s.parts if s.parts[1].size else [s.parts[0], s.parts[0]] + s.parts[2:])),
        pos=pos,
    )
    g_ffn1, g_att1, g_ffn0, g_att0 = grads
    scalars = lax.all_to_all(
        scalars.reshape(count, 1, 128), ("hi", "core", "mp"), 0, 0, tiled=True
    ).reshape(count, 128)
    g_qkv = jnp.stack(
        [jnp.stack([g[:, c * part : (c + 1) * part] for c in range(3)]) for g in (g_att0, g_att1)]
    )
    g_out = jnp.stack([g[:, 3 * part :] for g in (g_att0, g_att1)])
    g_up = jnp.stack([g[:, :wide] for g in (g_ffn0, g_ffn1)])
    g_down = jnp.stack([g[:, wide:] for g in (g_ffn0, g_ffn1)])
    g_norm = g_low[:, LOOK : LOOK + 2 * NORMS].T.reshape(norm_params.shape)
    g_head = g_head.reshape(width, QUANT, HEAD_PAD)[:, :, :HOR].reshape(width, -1)
    sets = (
        (*(v.transpose(0, 2, 1, 3) for v in (qkv_w, qkv_first, qkv_second)), g_qkv),
        (out_w, out_first, out_second, g_out),
        (up_w, up_first, up_second, g_up),
        (down_w, down_first, down_second, g_down),
    )
    shapes = [one[0].shape for one in sets for _ in range(3)]
    whole, away = pl.BlockSpec(memory_space=pltpu.VMEM), pl.BlockSpec(memory_space=pl.ANY)
    count = len(sets)
    scalars, *news = pl.pallas_call(
        functools.partial(update_kernel, count=count),
        out_shape=(like((1, 128), F32),) + tuple(like(shape, F32) for shape in shapes),
        in_specs=[whole] * (1 + count) + [away] * (3 * count),
        out_specs=(whole,) + (away,) * (3 * count),
        scratch_shapes=[pltpu.VMEM(shape, F32) for shape in shapes * 2] + [pltpu.SemaphoreType.DMA((3 * count,))] * 2,
        compiler_params=pltpu.CompilerParams(vmem_limit_bytes=20 * 1024 * 1024),
    )(after(scalars, g_head, g_norm), *(one[3] for one in sets), *(v for one in sets for v in one[:3]))
    news[:3] = [v.transpose(0, 2, 1, 3) for v in news[:3]]
    factor = scalars[0, 3]
    e_new = adam_update(
        embed_w.T, g_low[:, :LOOK] * factor, embed_first.T, embed_second.T, LEARN_RATE, WEIGHT_DECAY
    )
    h_new = adam_update(head_w, g_head * factor, head_first, head_second, LEARN_RATE, WEIGHT_DECAY)
    n_new = adam_update(norm_params, g_norm * factor, norm_first, norm_second, NORM_RATE, 0.0)
    return (scalars[0, 0], scalars[0, 1], scalars[0, 2], *(v.T for v in e_new), *news, *h_new, *n_new)


def solution(mesh):
    dp, mp = mesh.devices.shape
    split = Mesh(mesh.devices.reshape(dp // CORES, CORES, mp), ("hi", "core", "mp"))
    wide = ("hi", "core")
    tokens = ("hi", "core", "mp")
    embed = P(None, wide)
    qkv = P(None, wide, None, "mp")
    mat = P(None, wide, "mp")
    head = P(wide, None)
    norm = P(None, None, wide)
    weights = (embed, qkv, mat, mat, mat, head, norm)
    return jax.shard_map(
        body,
        mesh=split,
        in_specs=(P(None, tokens, None),) * 3
        + (P(None, tokens),)
        + weights
        + tuple(spec for spec in weights for _ in range(2)),
        out_specs=(P(),) * 3 + tuple(spec for spec in weights for _ in range(3)),
        check_vma=False,
    )
```

```python
import functools

import jax
import jax.numpy as jnp
from jax import lax
from jax.experimental import pallas as pl
from jax.experimental.pallas import tpu as pltpu
from jax.sharding import Mesh
from jax.sharding import PartitionSpec as P

HEAD_DIM = 64
LAYERS = 2
HOR = 96
LOOK = 96
QUANT = 3
MICRO = 2
STEP = 10
NORMS = 5
CORES = 2
HEAD_PAD = 128
SETS = 16
FAR = -1e30

SMOOTHING = 0.1
LEVELS = (0.1, 0.5, 0.9)
CLIP_NORM = 0.0001
LEARN_RATE = 0.05
NORM_RATE = 0.5
BETA_ONE = 0.9
BETA_TWO = 0.999
EPSILON = 1e-12
WEIGHT_DECAY = 0.1

BF = jnp.bfloat16
F32 = jnp.float32


def swap_core(v):
    return lax.ppermute(v, "core", [(0, 1), (1, 0)])


def swap_hi(v, bit):
    size = lax.axis_size("hi")
    return lax.ppermute(v, "hi", [(i, i ^ (1 << bit)) for i in range(size)])


def swap_mp(v, by):
    size = lax.axis_size("mp")
    return lax.ppermute(v, "mp", [(i, i ^ by) for i in range(size)])


def hi_bits():
    return (lax.axis_size("hi") - 1).bit_length()


def bit_order(flip):
    bits = list(range(hi_bits()))
    return bits[::-1] if flip else bits


def after(v, *deps):
    return lax.optimization_barrier((v, *deps))[0] if deps else v


def together(vs, *deps):
    return list(lax.optimization_barrier((*vs, *deps)))[: len(vs)]


def total_of(terms):
    total = terms[0].astype(F32)
    for term in terms[1:]:
        total = total + term.astype(F32)
    return total


class Gather:
    def __init__(self, v, flip):
        self.v = v
        self.order = bit_order(flip)
        self.done = []

    def hop(self, before=(), beside=()):
        bit = self.order[len(self.done)]
        axis = sum(1 for other in self.done if other > bit)
        got = swap_hi(after(self.v, *before), bit)
        self.v = jnp.stack([self.v, after(got, *beside)], axis=axis)
        self.done.append(bit)
        return got

    def halves(self):
        v = self.v.reshape((-1, self.v.shape[-1]))
        return v, swap_core(v)


class Scatter:
    def __init__(self, own, other, cols):
        self.own, self.cols = own, cols
        self.got = swap_core(other)
        self.stages = [self.spread, self.turn]

    def step(self, *deps):
        return self.stages.pop(0)(*deps) if self.stages else []

    def spread(self, *deps):
        size = lax.axis_size("hi")
        rows = self.own.shape[0] // size
        got = after(self.got, *deps)
        parts = [[v[r * rows : (r + 1) * rows] for v in (self.own, got)] for r in range(size)]
        sent = [total_of(part).astype(BF) for part in parts[1:]]
        self.terms = parts[0]
        self.got = [
            lax.ppermute(v, "hi", [(i, i ^ r) for i in range(size)]) for r, v in zip(range(1, size), sent)
        ]
        return sent

    def turn(self, *deps):
        self.terms = self.terms + [after(v, *deps) for v in self.got]
        return self.send()

    def landed(self):
        return [] if self.stages else self.parts[2:]

    def send(self):
        size = lax.axis_size("mp")
        cols = self.cols

        def block(j):
            return total_of([v[:, j * cols : (j + 1) * cols] for v in self.terms])

        shared = total_of([v[:, size * cols :] for v in self.terms]).astype(BF)
        sent = [jnp.concatenate([block(j).astype(BF), shared], axis=1) for j in range(1, size)]
        self.parts = [block(0), shared] + [swap_mp(v, j) for j, v in zip(range(1, size), sent)]
        return sent


class Halving:
    def __init__(self, halves, cols):
        self.cols = cols
        self.got = [swap_core(halves[1]), swap_core(halves[3])]
        self.stages = [self.halve] * hi_bits() + [self.turn]
        self.shape = (2,) * hi_bits() + (halves[0].shape[0] >> hi_bits(), halves[0].shape[1])
        self.pairs = [[halves[0].reshape(self.shape)], [halves[2].reshape(self.shape)]]
        self.orders = [bit_order(flip)[::-1] for flip in (False, True)]
        self.left = [list(range(hi_bits())) for _ in range(2)]

    def step(self, *deps):
        return self.stages.pop(0)(*deps) if self.stages else []

    def land(self, *deps):
        for p in range(2):
            self.pairs[p].append(after(self.got[p], *deps).reshape(self.pairs[p][0].shape))

    def halve(self, *deps):
        self.land(*deps)
        sent = []
        for p in range(2):
            bit = self.orders[p].pop(0)
            axis = sum(1 for other in self.left[p] if other > bit)
            send = total_of([lax.index_in_dim(t, 1, axis, keepdims=False) for t in self.pairs[p]]).astype(BF)
            self.pairs[p] = [lax.index_in_dim(t, 0, axis, keepdims=False) for t in self.pairs[p]]
            self.left[p].remove(bit)
            self.got[p] = swap_hi(send, bit)
            sent.append(send)
        return sent

    def turn(self, *deps):
        self.land(*deps)
        size = lax.axis_size("mp") // 2
        cols = self.cols

        def block(j):
            p, at = j // size, j % size * cols
            return total_of([v[:, at : at + cols] for v in self.pairs[p]])

        sent = [block(j).astype(BF) for j in range(1, 2 * size)]
        self.parts = [block(0), sent[0][:0]] + [swap_mp(v, j) for j, v in enumerate(sent, 1)]
        return sent

    def landed(self):
        return [] if self.stages else self.parts[2:]


def turns(v):
    return tuple(swap_mp(v, by) for by in range(1, lax.axis_size("mp")))


def pairs_of(v, turned):
    half = lax.axis_size("mp") // 2
    blocks = (v,) + turned
    return [
        Gather(jnp.concatenate(blocks[flip * half : (flip + 1) * half], axis=1), flip)
        for flip in (False, True)
    ]


def halves_of(pairs):
    return tuple(h for pair in pairs for h in pair.halves())


class Halves:
    def __init__(self, arrays):
        self.arrays = arrays
        self.blocks = lax.axis_size("mp")

    def specs(self):
        return [pl.BlockSpec(memory_space=pltpu.VMEM)] * len(self.arrays)

    def reader(self, refs):
        half = self.blocks // 2

        def read(j, lo, hi):
            own, other = refs[2 * (j // half)], refs[2 * (j // half) + 1]
            at = j % half * (own.shape[1] // half)
            return cut((own, other), at + lo, at + hi)

        return read


class Shards:
    def __init__(self, own, other, at, size):
        self.own, self.at, self.size = own, at, size
        self.blocks = lax.axis_size("mp")
        self.hi = lax.axis_size("hi")
        self.arrays = ((own,) * self.hi + (other,) * self.hi) * self.blocks

    def specs(self):
        width, blocks, at, size = self.own.shape[1], self.blocks, self.at, self.size
        return [
            pl.BlockSpec(
                (1, width, size),
                lambda i, pos, r=r, j=j: (
                    (pos[2] ^ r) * blocks + (pos[1] ^ j), 0, at,
                ),
            )
            for j in range(blocks)
            for _ in range(CORES)
            for r in range(self.hi)
        ]

    def reader(self, refs):
        def read(j, lo, hi):
            count = CORES * self.hi
            return jnp.concatenate([ref[0, :, lo:hi] for ref in refs[j * count : (j + 1) * count]], axis=0)

        return read


class GradOut:
    def __init__(self, width, cols, more=0, pairs=True):
        self.cols = cols
        self.count = lax.axis_size("mp") // 2 if pairs else lax.axis_size("mp") + 1
        size = self.count * cols if pairs else (self.count - 1) * cols + more
        self.shapes = (like((width // CORES, size), BF),) * (4 if pairs else 2)

    def writer(self, refs, pos):
        def write(j, lo, v):
            p = j // self.count
            put(refs[2 * p : 2 * p + 2], j % self.count * self.cols + lo, v)

        return write


def mm(a, b):
    return lax.dot_general(a, b, (((1,), (0,)), ((), ())), preferred_element_type=F32)


def mm_nt(a, b):
    return lax.dot_general(a, b, (((1,), (1,)), ((), ())), preferred_element_type=F32)


def mm_tn(a, b):
    return lax.dot_general(a, b, (((0,), (0,)), ((), ())), preferred_element_type=F32)


def unit_of(values):
    mean = jnp.mean(values, axis=-1, keepdims=True)
    centered = values - mean
    scaled = lax.rsqrt(jnp.mean(centered * centered, axis=-1, keepdims=True) + 1e-05)
    return centered * scaled, scaled


def norm_back(gradient, gain, unit, scaled):
    d_gain = jnp.sum(gradient * unit, axis=0, keepdims=True)
    d_shift = jnp.sum(gradient, axis=0, keepdims=True)
    d_unit = gradient * gain
    d_values = scaled * (
        d_unit
        - jnp.mean(d_unit, axis=-1, keepdims=True)
        - unit * jnp.mean(d_unit * unit, axis=-1, keepdims=True)
    )
    return d_values, d_gain, d_shift


def cut(pair, lo, hi):
    return jnp.concatenate([pair[0][:, lo:hi], pair[1][:, lo:hi]], axis=0)


def put(pair, lo, v):
    rows = pair[0].shape[0]
    pair[0][:, lo : lo + v.shape[1]] = v[:rows]
    pair[1][:, lo : lo + v.shape[1]] = v[rows:]


def affine(base, gs, row):
    return base[...] * gs[row : row + 1, :] + gs[row + 1 : row + 2, :]


def pack_kernel(qkv, out, up, down, *outs):
    part, wide = out.shape[2], up.shape[2]
    outs = list(outs)
    places = [(0, outs[0], 0), (1, outs[-1], outs[-1].shape[1] - 4 * part)]
    for l, ref, at in places:
        for c in range(3):
            ref[:, at + c * part : at + (c + 1) * part] = qkv[l, c].astype(BF)
        ref[:, at + 3 * part : at + 4 * part] = out[l].astype(BF)
    for l in range(LAYERS):
        outs[1 + l][:, :wide] = up[l].astype(BF)
        outs[1 + l][:, wide : 2 * wide] = down[l].astype(BF)


def qkv_kernel(ins, w, outs, *, row, part):
    if len(ins) == 2:
        h = affine(*ins, row).astype(BF)
    else:
        x_in, *rest = ins
        base, gs, head = outs[2:]
        embed = cut(rest, 0, HEAD_PAD)
        base[...] = mm_nt(x_in[...], embed)
        h = base[...].astype(BF)
        gs[...] = jnp.zeros_like(gs)
        gs[: 2 * NORMS, :] = embed.astype(F32).T[LOOK : LOOK + 2 * NORMS]
        gs[row : row + 1, :] = jnp.ones((1, gs.shape[1]), F32)
        head[...] = cut(rest, HEAD_PAD, rest[0].shape[1])
    q, kv = outs[:2]
    full = q.shape[1]
    for j in range(full // part):
        got = mm(h, w(j, 0, 3 * part)).astype(BF)
        q[:, j * part : (j + 1) * part] = got[:, :part]
        kv[:, j * part : (j + 1) * part] = got[:, part : 2 * part]
        kv[:, full + j * part : full + (j + 1) * part] = got[:, 2 * part :]


def lane_of(v):
    return lax.broadcasted_iota(jnp.int32, v.shape, 1)


def head_with(v, h, more):
    return jnp.where(lane_of(v) // HEAD_DIM == h, v, more)


def set_tags(id_row, width):
    id_col = jnp.broadcast_to(id_row[...], (8, id_row.shape[1])).T[:, :1]
    rows = id_col.shape[0]
    lane = (lax.broadcasted_iota(jnp.int32, (rows, width), 1) % HEAD_DIM).astype(F32)
    same = lane == id_col
    keys = jnp.where(same, 1.0, 0.0)
    queries = jnp.where(same[: rows // CORES], 0.0, FAR)
    return keys, queries


def three_parts(v):
    first = v.astype(BF).astype(F32)
    second = (v - first).astype(BF).astype(F32)
    return first, second, v - first - second


def with_lanes(tags, first, values):
    lane = lane_of(tags) % HEAD_DIM
    for k, value in enumerate(values):
        tags = jnp.where(lane == first + k, value, tags)
    return tags


def both_rows(own, other, at, part):
    return jnp.concatenate([own[:, at : at + part], other[:, at : at + part]], axis=0)


def attend_kernel(ins, w, outs, *, row, part):
    q, kv, kv_other, id_col, base, gs = ins
    mixed, lse, unit, scaled = outs
    key_tags, query_tags = (t.astype(BF) for t in set_tags(id_col, part))
    full = q.shape[1]
    total = affine(base, gs, row)
    for j in range(full // part):
        at = j * part
        q_part = q[:, at : at + part] * 0.125
        k_part = both_rows(kv, kv_other, at, part)
        v_flip = both_rows(kv, kv_other, full + at, part).T
        flat = []
        for h in range(part // HEAD_DIM):
            s = mm_nt(head_with(k_part, h, key_tags), head_with(q_part, h, query_tags))
            top = jnp.max(s, axis=0, keepdims=True)
            e = jnp.exp(s - top)
            sums = jnp.sum(e, axis=0, keepdims=True)
            o = mm(v_flip[h * HEAD_DIM : (h + 1) * HEAD_DIM], e.astype(BF))
            flat.append(o * (1.0 / sums))
            head = at // HEAD_DIM + h
            lse[head : head + 1, :] = top + jnp.log(sums)
        mixed_part = jnp.concatenate(flat, axis=0).T.astype(BF)
        mixed[:, at : at + part] = mixed_part
        total = total + mm_nt(mixed_part, w(j, 3 * part, 4 * part))
    unit[...], scaled[...] = unit_of(total)


def normal_cdf(x):
    bell = jnp.exp(-0.5 * x * x)
    t = 1.0 / (1.0 + 0.2316418876 * jnp.abs(x))
    tail = 0.5307027145
    for c in (-0.7265760135, 0.7107068705, -0.142248368, 0.127414796):
        tail = tail * t + c
    tail = tail * t * bell
    return jnp.where(x < 0, tail, 1.0 - tail), bell


def feed_kernel(ins, w, outs, *, row, wide):
    unit_in, gs = ins
    act, slope, unit, scaled = outs
    first = affine(unit_in, gs, row)
    y = first.astype(BF)
    total = first
    for j in range(act.shape[1] // wide):
        at = j * wide
        inner = mm(y, w(j, 0, wide))
        cdf, bell = normal_cdf(inner)
        act_part = (inner * cdf).astype(BF)
        act[:, at : at + wide] = act_part
        slope[:, at : at + wide] = (cdf + inner * bell * 0.3989422804014327).astype(BF)
        total = total + mm_nt(act_part, w(j, wide, 2 * wide))
    unit[...], scaled[...] = unit_of(total)


def head_kernel(ins, w, outs, *, row, last):
    unit_in, gs, head_w, counted, *targets = ins
    target = jnp.concatenate([t[...] for t in targets], axis=0)
    counted = counted[...].astype(F32)
    counted = jnp.where(lane_of(counted) < HOR, counted, 0.0)
    loss, g_head0, g_head1, d_hidden, d_norm = outs
    unit, scaled = unit_of(affine(unit_in, gs, row))
    gain = gs[last : last + 1, :]
    final = (unit * gain + gs[last + 1 : last + 2, :]).astype(BF)
    size = head_w.shape[1] // QUANT
    head = head_w[...]
    pred = mm(final, head)
    total = jnp.zeros((1, size), F32)
    grads = []
    for t, level in enumerate(LEVELS):
        gap = target - pred[:, t * size : (t + 1) * size]
        x = gap * (-1.0 / SMOOTHING)
        e = jnp.exp(-jnp.abs(x))
        soft = jnp.maximum(x, 0.0) + jnp.log(1.0 + e)
        sig = jnp.where(x >= 0, 1.0, e) / (1.0 + e)
        total = total + jnp.sum((level * gap + SMOOTHING * soft) * counted, axis=0, keepdims=True)
        grads.append(((sig - level) * counted).astype(BF))
    loss[...] = jnp.concatenate([total, jnp.sum(counted, axis=0, keepdims=True)], axis=0)
    d_pred = jnp.concatenate(grads, axis=1)
    put((g_head0, g_head1), 0, mm(final.T, d_pred).astype(BF))
    d_hidden[...], d_gain, d_shift = norm_back(mm_nt(d_pred, head), gain, unit, scaled)
    d_norm[...] = jnp.concatenate([d_gain, d_shift], axis=0)


def feed_back_kernel(ins, w, outs, g, *, row, wide):
    grad, unit_two, scaled_two, unit_one, scaled_one, gs, act, slope = ins
    d_one, d_norm = outs
    d_two, gain_two, shift_two = norm_back(
        grad[...], gs[row + 2 : row + 3, :], unit_two[...], scaled_two[...]
    )
    d_ffn = d_two.astype(BF)
    d_flip = d_ffn.T
    y_flip = affine(unit_one, gs, row).astype(BF).T
    total = d_two
    for j in range(act.shape[1] // wide):
        at = j * wide
        g(j, wide, mm(d_flip, act[:, at : at + wide]).astype(BF))
        d_act = mm(d_ffn, w(j, wide, 2 * wide))
        d_inner = (d_act * slope[:, at : at + wide].astype(F32)).astype(BF)
        g(j, 0, mm(y_flip, d_inner).astype(BF))
        total = total + mm_nt(d_inner, w(j, 0, wide))
    d_one[...], gain_one, shift_one = norm_back(
        total, gs[row : row + 1, :], unit_one[...], scaled_one[...]
    )
    d_norm[...] = jnp.concatenate([gain_one, shift_one, gain_two, shift_two], axis=0)


def attend_back_kernel(ins, w, outs, *, part, first):
    d_one, q, kv, kv_other, id_col, lse, mixed = ins
    g_out, d_q, d_kv, d_kv_other = outs
    key_tags, query_tags = set_tags(id_col, part)
    key_tags = with_lanes(key_tags, SETS, (1.0, 1.0, 1.0)).astype(BF)
    value_tags = with_lanes(jnp.zeros(key_tags.shape, F32), 0, (1.0, 1.0, 1.0)).astype(BF)
    log_sums = lse[...].T
    full = q.shape[1]
    rows, here = d_q.shape
    d_branch = d_one[...].astype(BF)
    g_out[...] = mm(d_branch.T, mixed[:, first * part : first * part + here]).astype(BF)
    for j in range(first, first + here // part):
        at, to = j * part, (j - first) * part
        d_mixed_wide = mm(d_branch, w(j, 3 * part, 4 * part))
        d_mixed = d_mixed_wide.astype(BF)
        q_part = q[:, at : at + part] * 0.125
        k_part = both_rows(kv, kv_other, at, part)
        v_part = both_rows(kv, kv_other, full + at, part)
        k_flip = k_part.T
        product = d_mixed.astype(F32) * mixed[:, at : at + part].astype(F32)
        d_k = d_v = None
        d_q_flip = []
        for h in range(part // HEAD_DIM):
            head = at // HEAD_DIM + h
            log_sum = log_sums[:, head : head + 1]
            dots = jnp.sum(head_with(product, h, 0.0), axis=1, keepdims=True)
            q_tags = with_lanes(query_tags, SETS, three_parts(-log_sum)).astype(BF)
            d_tags = with_lanes(jnp.zeros_like(product), 0, three_parts(-dots)).astype(BF)
            probs = jnp.exp(mm_nt(head_with(k_part, h, key_tags), head_with(q_part, h, q_tags)))
            shifted = mm_nt(head_with(v_part, h, value_tags), head_with(d_mixed, h, d_tags))
            d_s = (probs * shifted).astype(BF)
            more_v = mm(probs.astype(BF), d_mixed)
            more_k = mm(d_s, q_part)
            d_v = more_v if d_v is None else head_with(more_v, h, d_v)
            d_k = more_k if d_k is None else head_with(more_k, h, d_k)
            d_q_flip.append(mm(k_flip[h * HEAD_DIM : (h + 1) * HEAD_DIM], d_s))
        d_q[:, to : to + part] = (jnp.concatenate(d_q_flip, axis=0) * 0.125).T.astype(BF)
        d_kv[:, to : to + part] = d_k[:rows]
        d_kv_other[:, to : to + part] = d_k[rows:].astype(BF)
        d_kv[:, here + to : here + to + part] = d_v[:rows]
        d_kv_other[:, here + to : here + to + part] = d_v[rows:].astype(BF)


def qkv_back_kernel(ins, w, outs, g, *, row, part):
    d_one, base, gs, *rest = ins
    halves, rest = (rest[:4], rest[4:8]), rest[8:]
    (d_hidden,) = outs
    full = d_one.shape[1]
    h_flip = affine(base, gs, row).astype(BF).T
    total = d_one[...]
    for j in range(full // part):
        here = halves[0][0].shape[1]
        d_q, d_kv, got, g_out = halves[j * part // here]
        at = j * part % here
        d_all = [d_q[:, at : at + part]]
        for base_at in (at, here + at):
            d_all.append(
                (
                    d_kv[:, base_at : base_at + part] + got[:, base_at : base_at + part].astype(F32)
                ).astype(BF)
            )
        d_all = jnp.concatenate(d_all, axis=1)
        g(j, 0, mm(h_flip, d_all).astype(BF))
        g(j, 3 * part, g_out[:, at : at + part])
        total = total + mm_nt(d_all, w(j, 0, 3 * part))
    d_hidden[...] = total
    if len(rest) == CORES:
        g(full // part, 0, jnp.concatenate([r[...] for r in rest], axis=0))
    else:
        x_in, *norms = rest
        rows = [jnp.zeros((LOOK, total.shape[1]), F32)] + [n[...] for n in norms]
        rows.append(jnp.zeros((HEAD_PAD - LOOK - 2 * NORMS, total.shape[1]), F32))
        g(full // part, 0, (mm(total.astype(BF).T, x_in[...]) + jnp.concatenate(rows, axis=0).T).astype(BF))


def finish_kernel(at, *refs, blocks, shared):
    count = len(shared)
    ins, outs = refs[: 1 + count * (blocks + 1)], refs[1 + count * (blocks + 1) :]
    z = at[1]
    squares = jnp.zeros((), F32)
    for c in range(count):
        own, common, *turned = ins[1 + c * (blocks + 1) : 1 + (c + 1) * (blocks + 1)]
        cols = own.shape[1]
        total = own[...]
        for t in turned:
            total = total + t[:, :cols].astype(F32)
        outs[c][...] = total
        squares = squares + jnp.sum(total * total)
        if shared[c]:
            held = [common[...].astype(F32)] + [t[:, cols:].astype(F32) for t in turned]
            total = jnp.zeros_like(held[0])
            for owner in range(blocks):
                by = z ^ owner
                term = held[0]
                for j in range(1, blocks):
                    term = jnp.where(by == j, held[j], term)
                total = total + term
            outs[count + sum(shared[:c])][...] = total
            squares = squares + jnp.where(z == 0, jnp.sum(total * total), 0.0)
    loss = ins[0]
    place = lax.broadcasted_iota(jnp.int32, outs[-1].shape, 1)
    outs[-1][...] = jnp.where(
        place == 0,
        jnp.sum(loss[0:1, :]),
        jnp.where(place == 1, jnp.sum(loss[1:2, :]), jnp.where(place == 2, squares, 0.0)),
    )


def scalars_of(sums):
    total = jnp.sum(sums, axis=0, keepdims=True)

    def lane(k):
        return jnp.sum(jnp.where(lane_of(total) == k, total, 0.0), axis=1, keepdims=True)

    valid_count = lane(1)
    grad_norm = jnp.sqrt(lane(2)) / valid_count
    factor = jnp.minimum(1.0, CLIP_NORM / grad_norm) / valid_count
    place = lane_of(total)
    return jnp.where(place == 2, grad_norm, jnp.where(place == 3, factor, total)), factor


def scalars_kernel(sums, out):
    out[...], _ = scalars_of(sums[...])


def update_kernel(sums, *refs, count):
    grads, held, refs = refs[:count], refs[count : 4 * count], refs[4 * count :]
    scalars, outs, refs = refs[0], refs[1 : 1 + 3 * count], refs[1 + 3 * count :]
    old, new, (arrived, left) = refs[: 3 * count], refs[3 * count : 6 * count], refs[6 * count :]
    into = [pltpu.make_async_copy(a, b, arrived.at[k]) for k, (a, b) in enumerate(zip(held, old))]
    back = [pltpu.make_async_copy(a, b, left.at[k]) for k, (a, b) in enumerate(zip(new, outs))]
    for copy in into:
        copy.start()
    scalars[...], factor = scalars_of(sums[...])
    for n in range(count):
        for k in range(3 * n, 3 * n + 3):
            into[k].wait()
        w, m, v = (ref[...] for ref in old[3 * n : 3 * n + 3])
        g = grads[n][...] * factor.reshape((1,) * len(w.shape))
        done = adam_update(w, g, m, v, LEARN_RATE, WEIGHT_DECAY)
        for k, value in enumerate(done, 3 * n):
            new[k][...] = value
            back[k].start()
    for copy in back:
        copy.wait()


def kernel_call(kernel, pos, ins, weights, outs, grads=None, scratch=(), us=1.0, **static):
    whole = pl.BlockSpec(memory_space=pltpu.VMEM)
    w_arrays = weights.arrays if weights else ()
    g_shapes = grads.shapes if grads else ()

    def run(at, *refs):
        refs = list(refs)

        def take(count):
            got = refs[:count]
            del refs[:count]
            return got

        in_refs = take(len(ins))
        w_refs = take(len(w_arrays))
        out_refs = take(len(outs))
        g_refs = take(len(g_shapes))
        more = [grads.writer(g_refs, at)] if grads else []
        kernel(in_refs, weights.reader(w_refs) if weights else None, out_refs, *more, *refs, **static)

    return pl.pallas_call(
        run,
        out_shape=tuple(outs) + tuple(g_shapes),
        grid_spec=pltpu.PrefetchScalarGridSpec(
            num_scalar_prefetch=1,
            grid=(1,),
            in_specs=[whole] * len(ins) + (weights.specs() if weights else []),
            out_specs=tuple(whole for _ in range(len(outs) + len(g_shapes))),
            scratch_shapes=scratch,
        ),
        compiler_params=pltpu.CompilerParams(vmem_limit_bytes=20 * 1024 * 1024),
        cost_estimate=pl.CostEstimate(flops=int(us * 1.15e9), bytes_accessed=0, transcendentals=0),
    )(pos, *ins, *w_arrays)


def kernel_call_plain(kernel, outs, *args, pos=None, limit=20):
    whole = pl.BlockSpec(memory_space=pltpu.VMEM)
    first = [] if pos is None else [pl.BlockSpec(memory_space=pltpu.SMEM)]
    return pl.pallas_call(
        kernel,
        out_shape=outs,
        in_specs=first + [whole] * len(args),
        out_specs=tuple(whole for _ in outs),
        compiler_params=pltpu.CompilerParams(vmem_limit_bytes=limit * 1024 * 1024),
    )(*(() if pos is None else (pos,)), *args)


def like(shape, dtype):
    return jax.ShapeDtypeStruct(shape, dtype)


def adam_update(weight, gradient, first_moment, second_moment, rate, decay):
    first_moment = BETA_ONE * first_moment + (1 - BETA_ONE) * gradient
    second_moment = BETA_TWO * second_moment + (1 - BETA_TWO) * gradient * gradient
    update = (
        first_moment
        / (1 - BETA_ONE**STEP)
        / (jnp.sqrt(second_moment / (1 - BETA_TWO**STEP)) + EPSILON)
    )
    return (weight - rate * (update + decay * weight), first_moment, second_moment)


def deal_swap(v):
    rows = v.shape[1] // CORES
    core = lax.axis_index("core")
    v = v.reshape(MICRO, CORES, rows, v.shape[-1])
    keep = lax.dynamic_index_in_dim(v, core, 1, keepdims=False)
    send = lax.dynamic_index_in_dim(v, 1 - core, 1, keepdims=False)
    got = swap_core(send)
    return jnp.where(core == 0, jnp.concatenate([keep, got]), jnp.concatenate([got, keep]))


def deal_halves_kernel(at, whole, keep, send):
    rows = keep.shape[1]
    for m in range(MICRO):
        keep[m] = whole[m, pl.ds(pl.multiple_of(at[3] * rows, rows), rows), :]
        send[m] = whole[m, pl.ds(pl.multiple_of((1 - at[3]) * rows, rows), rows), :]


def deal_parts_kernel(at, keep, got, *parts):
    for by, part in enumerate(parts):
        owner = at[1] ^ by
        part[...] = jnp.zeros_like(part)
        part[:, : keep.shape[2]] = jnp.where(
            owner // MICRO == at[3], keep[owner % MICRO], got[owner % MICRO]
        )


def deal_rows(v):
    size = lax.axis_size("mp")
    z = lax.axis_index("mp")
    parts = [lax.dynamic_index_in_dim(v, z ^ by, 0, keepdims=False) for by in range(size)]
    return jnp.concatenate(parts[:1] + [swap_mp(parts[by], by) for by in range(1, size)])


def body(
    series,
    targets,
    valid,
    dataset_ids,
    embed_w,
    qkv_w,
    out_w,
    up_w,
    down_w,
    head_w,
    norm_params,
    *moments,
):
    (
        embed_first,
        embed_second,
        qkv_first,
        qkv_second,
        out_first,
        out_second,
        up_first,
        up_second,
        down_first,
        down_second,
        head_first,
        head_second,
        norm_first,
        norm_second,
    ) = moments
    width = embed_w.shape[1]
    part = qkv_w.shape[3]
    wide = up_w.shape[2]
    blocks_n = lax.axis_size("mp")

    bits = hi_bits()
    hi_at, core_at, z_at = lax.axis_index("hi"), lax.axis_index("core"), lax.axis_index("mp")
    pos = jnp.stack([hi_at * CORES + core_at, z_at, hi_at, core_at]).astype(jnp.int32)
    att_w, ffn_w, late = {}, {}, None
    placed = width % 16 == 0
    packed = kernel_call_plain(
        pack_kernel,
        tuple(like((width, cols), BF) for cols in (4 * part, 2 * wide, 2 * wide, 4 * part))
        if not placed
        else (like((width, 4 * part), BF), like((width, 2 * wide), BF), like((width, 2 * wide + 4 * part), BF)),
        qkv_w.transpose(0, 2, 1, 3), out_w, up_w, down_w,
        limit=56,
    )
    att_w[0], ffn_w[0], ffn_w[1], att_w[1] = (*packed, None) if placed else packed
    if placed:
        late = lax.all_gather(ffn_w[1], ("hi", "mp"), axis=0, tiled=False)
        late = late.reshape((-1,) + late.shape[-2:])

    low_pad = HEAD_PAD - LOOK - 2 * NORMS
    embed_cols = jnp.concatenate([embed_w.T, norm_params.reshape(-1, width).T], axis=1)
    head_cols = jnp.pad(head_w.reshape(width, QUANT, HOR), ((0, 0), (0, 0), (0, HEAD_PAD - HOR)))
    rest = Gather(
        jnp.concatenate(
            [jnp.pad(embed_cols, ((0, 0), (0, low_pad))), head_cols.reshape(width, -1)], axis=1
        ).astype(BF),
        False,
    )
    low = deal_swap(
        jnp.pad(
            jnp.concatenate(
                [
                    jnp.pad(series, ((0, 0), (0, 0), (0, HEAD_PAD - LOOK))),
                    valid.astype(BF),
                    dataset_ids[..., None].astype(BF),
                ],
                axis=-1,
            ),
            ((0, 0), (0, 0), (0, HEAD_PAD - HOR - 1)),
        )
    )
    z_att = turns(att_w[0])
    rest.hop()
    att_pairs = pairs_of(att_w[0], z_att)
    hop_att = [pair.hop() for pair in att_pairs]
    low = deal_rows(after(low, *z_att))
    for _ in range(1, bits):
        rest.hop(before=hop_att)
    rest = rest.halves()
    ffn_first = after(ffn_w[0], *hop_att)
    z_ffn = turns(ffn_first)
    for _ in range(1, bits):
        hop_att = [pair.hop() for pair in att_pairs]
    att = [Halves(halves_of(att_pairs))]
    ffn_pairs = pairs_of(ffn_first, z_ffn)
    for _ in range(bits - 1):
        for pair in ffn_pairs:
            pair.hop()

    model = CORES * rest[0].shape[0]
    ident = 2 * NORMS
    x_in = low[:, :HEAD_PAD]
    counted = low[:, HEAD_PAD : 2 * HEAD_PAD]
    ids_here = low[:, HEAD_PAD + HOR].reshape(1, -1)
    ids = jnp.concatenate([ids_here, swap_core(ids_here)], axis=1).astype(F32)
    rows = x_in.shape[0]
    heads = model // HEAD_DIM
    hidden_n = wide * blocks_n

    base, row = None, ident
    stored = []
    ffn = []
    for l in range(LAYERS):
        q, kv, *more = kernel_call(
            qkv_kernel, pos, (base, gs) if l else (x_in, *rest), att[l],
            (like((rows, model), BF), like((rows, 2 * model), BF))
            + (() if l else (like((rows, model), F32), like((16, model), F32), like((model, QUANT * HEAD_PAD), BF))),
            us=1.3, row=row, part=part,
        )
        if l == 0:
            base, gs, head_w_all = more
        kv_other = swap_core(kv)
        if l == 0:
            q = after(q, *(pair.v for pair in ffn_pairs))
        mixed, lse, unit_one, scaled_one = kernel_call(
            attend_kernel, pos, (q, kv, kv_other, ids, base, gs), att[l],
            (like((rows, model), BF), like((heads, rows), F32), like((rows, model), F32), like((rows, 1), F32)),
            us=11, row=row, part=part,
        )
        if l == 1:
            target = [parts[0]] + [swap_mp(parts[by], by) for by in range(1, blocks_n)]
            unit_one = after(unit_one, *together(target, mixed))
        if l == 0:
            for pair in ffn_pairs:
                pair.hop(before=(kv,), beside=(mixed,))
            half = (MICRO, targets.shape[1] // CORES, HOR)
            keep, send = kernel_call_plain(
                deal_halves_kernel, (like(half, F32), like(half, F32)), after(targets, mixed), pos=pos
            )
            parts = kernel_call_plain(
                deal_parts_kernel,
                (like((half[1], HEAD_PAD), F32),) * blocks_n,
                keep, swap_core(send),
                pos=pos,
            )
            unit_one = after(unit_one, *parts)
            ffn.append(Halves(halves_of(ffn_pairs)))
            if not placed:
                for kept, v in ((att, att_w[1]), (ffn, ffn_w[1])):
                    pairs = pairs_of(v, turns(v))
                    for _ in range(bits):
                        for pair in pairs:
                            pair.hop()
                    kept.append(Halves(halves_of(pairs)))
        act, slope, unit_two, scaled_two = kernel_call(
            feed_kernel, pos, (unit_one, gs), ffn[l],
            (like((rows, hidden_n), BF), like((rows, hidden_n), BF), like((rows, model), F32), like((rows, 1), F32)),
            us=10, row=4 * l, wide=wide,
        )
        stored.append((base, row, q, kv, kv_other, mixed, lse, unit_one, scaled_one, act, slope, unit_two, scaled_two))
        base, row = unit_two, 4 * l + 2
        if l == 0 and placed:
            late = after(late, unit_two)
            other = swap_core(late)
            att.append(Shards(late, other, 2 * wide // (4 * part), 4 * part))
            ffn.append(Shards(late, other, 0, 2 * wide))
    loss_row, *g_head, grad, d_norm_last = kernel_call(
        head_kernel, pos, (base, gs, head_w_all, counted, *target), None,
        (like((2, HEAD_PAD), F32),)
        + (like((model // CORES, QUANT * HEAD_PAD), BF),) * CORES
        + (like((rows, model), F32), like((2, model), F32)),
        us=2, row=row, last=2 * NORMS - 2,
    )
    norm_grads = [None] * LAYERS
    sums = []

    def feed_back(l, grad):
        unit_one, scaled_one, act, slope, unit_two, scaled_two = stored[l][7:]
        return kernel_call(
            feed_back_kernel, pos,
            (grad, unit_two, scaled_two, unit_one, scaled_one, gs, act, slope), ffn[l],
            (like((rows, model), F32), like((4, model), F32)),
            grads=GradOut(model, 2 * wide),
            us=10.5, row=4 * l, wide=wide,
        )

    def attend_back(l, d_one, half):
        q, kv, kv_other, mixed, lse = stored[l][2:7]
        here = model // 2
        g_out, d_q, d_kv, d_kv_other = kernel_call(
            attend_back_kernel, pos,
            (d_one, q, kv, kv_other, ids, lse, mixed), att[l],
            (like((model, here), BF), like((rows, here), BF), like((rows, 2 * here), F32), like((rows, 2 * here), BF)),
            us=8, part=part, first=half * here // part,
        )
        return d_q, d_kv, swap_core(d_kv_other), g_out

    def qkv_back(l, d_one, *args):
        base, row = stored[l][:2]
        more = (x_in, *norm_grads, d_norm_last) if l == 0 else tuple(g_head)
        return kernel_call(
            qkv_back_kernel, pos, (d_one, base, gs, *args, *more), att[l],
            (like((rows, model), F32),),
            grads=GradOut(model, 4 * part, more=HEAD_PAD if l == 0 else QUANT * HEAD_PAD, pairs=False),
            us=5.5, row=row, part=part,
        )

    d_one, norm_grads[1], *halves = feed_back(1, grad)
    ffn_sum = Halving(halves, 2 * wide)
    first = attend_back(1, d_one, 0)
    sent = ffn_sum.step(first[0])
    second = attend_back(1, after(d_one, first[0], *sent), 1)
    sent = ffn_sum.step(second[0])
    grad, *halves = qkv_back(1, after(d_one, *sent), *first, *second)
    att_sum = Scatter(*halves, 4 * part)
    sent = ffn_sum.step(grad)

    d_one, norm_grads[0], *halves = feed_back(0, after(grad, *sent))
    ffn_low = Halving(halves, 2 * wide)
    sent = att_sum.step(d_one) + ffn_sum.step(d_one)
    d_one = after(d_one, *sent, *ffn_sum.landed())
    first = attend_back(0, d_one, 0)
    sent = ffn_low.step(first[0])
    second = attend_back(0, after(d_one, first[0], *sent), 1)
    sent = att_sum.step(second[0]) + ffn_low.step(second[0])
    _, own, other = qkv_back(0, after(d_one, *sent), *first, *second)
    att_low = Scatter(own, other, 4 * part)
    for chunk in (ffn_sum, att_sum, ffn_low):
        while chunk.stages:
            chunk.step(own)
    att_low.step()
    att_low.step(*ffn_low.landed(), *att_sum.landed())
    sums = [ffn_sum, att_sum, ffn_low, att_low]

    count = lax.axis_size("hi") * CORES * blocks_n
    *grads, g_head, g_low, scalars = kernel_call_plain(
        functools.partial(finish_kernel, blocks=blocks_n, shared=(False, True, False, True)),
        tuple(like((width, s.cols), F32) for s in sums)
        + (like((width, QUANT * HEAD_PAD), F32), like((width, HEAD_PAD), F32), like((count, 128), F32)),
        loss_row,
        *(v for s in sums for v in (s.parts if s.parts[1].size else [s.parts[0], s.parts[0]] + s.parts[2:])),
        pos=pos,
    )
    g_ffn1, g_att1, g_ffn0, g_att0 = grads
    scalars = lax.all_to_all(
        scalars.reshape(count, 1, 128), ("hi", "core", "mp"), 0, 0, tiled=True
    ).reshape(count, 128)
    g_qkv = jnp.stack(
        [jnp.stack([g[:, c * part : (c + 1) * part] for c in range(3)]) for g in (g_att0, g_att1)]
    )
    g_out = jnp.stack([g[:, 3 * part :] for g in (g_att0, g_att1)])
    g_up = jnp.stack([g[:, :wide] for g in (g_ffn0, g_ffn1)])
    g_down = jnp.stack([g[:, wide:] for g in (g_ffn0, g_ffn1)])
    g_norm = g_low[:, LOOK : LOOK + 2 * NORMS].T.reshape(norm_params.shape)
    g_head = g_head.reshape(width, QUANT, HEAD_PAD)[:, :, :HOR].reshape(width, -1)
    sets = (
        (*(v.transpose(0, 2, 1, 3) for v in (qkv_w, qkv_first, qkv_second)), g_qkv),
        (out_w, out_first, out_second, g_out),
        (up_w, up_first, up_second, g_up),
        (down_w, down_first, down_second, g_down),
    )
    shapes = [one[0].shape for one in sets for _ in range(3)]
    whole, away = pl.BlockSpec(memory_space=pltpu.VMEM), pl.BlockSpec(memory_space=pl.ANY)
    count = len(sets)
    scalars, *news = pl.pallas_call(
        functools.partial(update_kernel, count=count),
        out_shape=(like((1, 128), F32),) + tuple(like(shape, F32) for shape in shapes),
        in_specs=[whole] * (1 + count) + [away] * (3 * count),
        out_specs=(whole,) + (away,) * (3 * count),
        scratch_shapes=[pltpu.VMEM(shape, F32) for shape in shapes * 2] + [pltpu.SemaphoreType.DMA((3 * count,))] * 2,
        compiler_params=pltpu.CompilerParams(vmem_limit_bytes=20 * 1024 * 1024),
    )(after(scalars, g_head, g_norm), *(one[3] for one in sets), *(v for one in sets for v in one[:3]))
    news[:3] = [v.transpose(0, 2, 1, 3) for v in news[:3]]
    factor = scalars[0, 3]
    e_new = adam_update(
        embed_w.T, g_low[:, :LOOK] * factor, embed_first.T, embed_second.T, LEARN_RATE, WEIGHT_DECAY
    )
    h_new = adam_update(head_w, g_head * factor, head_first, head_second, LEARN_RATE, WEIGHT_DECAY)
    n_new = adam_update(norm_params, g_norm * factor, norm_first, norm_second, NORM_RATE, 0.0)
    return (scalars[0, 0], scalars[0, 1], scalars[0, 2], *(v.T for v in e_new), *news, *h_new, *n_new)


def solution(mesh):
    dp, mp = mesh.devices.shape
    split = Mesh(mesh.devices.reshape(dp // CORES, CORES, mp), ("hi", "core", "mp"))
    wide = ("hi", "core")
    tokens = ("hi", "core", "mp")
    embed = P(None, wide)
    qkv = P(None, wide, None, "mp")
    mat = P(None, wide, "mp")
    head = P(wide, None)
    norm = P(None, None, wide)
    weights = (embed, qkv, mat, mat, mat, head, norm)
    return jax.shard_map(
        body,
        mesh=split,
        in_specs=(P(None, tokens, None),) * 3
        + (P(None, tokens),)
        + weights
        + tuple(spec for spec in weights for _ in range(2)),
        out_specs=(P(),) * 3 + tuple(spec for spec in weights for _ in range(3)),
        check_vma=False,
    )
```
